128 devices in a mesh: vtx: 32 (over y, x, core), edg: 4 (over z).
Axes of the slice: x: 4, y: 4, z: 4, core: 2. Of those that a mesh axis runs over, the one named last changes fastest.
Arguments:
- sketch_cols: bfloat16 [524288, 128], P(('vtx', 'edg')), may hold values from -6 to 6
- edge_weight: float32 [524288], P(('vtx', 'edg')), may hold values from 0.25 to 4
- ground: float32 [65536], P('vtx'), may hold values from 0.05 to 0.5
- src_local: int32 [524288], P(('vtx', 'edg')), may hold values from 0 to 2047
- dst_index: int32 [524288], P(('vtx', 'edg')), may hold values from 0 to 3583
- send_rows: int32 [128, 32, 48], P(('vtx', 'edg')), may hold values from 0 to 2047
- edge_count: int32 [128], P(('vtx', 'edg')), may hold values from 512 to 4096, as said below
Outputs:
- solution: float32 [65536, 128], P('vtx')
- resistance: float32 [524288], P(('vtx', 'edg'))
The draws below stay inside these ranges and needn't reach their ends.
Inputs may be any that keep to these rules, and one draw needn't show every extreme that they name: `edge_count`: edge slots of a device at positions of its count or beyond are unused. In every draw some device has all 4096 slots live.
All inputs are finite; a program needn't handle non-finite values.
Results may differ from the reference program's by a relative error of at most 0.0003.
Values sent between devices are 32-bit elements; how exact they have to be, the bound alone decides.
No kernel may reach another device: no remote copies, remote signals or barrier semaphores. Data moves between devices by JAX's collectives and lax.ppermute only.
A program may use at most 64 MiB of HBM per device.

```python
import math
import jax
import jax.numpy as jnp
from jax import lax

COLS = 128
VB = 2048
ED = 4096
H = 48
ITERS = 3
GROUPS = 128
V = 65536
EDGES = 524288
N_VTX = 32
N_EDG = 4


def draw_edge_count(key, part):
    mixed = jax.random.fold_in(key, 11)
    first_key, second_key = jax.random.split(mixed)
    powers = jax.random.randint(first_key, (GROUPS,), 0, 4)
    counts = jnp.right_shift(jnp.full((GROUPS,), ED, jnp.int32), powers.astype(jnp.int32))
    chosen = jax.random.randint(second_key, (), 0, GROUPS)
    counts = counts.at[chosen].set(ED)
    return counts.astype(jnp.int32)


def set_ends(array, rng, smallest, high):
    dims = array.shape
    index_at = [jax.random.randint(jax.random.fold_in(rng, axis), (), 0, dims[axis]) for axis in range(len(dims))]
    array = array.at[tuple(index_at)].set(smallest)
    longest = dims.index(max(dims))
    index_at[longest] = (index_at[longest] + 1) % dims[longest]
    return array.at[tuple(index_at)].set(high)


def level_of(own_key, shape, pieces, low, top_value):
    gain = 1.0
    for axis_at, parts in pieces:
        steps = jax.random.uniform(jax.random.fold_in(jax.random.fold_in(own_key, 6), axis_at), (parts,), jnp.float32, low / len(pieces), top_value / len(pieces))
        gain = gain * jnp.repeat(jnp.exp(steps), shape[axis_at] // parts).reshape((-1,) + (1,) * (len(shape) - 1 - axis_at))
    return gain


def gaussian(own_key, extent, deviation, reach, cuts=(), kind=jnp.bfloat16):
    entries = jax.random.normal(own_key, extent, jnp.float32) * deviation
    if len(cuts) > 0:
        entries = level_of(own_key, extent, cuts, -0.22, 0.18) * entries
    return jnp.clip(entries, min=-reach, max=reach).astype(kind)


def setup_inputs(seed: int = 0) -> dict:
    streams_of = jax.random.split(jax.random.key(seed), 8)
    sketch_cols = gaussian(streams_of[0], (EDGES, COLS), 1.0, 6.0, ((0, 128),))
    edge_weight = jnp.clip(jnp.exp(math.log(4.0) - 2.7725887 * jax.random.uniform(streams_of[1], (EDGES,), jnp.float32) ** level_of(streams_of[1], (EDGES,), ((0, 128),), -0.2, 0.2)), 0.25, 4.0)
    ground = jnp.clip(jnp.exp(math.log(0.5) - 2.3025851 * jax.random.uniform(streams_of[2], (V,), jnp.float32) ** level_of(streams_of[2], (V,), ((0, 32),), -0.2, 0.2)), 0.05, 0.5)
    src_local = set_ends(jax.random.randint(streams_of[3], (EDGES,), 0, VB), jax.random.fold_in(streams_of[3], 1), 0, VB - 1).astype(jnp.int32)
    dst_index = set_ends(jax.random.randint(streams_of[4], (EDGES,), 0, VB + N_VTX * H), jax.random.fold_in(streams_of[4], 1), 0, (VB + N_VTX * H) - 1).astype(jnp.int32)
    send_rows = set_ends(jax.random.randint(streams_of[5], (GROUPS, N_VTX, H), 0, VB), jax.random.fold_in(streams_of[5], 1), 0, VB - 1).astype(jnp.int32)
    edge_count = draw_edge_count(jax.random.fold_in(streams_of[7], 71), 0)
    return {"sketch_cols": sketch_cols, "edge_weight": edge_weight, "ground": ground, "src_local": src_local, "dst_index": dst_index, "send_rows": send_rows, "edge_count": edge_count}


lam_low = 0.05
lam_high = 2.0

def chebyshev_terms(steps):
    centre = (lam_high + lam_low) / 2.0
    half_width = (lam_high - lam_low) / 2.0
    sigma_val = centre / half_width
    rho_prev = 1.0 / sigma_val
    pairs = []
    for count_idx in range(steps - 1):
        rho_next = 1.0 / (2.0 * sigma_val - rho_prev)
        pairs.append((rho_next * rho_prev, 2.0 * rho_next / half_width))
        rho_prev = rho_next
    return (1.0 / centre, pairs)

def reference(sketch_cols, edge_weight, ground, src_local, dst_index, send_rows, edge_count):
    vertices = VB * N_VTX
    position = jnp.arange(EDGES, dtype=jnp.int32)
    device = position // ED
    block_id = device // N_EDG
    lane_idx = device % N_EDG
    live_mask = (position % ED < edge_count[device]).astype(jnp.float32)
    source = block_id * VB + src_local
    slot_idx = jnp.maximum(dst_index - VB, 0)
    owner_blk = slot_idx // H
    within = slot_idx % H
    remote = send_rows[owner_blk * N_EDG + lane_idx, block_id, within]
    target = jnp.where(dst_index < VB, block_id * VB + dst_index, owner_blk * VB + remote).astype(jnp.int32)
    weight_live = edge_weight * live_mask
    root_live = jnp.sqrt(edge_weight) * live_mask
    edge_terms = root_live[:, None] * sketch_cols.astype(jnp.float32)
    right_side = jax.ops.segment_sum(edge_terms, source, vertices) - jax.ops.segment_sum(edge_terms, target, vertices)
    degree = jax.ops.segment_sum(weight_live, source, vertices) + jax.ops.segment_sum(weight_live, target, vertices)
    inverse = (1.0 / (degree + ground))[:, None]

    def operate(field_in):
        edge_diffs = weight_live[:, None] * (field_in[source] - field_in[target])
        return ground[:, None] * field_in + jax.ops.segment_sum(edge_diffs, source, vertices) - jax.ops.segment_sum(edge_diffs, target, vertices)
    first, pairs = chebyshev_terms(ITERS)
    residual_now = right_side
    direction = first * inverse * right_side
    solution = jnp.zeros_like(right_side)
    for step_idx in range(ITERS):
        solution = solution + direction
        if step_idx + 1 < ITERS:
            residual_now = residual_now - operate(direction)
            keep_coef, push_coef = pairs[step_idx]
            direction = keep_coef * direction + push_coef * inverse * residual_now
    gaps = solution[source] - solution[target]
    resistance = live_mask * lax.optimization_barrier(jnp.sum(gaps * gaps, axis=1)) / COLS
    return (solution, resistance)
```

```python
import functools

import jax
import jax.numpy as jnp
from jax import lax
from jax.experimental import pallas as pl
from jax.experimental.pallas import tpu as pltpu
from jax.sharding import PartitionSpec as P

ITERS = 3
LANES = 128
UNROLL = 16
BANKS = 4

lam_low = 0.05
lam_high = 2.0

SMEM = pl.BlockSpec(memory_space=pltpu.SMEM)
VMEM = pl.BlockSpec(memory_space=pltpu.VMEM)
LIMIT = 48 * 2**20


def chebyshev_terms(steps):
    centre = (lam_high + lam_low) / 2.0
    half_width = (lam_high - lam_low) / 2.0
    sigma_val = centre / half_width
    rho_prev = 1.0 / sigma_val
    pairs = []
    for count_idx in range(steps - 1):
        rho_next = 1.0 / (2.0 * sigma_val - rho_prev)
        pairs.append((rho_next * rho_prev, 2.0 * rho_next / half_width))
        rho_prev = rho_next
    return (1.0 / centre, pairs)


def call(kernel, outs, ins, scratch, name, flops=0, moved=2**22):
    return pl.pallas_call(
        kernel,
        out_shape=[jax.ShapeDtypeStruct(shape, dtype) for shape, dtype, _ in outs],
        in_specs=ins,
        out_specs=[space for _, _, space in outs],
        scratch_shapes=scratch,
        compiler_params=pltpu.CompilerParams(vmem_limit_bytes=LIMIT),
        cost_estimate=pl.CostEstimate(flops=flops, bytes_accessed=moved, transcendentals=0),
        name=name,
    )


def split(x):
    high = x.astype(jnp.bfloat16)
    return high, (x - high.astype(jnp.float32)).astype(jnp.bfloat16)


def put_split(ref, rows, x):
    high, low = split(x)
    ref[rows, :LANES] = high
    ref[rows, LANES:] = low


def halves(x):
    return x[:, :LANES] + x[:, LANES:]


def one_hot(row, height, base):
    place = lax.broadcasted_iota(jnp.int32, (height, row.shape[1]), 0) + base
    return jnp.where(place == row, 1.0, 0.0)


def factored(pick, groups, high_of, low_of, weight_of, height):
    total = jnp.zeros((2 * height, LANES), jnp.float32)
    for k0 in range(0, groups, pick):
        left, right = [], []
        for k in range(k0, k0 + pick):
            member = one_hot(high_of(k), height, 0) * weight_of(k)
            high, low = split(member)
            left.append(jnp.concatenate([high, low], axis=0))
            right.append(one_hot(low_of(k), LANES, 0).astype(jnp.bfloat16))
        total = total + lax.dot_general(
            jnp.concatenate(left, axis=1),
            jnp.concatenate(right, axis=1),
            (((1,), (1,)), ((), ())),
            preferred_element_type=jnp.float32,
        )
    return total[:height] + total[height:]


def halo_side_kernel(rows, slots, width, terms, target, weight, out, both, hot):
    groups = target.shape[0]
    edges = terms.shape[0]
    put_split(both, slice(None), terms[...])
    tall = hot.shape[0]
    per = tall // width

    def chunk(i, _):
        base = rows + i * tall
        for k in range(groups):
            hot[:, k * LANES : (k + 1) * LANES] = one_hot(target[k : k + 1, :], tall, base).astype(jnp.bfloat16)
        got = halves(jnp.dot(hot[...], both[...], preferred_element_type=jnp.float32))
        for c in range(per):
            out[i * per + c, :width, :] = -got[c * width : (c + 1) * width]
        return 0

    lax.fori_loop(0, slots // tall, chunk, 0)
    blocks = slots // width

    def slot(k):
        return target[k : k + 1, :] - rows

    def block_of(k):
        return jnp.where(slot(k) < 0, -1, lax.shift_right_arithmetic(slot(k) * 1366, 16))

    def within(k):
        return slot(k) - block_of(k) * width

    deg = factored(4, groups, block_of, within, lambda k: weight[k : k + 1, :], blocks)
    for c in range(blocks):
        out[c, width : width + 8, :] = jnp.broadcast_to(deg[c : c + 1, :], (8, LANES))


def own_side_kernel(terms, source, target, weight, out, degree, both, hot):
    groups = target.shape[0]
    rows = out.shape[0]
    put_split(both, slice(None), terms[...])
    tall = hot.shape[0]

    def chunk(i, _):
        base = i * tall
        for k in range(groups):
            plus = one_hot(source[k : k + 1, :], tall, base)
            minus = one_hot(target[k : k + 1, :], tall, base)
            hot[:, k * LANES : (k + 1) * LANES] = (plus - minus).astype(jnp.bfloat16)
        out[pl.ds(pl.multiple_of(i * tall, tall), tall), :] = halves(
            jnp.dot(hot[...], both[...], preferred_element_type=jnp.float32)
        )
        return 0

    lax.fori_loop(0, rows // tall, chunk, 0)

    def total(ref):
        return factored(
            4,
            groups,
            lambda k: lax.shift_right_logical(ref[k : k + 1, :], 7),
            lambda k: ref[k : k + 1, :] & (LANES - 1),
            lambda k: weight[k : k + 1, :],
            rows // LANES,
        )

    degree[...] = total(source) + total(target)


def scatter_back(ret_both, listed, hot, emit, rows):
    tall = hot.shape[0]
    groups = listed.shape[0]

    def chunk(i, _):
        base = i * tall
        for k in range(groups):
            hot[:, k * LANES : (k + 1) * LANES] = one_hot(listed[k : k + 1, :], tall, base).astype(jnp.bfloat16)
        emit(i, halves(jnp.dot(hot[...], ret_both[...], preferred_element_type=jnp.float32)))
        return 0

    lax.fori_loop(0, rows // tall, chunk, 0)


def side_join_kernel(lane, returned, listed, padded, own, own_degree, *refs):
    lanes = 4
    outs, (acc, ret_both, hot) = refs[:lanes], refs[lanes:]
    blocks = returned.shape[0]
    rows = own.shape[0]
    width = listed.shape[0] * LANES // blocks
    share = rows // lanes
    for c in range(blocks):
        put_split(ret_both, slice(c * width, (c + 1) * width), returned[c, :width, :])

    def emit(i, got):
        at = pl.ds(pl.multiple_of(i * hot.shape[0], hot.shape[0]), hot.shape[0])
        acc[at, :] = own[at, :] + got

    scatter_back(ret_both, listed, hot, emit, rows)
    deg = own_degree[...] + factored(
        4,
        blocks,
        lambda k: lax.shift_right_arithmetic(padded[k : k + 1, :], 7),
        lambda k: padded[k : k + 1, :] & (LANES - 1),
        lambda k: returned[k, width : width + 1, :],
        rows // LANES,
    )
    deg_rows = share // LANES
    for s in range(lanes):
        q = lax.rem(lane[0] + s, lanes)
        outs[s][:share, :] = acc[pl.ds(pl.multiple_of(q * share, share), share), :]
        row = jnp.zeros((8, LANES), jnp.float32)
        place = lax.broadcasted_iota(jnp.int32, (8, LANES), 0)
        for p in range(lanes):
            for d in range(deg_rows):
                one = jnp.broadcast_to(deg[p * deg_rows + d : p * deg_rows + d + 1, :], (8, LANES))
                row = jnp.where((place == d) & (q == p), one, row)
        outs[s][share : share + 8, :] = row


def partition_kernel(rows, count, source, target, weight, order, heavy, edge, sizes):
    second = order.shape[0] // 2

    def step(i, at):
        near, far = at
        for u in range(8):
            e = i * 8 + u
            t = target[e]
            away = (t >= rows).astype(jnp.int32)
            pos = jnp.where(away == 1, far + second, near)
            order[pos] = source[e] | ((t - away * rows) << 12)
            heavy[pos] = weight[e]
            edge[pos] = e
            near, far = near + 1 - away, far + away
        return near, far

    near, far = lax.fori_loop(0, (count[0] + 7) // 8, step, (0, 0))
    for u in range(UNROLL):
        for pos in (near + u, far + second + u):
            order[pos] = 0
            heavy[pos] = 0.0
            edge[pos] = 0
    sizes[0] = near
    sizes[1] = far


def trips(n):
    return lax.div(n + UNROLL - 1, UNROLL)


def clear(banks):
    for a in banks:
        a[...] = jnp.zeros_like(a)


def field_kernel(lane, sizes, order, heavy, lists, *refs):
    lanes = 4
    shares, (field, out), banks = refs[:lanes], refs[lanes : lanes + 2], refs[lanes + 2 :]
    share = shares[0].shape[0]
    blocks, both, _ = out.shape
    width = both // 2
    second = order.shape[0] // 2
    for s in range(lanes):
        q = lax.rem(lane[0] - s + lanes, lanes)
        field[pl.ds(pl.multiple_of(q * share, share), share), :] = shares[s][...]

    def pack(c, _):
        for r in range(width):
            out[c, pl.ds(r, 1), :] = field[pl.ds(lists[c * width + r], 1), :]
        return 0

    lax.fori_loop(0, blocks, pack, 0)
    clear(banks)

    def step(i, _):
        for u in range(0, UNROLL, BANKS):
            at = second + i * UNROLL + u
            code = [order[at + k] for k in range(BANKS)]
            rows = [field[pl.ds(code[k] & 4095, 1), :] * heavy[at + k] for k in range(BANKS)]
            to = [pl.ds(code[k] >> 12, 1) for k in range(BANKS)]
            new = [banks[k][to[k], :] + rows[k] for k in range(BANKS)]
            for k in range(BANKS):
                banks[k][to[k], :] = new[k]
        return 0

    lax.fori_loop(0, trips(sizes[1]), step, 0)
    total = banks[0][...]
    for a in banks[1:]:
        total = total + a[...]
    for c in range(blocks):
        out[c, width:, :] = total[c * width : (c + 1) * width]


def near_kernel(sizes, order, heavy, field, out, *banks):
    clear(banks)

    def step(i, _):
        for u in range(0, UNROLL, BANKS):
            at = i * UNROLL + u
            code = [order[at + k] for k in range(BANKS)]
            mass = [heavy[at + k] for k in range(BANKS)]
            one = [pl.ds(code[k] & 4095, 1) for k in range(BANKS)]
            two = [pl.ds(code[k] >> 12, 1) for k in range(BANKS)]
            from_one = [field[one[k], :] * mass[k] for k in range(BANKS)]
            from_two = [field[two[k], :] * mass[k] for k in range(BANKS)]
            new = [banks[k][one[k], :] + from_two[k] for k in range(BANKS)]
            for k in range(BANKS):
                banks[k][one[k], :] = new[k]
            new = [banks[k][two[k], :] + from_one[k] for k in range(BANKS)]
            for k in range(BANKS):
                banks[k][two[k], :] = new[k]
        return 0

    lax.fori_loop(0, trips(sizes[0]), step, 0)
    total = banks[0][...]
    for a in banks[1:]:
        total = total + a[...]
    out[...] = total


def flow_join_kernel(lane, sizes, order, heavy, listed, near, arrived, *refs):
    lanes = 4
    outs, ret_both, hot, banks = refs[:lanes], refs[lanes], refs[lanes + 1], refs[lanes + 2 :]
    blocks, both, _ = arrived.shape
    width = both // 2
    rows = near.shape[0]
    share = rows // lanes
    second = order.shape[0] // 2
    halo = banks[-1]
    banks = banks[:-1]
    for c in range(blocks):
        halo[c * width : (c + 1) * width, :] = arrived[c, :width, :]
        put_split(ret_both, slice(c * width, (c + 1) * width), arrived[c, width:, :])

    def emit(i, got):
        at = pl.ds(pl.multiple_of(i * hot.shape[0], hot.shape[0]), hot.shape[0])
        banks[0][at, :] = near[at, :] + got

    scatter_back(ret_both, listed, hot, emit, rows)
    clear(banks[1:])

    def step(i, _):
        for u in range(0, UNROLL, BANKS):
            at = second + i * UNROLL + u
            code = [order[at + k] for k in range(BANKS)]
            got = [halo[pl.ds(code[k] >> 12, 1), :] * heavy[at + k] for k in range(BANKS)]
            to = [pl.ds(code[k] & 4095, 1) for k in range(BANKS)]
            new = [banks[k][to[k], :] + got[k] for k in range(BANKS)]
            for k in range(BANKS):
                banks[k][to[k], :] = new[k]
        return 0

    lax.fori_loop(0, trips(sizes[1]), step, 0)
    for s in range(lanes):
        q = lax.rem(lane[0] + s, lanes)
        at = pl.ds(pl.multiple_of(q * share, share), share)
        total = banks[0][at, :]
        for a in banks[1:]:
            total = total + a[at, :]
        outs[s][...] = total


def solution_kernel(lane, lists, *refs):
    lanes = 4
    shares, (field, out) = refs[:lanes], refs[lanes:]
    share = shares[0].shape[0]
    blocks, width, _ = out.shape
    for s in range(lanes):
        q = lax.rem(lane[0] - s + lanes, lanes)
        field[pl.ds(pl.multiple_of(q * share, share), share), :] = shares[s][...]

    def pack(c, _):
        for r in range(width):
            out[c, pl.ds(r, 1), :] = field[pl.ds(lists[c * width + r], 1), :]
        return 0

    lax.fori_loop(0, blocks, pack, 0)


def near_gap_kernel(count, source, target, field, gaps, more):
    rows = field.shape[0]
    more[:rows, :] = field[...]
    more[rows:, :] = jnp.zeros((more.shape[0] - rows, LANES), jnp.float32)

    def step(i, _):
        for u in range(UNROLL):
            e = i * UNROLL + u
            t = jnp.minimum(target[e], rows)
            gaps[pl.ds(e, 1), :] = field[pl.ds(source[e], 1), :] - more[pl.ds(t, 1), :]
        return 0

    lax.fori_loop(0, trips(count[0]), step, 0)


def far_gap_kernel(sizes, order, edge, near_gaps, halo, live, out, gaps):
    second = order.shape[0] // 2
    edges = near_gaps.shape[0]
    groups = edges // LANES
    gaps[:edges, :] = near_gaps[...]

    def step(i, _):
        left = sizes[1] - i * UNROLL
        for u in range(0, UNROLL, BANKS):
            at = second + i * UNROLL + u
            to = [pl.ds(jnp.where(u + k < left, edge[at + k], edges), 1) for k in range(BANKS)]
            new = [gaps[to[k], :] - halo[pl.ds(order[at + k] >> 12, 1), :] for k in range(BANKS)]
            for k in range(BANKS):
                gaps[to[k], :] = new[k]
        return 0

    lax.fori_loop(0, trips(sizes[1]), step, 0)
    for k in range(groups):
        gap = gaps[k * LANES : (k + 1) * LANES, :]
        total = jnp.sum((gap * gap).T, axis=0, keepdims=True)
        alive = live[k : k + 1, :]
        out[k : k + 1, :] = jnp.where(alive > 0, total * (alive / LANES), 0.0)


def passed_round(blocks, lanes, sign):
    return [blocks[0]] + [
        lax.ppermute(blocks[s], "edg", [(i, (i + sign * s) % lanes) for i in range(lanes)]) for s in (2, 1, 3)
    ]


def summed(blocks, lanes):
    got = passed_round(blocks, lanes, 1)
    return got[0] + got[1] + got[2] + got[3]


def to_all(mine, lanes):
    home, two, one, three = passed_round([mine] * lanes, lanes, 1)
    return [home, one, two, three]


def across(x):
    return lax.all_to_all(x, "vtx", split_axis=0, concat_axis=0, tiled=True)


def local(sketch_cols, edge_weight, ground, src_local, dst_index, send_rows, edge_count):
    blocks = lax.axis_size("vtx")
    lanes = lax.axis_size("edg")
    rows = ground.shape[0]
    edges = edge_weight.shape[0]
    width = send_rows.shape[2]
    slots = blocks * width
    share = rows // lanes
    groups = edges // LANES
    f32, i32, bf16 = jnp.float32, jnp.int32, jnp.bfloat16
    lane = lax.axis_index("edg").astype(i32).reshape(1)
    lists = send_rows[0].reshape(-1)
    listed = lists.reshape(slots // LANES, LANES)
    padded = jnp.pad(send_rows[0], ((0, 0), (0, LANES - width)), constant_values=-1)
    live = (jnp.arange(edges, dtype=i32) < edge_count[0]).astype(f32)
    weight = edge_weight * live
    root = jnp.sqrt(edge_weight) * live
    terms = root[:, None] * sketch_cols.astype(f32)
    live_rows = live.reshape(groups, LANES)
    weight_rows = weight.reshape(groups, LANES)
    source_rows = src_local.reshape(groups, LANES)
    target_rows = dst_index.reshape(groups, LANES)

    outgoing = call(
        functools.partial(halo_side_kernel, rows, slots, width),
        [((blocks, width + 8, LANES), f32, VMEM)],
        [VMEM] * 3,
        [pltpu.VMEM((edges, 2 * LANES), bf16), pltpu.VMEM((8 * width, edges), bf16)],
        "halo_side",
        flops=2 * slots * edges * 2 * LANES,
    )(terms, target_rows, weight_rows)[0]
    returned = across(outgoing)
    own, own_degree = call(
        own_side_kernel,
        [((rows, LANES), f32, VMEM), ((rows // LANES, LANES), f32, VMEM)],
        [VMEM] * 4,
        [pltpu.VMEM((edges, 2 * LANES), bf16), pltpu.VMEM((256, edges), bf16)],
        "own_side",
        flops=2 * rows * edges * 2 * LANES,
    )(terms, source_rows, target_rows, weight_rows)
    room = edges + LANES
    order, heavy, edge, sizes = call(
        functools.partial(partition_kernel, rows),
        [((2 * room,), i32, SMEM), ((2 * room,), f32, SMEM), ((2 * room,), i32, SMEM), ((2,), i32, SMEM)],
        [SMEM] * 4,
        [],
        "partition",
        moved=2**25,
    )(edge_count, src_local, dst_index, weight)
    sides = call(
        side_join_kernel,
        [((share + 8, LANES), f32, VMEM)] * lanes,
        [SMEM] + [VMEM] * 5,
        [pltpu.VMEM((rows, LANES), f32), pltpu.VMEM((slots, 2 * LANES), bf16), pltpu.VMEM((256, slots), bf16)],
        "side_join",
        flops=2 * rows * slots * 2 * LANES,
    )(lane, returned, listed, padded, own, own_degree)
    side = summed(sides, lanes)
    right_share = side[:share]
    degree_share = side[share : share + share // LANES].reshape(share)
    ground_share = lax.dynamic_slice_in_dim(ground, lane[0] * share, share)
    diagonal = (degree_share + ground_share)[:, None]
    inverse = 1.0 / diagonal

    first, pairs = chebyshev_terms(ITERS)
    residual = right_share
    direction = first * inverse * right_share
    solution_share = direction
    for keep, push in pairs:
        field, message = call(
            field_kernel,
            [((rows, LANES), f32, VMEM), ((blocks, 2 * width, LANES), f32, VMEM)],
            [SMEM] * 5 + [VMEM] * lanes,
            [pltpu.VMEM((slots, LANES), f32)] * BANKS,
            "field",
        )(lane, sizes, order, heavy, lists, *to_all(direction, lanes))
        arrived = across(message)
        near = call(
            near_kernel,
            [((rows, LANES), f32, VMEM)],
            [SMEM] * 3 + [VMEM],
            [pltpu.VMEM((rows, LANES), f32)] * BANKS,
            "near",
            moved=2**25,
        )(sizes, order, heavy, field)[0]
        flows = call(
            flow_join_kernel,
            [((share, LANES), f32, VMEM)] * lanes,
            [SMEM] * 4 + [VMEM] * 3,
            [pltpu.VMEM((slots, 2 * LANES), bf16), pltpu.VMEM((256, slots), bf16)]
            + [pltpu.VMEM((rows, LANES), f32)] * BANKS
            + [pltpu.VMEM((slots, LANES), f32)],
            "flow_join",
            flops=2 * rows * slots * 2 * LANES,
        )(lane, sizes, order, heavy, listed, near, arrived)
        residual = residual - (diagonal * direction - summed(flows, lanes))
        direction = keep * direction + push * inverse * residual
        solution_share = solution_share + direction
    field, message = call(
        solution_kernel,
        [((rows, LANES), f32, VMEM), ((blocks, width, LANES), f32, VMEM)],
        [SMEM] * 2 + [VMEM] * lanes,
        [],
        "solution_rows",
    )(lane, lists, *to_all(solution_share, lanes))
    halo = across(message)
    gaps = call(
        near_gap_kernel,
        [((edges, LANES), f32, VMEM)],
        [SMEM] * 3 + [VMEM],
        [pltpu.VMEM((rows + 8, LANES), f32)],
        "near_gap",
        moved=2**25,
    )(edge_count, src_local, dst_index, field)[0]
    resistance = call(
        far_gap_kernel,
        [((groups, LANES), f32, VMEM)],
        [SMEM] * 3 + [VMEM] * 3,
        [pltpu.VMEM((edges + 8, LANES), f32)],
        "far_gap",
    )(sizes, order, edge, gaps, halo.reshape(slots, LANES), live_rows)[0]
    return (field, resistance.reshape(edges))


def solution(mesh):
    in_specs = (
        P(("vtx", "edg"), None),
        P(("vtx", "edg")),
        P("vtx"),
        P(("vtx", "edg")),
        P(("vtx", "edg")),
        P(("vtx", "edg"), None, None),
        P(("vtx", "edg")),
    )
    out_specs = (P("vtx", None), P(("vtx", "edg")))
    return jax.shard_map(local, mesh=mesh, in_specs=in_specs, out_specs=out_specs, check_vma=False)
```

```python
import functools

import jax
import jax.numpy as jnp
from jax import lax
from jax.experimental import pallas as pl
from jax.experimental.pallas import tpu as pltpu
from jax.sharding import PartitionSpec as P

ITERS = 3
LANES = 128
UNROLL = 16
BANKS = 4

lam_low = 0.05
lam_high = 2.0

SMEM = pl.BlockSpec(memory_space=pltpu.SMEM)
VMEM = pl.BlockSpec(memory_space=pltpu.VMEM)
LIMIT = 40 * 2**20


def chebyshev_terms(steps):
    centre = (lam_high + lam_low) / 2.0
    half_width = (lam_high - lam_low) / 2.0
    sigma_val = centre / half_width
    rho_prev = 1.0 / sigma_val
    pairs = []
    for count_idx in range(steps - 1):
        rho_next = 1.0 / (2.0 * sigma_val - rho_prev)
        pairs.append((rho_next * rho_prev, 2.0 * rho_next / half_width))
        rho_prev = rho_next
    return (1.0 / centre, pairs)


def call(kernel, outs, ins, scratch, name, flops=0, moved=2**22):
    return pl.pallas_call(
        kernel,
        out_shape=[jax.ShapeDtypeStruct(shape, dtype) for shape, dtype, _ in outs],
        in_specs=ins,
        out_specs=[space for _, _, space in outs],
        scratch_shapes=scratch,
        compiler_params=pltpu.CompilerParams(vmem_limit_bytes=LIMIT),
        cost_estimate=pl.CostEstimate(flops=flops, bytes_accessed=moved, transcendentals=0),
        name=name,
    )


def split(x):
    high = x.astype(jnp.bfloat16)
    return high, (x - high.astype(jnp.float32)).astype(jnp.bfloat16)


def put_split(ref, rows, x):
    high, low = split(x)
    ref[rows, :LANES] = high
    ref[rows, LANES:] = low


def halves(x):
    return x[:, :LANES] + x[:, LANES:]


def one_hot(row, height, base):
    place = lax.broadcasted_iota(jnp.int32, (height, row.shape[1]), 0) + base
    return jnp.where(place == row, 1.0, 0.0)


def factored(pick, groups, high_of, low_of, weight_of, height):
    total = jnp.zeros((2 * height, LANES), jnp.float32)
    for k0 in range(0, groups, pick):
        left, right = [], []
        for k in range(k0, k0 + pick):
            member = one_hot(high_of(k), height, 0) * weight_of(k)
            high, low = split(member)
            left.append(jnp.concatenate([high, low], axis=0))
            right.append(one_hot(low_of(k), LANES, 0).astype(jnp.bfloat16))
        total = total + lax.dot_general(
            jnp.concatenate(left, axis=1),
            jnp.concatenate(right, axis=1),
            (((1,), (1,)), ((), ())),
            preferred_element_type=jnp.float32,
        )
    return total[:height] + total[height:]


def halo_side_kernel(rows, slots, width, terms, target, weight, out, both, hot):
    groups = target.shape[0]
    edges = terms.shape[0]
    put_split(both, slice(None), terms[...])
    tall = hot.shape[0]
    per = tall // width

    def chunk(i, _):
        base = rows + i * tall
        for k in range(groups):
            hot[:, k * LANES : (k + 1) * LANES] = one_hot(target[k : k + 1, :], tall, base).astype(jnp.bfloat16)
        got = halves(jnp.dot(hot[...], both[...], preferred_element_type=jnp.float32))
        for c in range(per):
            out[i * per + c, :width, :] = -got[c * width : (c + 1) * width]
        return 0

    lax.fori_loop(0, slots // tall, chunk, 0)
    blocks = slots // width

    def slot(k):
        return target[k : k + 1, :] - rows

    def block_of(k):
        return jnp.where(slot(k) < 0, -1, lax.shift_right_arithmetic(slot(k) * 1366, 16))

    def within(k):
        return slot(k) - block_of(k) * width

    deg = factored(4, groups, block_of, within, lambda k: weight[k : k + 1, :], blocks)
    for c in range(blocks):
        out[c, width : width + 8, :] = jnp.broadcast_to(deg[c : c + 1, :], (8, LANES))


def own_side_kernel(terms, source, target, weight, out, degree, both, hot):
    groups = target.shape[0]
    rows = out.shape[0]
    put_split(both, slice(None), terms[...])
    tall = hot.shape[0]

    def chunk(i, _):
        base = i * tall
        for k in range(groups):
            plus = one_hot(source[k : k + 1, :], tall, base)
            minus = one_hot(target[k : k + 1, :], tall, base)
            hot[:, k * LANES : (k + 1) * LANES] = (plus - minus).astype(jnp.bfloat16)
        out[pl.ds(pl.multiple_of(i * tall, tall), tall), :] = halves(
            jnp.dot(hot[...], both[...], preferred_element_type=jnp.float32)
        )
        return 0

    lax.fori_loop(0, rows // tall, chunk, 0)

    def total(ref):
        return factored(
            4,
            groups,
            lambda k: lax.shift_right_logical(ref[k : k + 1, :], 7),
            lambda k: ref[k : k + 1, :] & (LANES - 1),
            lambda k: weight[k : k + 1, :],
            rows // LANES,
        )

    degree[...] = total(source) + total(target)


def scatter_back(ret_both, listed, hot, emit, rows):
    tall = hot.shape[0]
    groups = listed.shape[0]

    def chunk(i, _):
        base = i * tall
        for k in range(groups):
            hot[:, k * LANES : (k + 1) * LANES] = one_hot(listed[k : k + 1, :], tall, base).astype(jnp.bfloat16)
        emit(i, halves(jnp.dot(hot[...], ret_both[...], preferred_element_type=jnp.float32)))
        return 0

    lax.fori_loop(0, rows // tall, chunk, 0)


def side_join_kernel(lane, returned, listed, padded, own, own_degree, *refs):
    lanes = 4
    outs, (acc, ret_both, hot) = refs[:lanes], refs[lanes:]
    blocks = returned.shape[0]
    rows = own.shape[0]
    width = listed.shape[0] * LANES // blocks
    share = rows // lanes
    for c in range(blocks):
        put_split(ret_both, slice(c * width, (c + 1) * width), returned[c, :width, :])

    def emit(i, got):
        at = pl.ds(pl.multiple_of(i * hot.shape[0], hot.shape[0]), hot.shape[0])
        acc[at, :] = own[at, :] + got

    scatter_back(ret_both, listed, hot, emit, rows)
    deg = own_degree[...] + factored(
        4,
        blocks,
        lambda k: lax.shift_right_arithmetic(padded[k : k + 1, :], 7),
        lambda k: padded[k : k + 1, :] & (LANES - 1),
        lambda k: returned[k, width : width + 1, :],
        rows // LANES,
    )
    deg_rows = share // LANES
    for s in range(lanes):
        q = lax.rem(lane[0] + s, lanes)
        outs[s][:share, :] = acc[pl.ds(pl.multiple_of(q * share, share), share), :]
        row = jnp.zeros((8, LANES), jnp.float32)
        place = lax.broadcasted_iota(jnp.int32, (8, LANES), 0)
        for p in range(lanes):
            for d in range(deg_rows):
                one = jnp.broadcast_to(deg[p * deg_rows + d : p * deg_rows + d + 1, :], (8, LANES))
                row = jnp.where((place == d) & (q == p), one, row)
        outs[s][share : share + 8, :] = row


def trips(n):
    return lax.div(n + UNROLL - 1, UNROLL)


def clear(banks):
    for a in banks:
        a[...] = jnp.zeros_like(a)


def matrix_kernel(count, place, mass, high, low, acc):
    flat = acc.shape[0]
    chunk = 2048

    def wipe(i, _):
        acc[pl.ds(pl.multiple_of(i * chunk, chunk), chunk), :] = jnp.zeros((chunk, LANES), jnp.float32)
        return 0

    lax.fori_loop(0, flat // chunk, wipe, 0)
    column = lax.broadcasted_iota(jnp.int32, (1, LANES), 1)

    def step(i, _):
        for u in range(0, UNROLL, 2):
            e = i * UNROLL + u
            p, q = place[e], place[e + 1]
            rp, rq = lax.shift_right_logical(p, 7), lax.shift_right_logical(q, 7)
            one = jnp.where(column == (p & (LANES - 1)), mass[e], 0.0)
            two = jnp.where(column == (q & (LANES - 1)), mass[e + 1], 0.0)
            two = two + one * (rp == rq).astype(jnp.float32)
            one = one + acc[pl.ds(rp, 1), :]
            two = two + acc[pl.ds(rq, 1), :]
            acc[pl.ds(rp, 1), :] = one
            acc[pl.ds(rq, 1), :] = two
        return 0

    lax.fori_loop(0, trips(count[0]), step, 0)
    slots = high.shape[1]

    def part(i, _):
        top, rest = split(acc[pl.ds(pl.multiple_of(i * slots, slots), slots), :])
        high[i] = top
        low[i] = rest
        return 0

    lax.fori_loop(0, high.shape[0], part, 0)


def send_kernel(shifts, first, lanes, lane, high, low, wanted, *refs):
    shares = refs[: len(shifts)]
    before, (out, both) = (None, refs[-2:]) if first else (refs[len(shifts)], refs[-2:])
    blocks, wide, _ = out.shape
    width = wide // 2
    share = shares[0].shape[0]
    tiles = share // LANES
    tall = 8 * width
    for n, (s, mine) in enumerate(zip(shifts, shares)):
        q = lax.rem(lane[0] - s + lanes, lanes)
        put_split(both, slice(None), mine[...])

        def chunk(i, _):
            at = pl.ds(pl.multiple_of(i * tall, tall), tall)
            want = wanted[at, :] - q * share
            column = lax.broadcasted_iota(jnp.int32, (tall, LANES), 1)
            hot = jnp.concatenate(
                [jnp.where(want == column + k * LANES, 1.0, 0.0).astype(jnp.bfloat16) for k in range(tiles)], axis=1
            )
            top = jnp.concatenate([high[q * tiles + k, at, :] for k in range(tiles)], axis=1)
            rest = jnp.concatenate([low[q * tiles + k, at, :] for k in range(tiles)], axis=1)
            rows = both[...]
            copied = halves(jnp.dot(hot, rows, preferred_element_type=jnp.float32))
            summed_at = halves(
                jnp.dot(top, rows, preferred_element_type=jnp.float32)
                + jnp.dot(rest, rows, preferred_element_type=jnp.float32)
            )
            old = out if n else before
            for c in range(8):
                a, b = copied[c * width : (c + 1) * width], summed_at[c * width : (c + 1) * width]
                if old is not None:
                    a = a + old[i * 8 + c, :width, :]
                    b = b + old[i * 8 + c, width:, :]
                out[i * 8 + c, :width, :] = a
                out[i * 8 + c, width:, :] = b
            return 0

        lax.fori_loop(0, blocks // 8, chunk, 0)


def near_kernel(lanes, lane, count, order, heavy, *refs):
    shares, (out, field), banks = refs[:lanes], refs[lanes : lanes + 2], refs[lanes + 2 :]
    share = shares[0].shape[0]
    for s in range(lanes):
        q = lax.rem(lane[0] - s + lanes, lanes)
        field[pl.ds(pl.multiple_of(q * share, share), share), :] = shares[s][...]
    clear(banks)

    def step(i, _):
        for u in range(0, UNROLL, BANKS):
            at = i * UNROLL + u
            code = [order[at + k] for k in range(BANKS)]
            mass = [heavy[at + k] for k in range(BANKS)]
            one = [pl.ds(code[k] & 4095, 1) for k in range(BANKS)]
            two = [pl.ds(lax.shift_right_logical(code[k], 12), 1) for k in range(BANKS)]
            from_one = [field[one[k], :] * mass[k] for k in range(BANKS)]
            from_two = [field[two[k], :] * mass[k] for k in range(BANKS)]
            new = [banks[k][one[k], :] + from_two[k] for k in range(BANKS)]
            for k in range(BANKS):
                banks[k][one[k], :] = new[k]
            new = [banks[k][two[k], :] + from_one[k] for k in range(BANKS)]
            for k in range(BANKS):
                banks[k][two[k], :] = new[k]
        return 0

    lax.fori_loop(0, trips(count[0]), step, 0)
    total = banks[0][...]
    for a in banks[1:]:
        total = total + a[...]
    out[...] = total


def land_kernel(arrived, turned, ret_both, halo):
    blocks, wide, _ = arrived.shape
    width = wide // 2
    for c in range(blocks):
        halo[c * width : (c + 1) * width, :] = arrived[c, :width, :]
        put_split(ret_both, slice(c * width, (c + 1) * width), arrived[c, width:, :])
    for k in range(halo.shape[0] // LANES):
        at = slice(k * LANES, (k + 1) * LANES)
        top, rest = split(halo[at, :].T)
        turned[:LANES, at] = top
        turned[LANES:, at] = rest


def join(q, high, low, listed, near, turned, ret_both, out, hot):
    share = out.shape[0]
    tiles = share // LANES
    for k in range(listed.shape[0]):
        hot[:, k * LANES : (k + 1) * LANES] = one_hot(listed[k : k + 1, :], share, q * share).astype(jnp.bfloat16)
    got = halves(jnp.dot(hot[...], ret_both[...], preferred_element_type=jnp.float32))
    top = jnp.concatenate([high[q * tiles + k] for k in range(tiles)], axis=1)
    rest = jnp.concatenate([low[q * tiles + k] for k in range(tiles)], axis=1)
    sides = jnp.dot(turned[...], top, preferred_element_type=jnp.float32)
    more = jnp.dot(turned[:LANES, :], rest, preferred_element_type=jnp.float32)
    back = sides[:LANES] + sides[LANES:] + more
    for k in range(tiles):
        at = pl.ds(pl.multiple_of(q * share + k * LANES, LANES), LANES)
        part = slice(k * LANES, (k + 1) * LANES)
        out[part, :] = near[at, :] + got[part] + back[:, part].T


def first_join_kernel(shift, lanes, lane, high, low, listed, near, arrived, out, turned, ret_both, halo, hot):
    land_kernel(arrived, turned, ret_both, halo)
    join(lax.rem(lane[0] + shift, lanes), high, low, listed, near, turned, ret_both, out, hot)


def join_kernel(shifts, lanes, lane, high, low, listed, near, turned, ret_both, *refs):
    outs, hot = refs[:-1], refs[-1]
    for s, out in zip(shifts, outs):
        join(lax.rem(lane[0] + s, lanes), high, low, listed, near, turned, ret_both, out, hot)


def solution_kernel(lane, lists, *refs):
    lanes = 4
    shares, (field, out) = refs[:lanes], refs[lanes:]
    share = shares[0].shape[0]
    blocks, width, _ = out.shape
    for s in range(lanes):
        q = lax.rem(lane[0] - s + lanes, lanes)
        field[pl.ds(pl.multiple_of(q * share, share), share), :] = shares[s][...]

    def pack(c, _):
        for r in range(width):
            out[c, pl.ds(r, 1), :] = field[pl.ds(lists[c * width + r], 1), :]
        return 0

    lax.fori_loop(0, blocks, pack, 0)


def near_gap_kernel(count, order, field, gaps, more):
    rows = field.shape[0]
    more[:rows, :] = field[...]
    more[rows:, :] = jnp.zeros((more.shape[0] - rows, LANES), jnp.float32)

    def step(i, _):
        for u in range(UNROLL):
            e = i * UNROLL + u
            code = order[e]
            gaps[pl.ds(e, 1), :] = (
                field[pl.ds(code & 4095, 1), :] - more[pl.ds(lax.shift_right_logical(code, 12), 1), :]
            )
        return 0

    lax.fori_loop(0, trips(count[0]), step, 0)


def far_gap_kernel(count, slot, gaps, halo, live, out, more, taken):
    slots = halo.shape[0]
    groups = live.shape[0]
    more[:slots, :] = halo[...]
    more[slots:, :] = jnp.zeros((more.shape[0] - slots, LANES), jnp.float32)

    def step(i, _):
        for u in range(UNROLL):
            e = i * UNROLL + u
            taken[pl.ds(e, 1), :] = more[pl.ds(slot[e], 1), :]
        return 0

    lax.fori_loop(0, trips(count[0]), step, 0)
    for k in range(groups):
        at = slice(k * LANES, (k + 1) * LANES)
        gap = gaps[at, :] - taken[at, :]
        total = jnp.sum((gap * gap).T, axis=0, keepdims=True)
        alive = live[k : k + 1, :]
        out[k : k + 1, :] = jnp.where(alive > 0, total * (alive / LANES), 0.0)


def passed_round(blocks, lanes, sign):
    return [blocks[0]] + [
        lax.ppermute(blocks[s], "edg", [(i, (i + sign * s) % lanes) for i in range(lanes)]) for s in (2, 1, 3)
    ]


def summed(blocks, lanes):
    got = passed_round(blocks, lanes, 1)
    return got[0] + got[1] + got[2] + got[3]


def to_all(mine, lanes):
    home, two, one, three = passed_round([mine] * lanes, lanes, 1)
    return (home, one, two, three)


def across(x):
    return lax.all_to_all(x, "vtx", split_axis=0, concat_axis=0, tiled=True)


def local(sketch_cols, edge_weight, ground, src_local, dst_index, send_rows, edge_count):
    blocks = lax.axis_size("vtx")
    lanes = lax.axis_size("edg")
    rows = ground.shape[0]
    edges = edge_weight.shape[0]
    width = send_rows.shape[2]
    slots = blocks * width
    share = rows // lanes
    groups = edges // LANES
    f32, i32, bf16 = jnp.float32, jnp.int32, jnp.bfloat16
    lane = lax.axis_index("edg").astype(i32).reshape(1)
    lists = send_rows[0].reshape(-1)
    listed = lists.reshape(slots // LANES, LANES)
    padded = jnp.pad(send_rows[0], ((0, 0), (0, LANES - width)), constant_values=-1)
    live = (jnp.arange(edges, dtype=i32) < edge_count[0]).astype(f32)
    weight = edge_weight * live
    root = jnp.sqrt(edge_weight) * live
    terms = root[:, None] * sketch_cols.astype(f32)
    live_rows = live.reshape(groups, LANES)
    weight_rows = weight.reshape(groups, LANES)
    source_rows = src_local.reshape(groups, LANES)
    target_rows = dst_index.reshape(groups, LANES)

    outgoing = call(
        functools.partial(halo_side_kernel, rows, slots, width),
        [((blocks, width + 8, LANES), f32, VMEM)],
        [VMEM] * 3,
        [pltpu.VMEM((edges, 2 * LANES), bf16), pltpu.VMEM((8 * width, edges), bf16)],
        "halo_side",
        flops=2 * slots * edges * 2 * LANES,
    )(terms, target_rows, weight_rows)[0]
    returned = across(outgoing)
    own, own_degree = call(
        own_side_kernel,
        [((rows, LANES), f32, VMEM), ((rows // LANES, LANES), f32, VMEM)],
        [VMEM] * 4,
        [pltpu.VMEM((edges, 2 * LANES), bf16), pltpu.VMEM((256, edges), bf16)],
        "own_side",
        flops=2 * rows * edges * 2 * LANES,
    )(terms, source_rows, target_rows, weight_rows)
    sides = call(
        side_join_kernel,
        [((share + 8, LANES), f32, VMEM)] * lanes,
        [SMEM] + [VMEM] * 5,
        [pltpu.VMEM((rows, LANES), f32), pltpu.VMEM((slots, 2 * LANES), bf16), pltpu.VMEM((256, slots), bf16)],
        "side_join",
        flops=2 * rows * slots * 2 * LANES,
    )(lane, returned, listed, padded, own, own_degree)
    side = summed(sides, lanes)
    right_share = side[:share]
    degree_share = side[share : share + share // LANES].reshape(share)
    ground_share = lax.dynamic_slice_in_dim(ground, lane[0] * share, share)
    diagonal = (degree_share + ground_share)[:, None]
    inverse = 1.0 / diagonal

    away = dst_index >= rows
    slot = jnp.where(away, dst_index - rows, 0)
    place = (lax.shift_right_logical(src_local, 7) * slots + slot) * LANES + (src_local & (LANES - 1))
    place = jnp.where(away, place, 0)
    far_weight = jnp.where(away, weight, 0.0)
    near_weight = jnp.where(away, 0.0, weight)
    near_order = src_local | (jnp.where(away, 0, dst_index) << 12)
    gap_order = src_local | (jnp.minimum(dst_index, rows) << 12)
    gap_slot = jnp.where(away, dst_index - rows, slots)
    wanted = jnp.broadcast_to(lists[:, None], (slots, LANES))
    tiles = rows // LANES
    high, low = call(
        matrix_kernel,
        [((tiles, slots, LANES), bf16, VMEM)] * 2,
        [SMEM] * 3,
        [pltpu.VMEM((tiles * slots, LANES), f32)],
        "matrix",
        moved=2**25,
    )(edge_count, place, far_weight)

    first, pairs = chebyshev_terms(ITERS)
    residual = right_share
    direction = first * inverse * right_share
    solution_share = direction
    message_shape = ((blocks, 2 * width, LANES), f32, VMEM)

    def send(shifts, before, parts):
        return call(
            functools.partial(send_kernel, shifts, before is None, lanes),
            [message_shape],
            [SMEM] + [VMEM] * (3 + len(parts) + (before is not None)),
            [pltpu.VMEM((share, 2 * LANES), bf16)],
            "send",
            flops=6 * slots * share * 2 * LANES * len(parts),
        )(lane, high, low, wanted, *parts, *(() if before is None else (before,)))[0]

    for keep, push in pairs:
        parts = to_all(direction, lanes)
        message = send((0,), None, parts[:1])
        message = send((1, 3), message, (parts[1], parts[3]))
        message = send((2,), message, parts[2:3])
        arrived = across(message)
        near = call(
            functools.partial(near_kernel, lanes),
            [((rows, LANES), f32, VMEM)],
            [SMEM] * 4 + [VMEM] * lanes,
            [pltpu.VMEM((rows, LANES), f32)] * (1 + BANKS),
            "near",
            moved=2**25,
        )(lane, edge_count, near_order, near_weight, *parts)[0]
        two, turned, ret_both = call(
            functools.partial(first_join_kernel, 2, lanes),
            [((share, LANES), f32, VMEM), ((2 * LANES, slots), bf16, VMEM), ((slots, 2 * LANES), bf16, VMEM)],
            [SMEM] + [VMEM] * 5,
            [pltpu.VMEM((slots, LANES), f32), pltpu.VMEM((share, slots), bf16)],
            "join_two",
            flops=6 * share * slots * 2 * LANES,
        )(lane, high, low, listed, near, arrived)
        one, three = call(
            functools.partial(join_kernel, (1, 3), lanes),
            [((share, LANES), f32, VMEM)] * 2,
            [SMEM] + [VMEM] * 6,
            [pltpu.VMEM((share, slots), bf16)],
            "join_one_three",
            flops=12 * share * slots * 2 * LANES,
        )(lane, high, low, listed, near, turned, ret_both)
        home = call(
            functools.partial(join_kernel, (0,), lanes),
            [((share, LANES), f32, VMEM)],
            [SMEM] + [VMEM] * 6,
            [pltpu.VMEM((share, slots), bf16)],
            "join_home",
            flops=6 * share * slots * 2 * LANES,
        )(lane, high, low, listed, near, turned, ret_both)[0]
        flows = summed((home, one, two, three), lanes)
        residual = residual - (diagonal * direction - flows)
        direction = keep * direction + push * inverse * residual
        solution_share = solution_share + direction
    field, message = call(
        solution_kernel,
        [((rows, LANES), f32, VMEM), ((blocks, width, LANES), f32, VMEM)],
        [SMEM] * 2 + [VMEM] * lanes,
        [],
        "solution_rows",
    )(lane, lists, *to_all(solution_share, lanes))
    halo = across(message)
    gaps = call(
        near_gap_kernel,
        [((edges, LANES), f32, VMEM)],
        [SMEM] * 2 + [VMEM],
        [pltpu.VMEM((rows + 8, LANES), f32)],
        "near_gap",
        moved=2**25,
    )(edge_count, gap_order, field)[0]
    resistance = call(
        far_gap_kernel,
        [((groups, LANES), f32, VMEM)],
        [SMEM] * 2 + [VMEM] * 3,
        [pltpu.VMEM((slots + 8, LANES), f32), pltpu.VMEM((edges, LANES), f32)],
        "far_gap",
    )(edge_count, gap_slot, gaps, halo.reshape(slots, LANES), live_rows)[0]
    return (field, resistance.reshape(edges))


def solution(mesh):
    in_specs = (
        P(("vtx", "edg"), None),
        P(("vtx", "edg")),
        P("vtx"),
        P(("vtx", "edg")),
        P(("vtx", "edg")),
        P(("vtx", "edg"), None, None),
        P(("vtx", "edg")),
    )
    out_specs = (P("vtx", None), P(("vtx", "edg")))
    return jax.shard_map(local, mesh=mesh, in_specs=in_specs, out_specs=out_specs, check_vma=False)
```

```python
import functools

import jax
import jax.numpy as jnp
from jax import lax
from jax.experimental import pallas as pl
from jax.experimental.pallas import tpu as pltpu
from jax.sharding import PartitionSpec as P

ITERS = 3
LANES = 128
UNROLL = 16
BANKS = 4

lam_low = 0.05
lam_high = 2.0

SMEM = pl.BlockSpec(memory_space=pltpu.SMEM)
VMEM = pl.BlockSpec(memory_space=pltpu.VMEM)
ANY = pl.BlockSpec(memory_space=pl.ANY)
LIMIT = 24 * 2**20


def chebyshev_terms(steps):
    centre = (lam_high + lam_low) / 2.0
    half_width = (lam_high - lam_low) / 2.0
    sigma_val = centre / half_width
    rho_prev = 1.0 / sigma_val
    pairs = []
    for count_idx in range(steps - 1):
        rho_next = 1.0 / (2.0 * sigma_val - rho_prev)
        pairs.append((rho_next * rho_prev, 2.0 * rho_next / half_width))
        rho_prev = rho_next
    return (1.0 / centre, pairs)


def call(kernel, outs, ins, scratch, name, flops=0, moved=2**22):
    return pl.pallas_call(
        kernel,
        out_shape=[jax.ShapeDtypeStruct(shape, dtype) for shape, dtype, _ in outs],
        in_specs=ins,
        out_specs=[space for _, _, space in outs],
        scratch_shapes=scratch,
        compiler_params=pltpu.CompilerParams(vmem_limit_bytes=LIMIT),
        cost_estimate=pl.CostEstimate(flops=flops, bytes_accessed=moved, transcendentals=0),
        name=name,
    )


def split(x):
    high = x.astype(jnp.bfloat16)
    return high, (x - high.astype(jnp.float32)).astype(jnp.bfloat16)


def put_split(ref, rows, x):
    high, low = split(x)
    ref[rows, :LANES] = high
    ref[rows, LANES:] = low


def halves(x):
    return x[:, :LANES] + x[:, LANES:]


def one_hot(row, height, base):
    place = lax.broadcasted_iota(jnp.int32, (height, row.shape[1]), 0) + base
    return jnp.where(place == row, 1.0, 0.0)


def factored(pick, groups, high_of, low_of, weight_of, height):
    total = jnp.zeros((2 * height, LANES), jnp.float32)
    for k0 in range(0, groups, pick):
        left, right = [], []
        for k in range(k0, k0 + pick):
            member = one_hot(high_of(k), height, 0) * weight_of(k)
            high, low = split(member)
            left.append(jnp.concatenate([high, low], axis=0))
            right.append(one_hot(low_of(k), LANES, 0).astype(jnp.bfloat16))
        total = total + lax.dot_general(
            jnp.concatenate(left, axis=1),
            jnp.concatenate(right, axis=1),
            (((1,), (1,)), ((), ())),
            preferred_element_type=jnp.float32,
        )
    return total[:height] + total[height:]


def halo_side_kernel(rows, slots, width, terms, target, weight, sent, both, hot, out, leave):
    groups = target.shape[0]
    edges = terms.shape[0]
    put_split(both, slice(None), terms[...])
    tall = hot.shape[0]
    per = tall // width

    def chunk(i, _):
        base = rows + i * tall
        for k in range(groups):
            hot[:, k * LANES : (k + 1) * LANES] = one_hot(target[k : k + 1, :], tall, base).astype(jnp.bfloat16)
        got = halves(jnp.dot(hot[...], both[...], preferred_element_type=jnp.float32))
        for c in range(per):
            out[i * per + c, :width, :] = -got[c * width : (c + 1) * width]
        return 0

    lax.fori_loop(0, slots // tall, chunk, 0)
    blocks = slots // width

    def slot(k):
        return target[k : k + 1, :] - rows

    def block_of(k):
        return jnp.where(slot(k) < 0, -1, lax.shift_right_arithmetic(slot(k) * 1366, 16))

    def within(k):
        return slot(k) - block_of(k) * width

    deg = factored(4, groups, block_of, within, lambda k: weight[k : k + 1, :], blocks)
    for c in range(blocks):
        out[c, width : width + 8, :] = jnp.broadcast_to(deg[c : c + 1, :], (8, LANES))
    go = pltpu.make_async_copy(out, sent, leave)
    go.start()
    go.wait()


def own_side_kernel(terms, source, target, weight, out, degree, both, hot):
    groups = target.shape[0]
    rows = out.shape[0]
    put_split(both, slice(None), terms[...])
    tall = hot.shape[0]

    def chunk(i, _):
        base = i * tall
        for k in range(groups):
            plus = one_hot(source[k : k + 1, :], tall, base)
            minus = one_hot(target[k : k + 1, :], tall, base)
            hot[:, k * LANES : (k + 1) * LANES] = (plus - minus).astype(jnp.bfloat16)
        out[pl.ds(pl.multiple_of(i * tall, tall), tall), :] = halves(
            jnp.dot(hot[...], both[...], preferred_element_type=jnp.float32)
        )
        return 0

    lax.fori_loop(0, rows // tall, chunk, 0)

    def total(ref):
        return factored(
            4,
            groups,
            lambda k: lax.shift_right_logical(ref[k : k + 1, :], 7),
            lambda k: ref[k : k + 1, :] & (LANES - 1),
            lambda k: weight[k : k + 1, :],
            rows // LANES,
        )

    degree[...] = total(source) + total(target)


def scatter_back(ret_both, listed, hot, emit, rows):
    tall = hot.shape[0]
    groups = listed.shape[0]

    def chunk(i, _):
        base = i * tall
        for k in range(groups):
            hot[:, k * LANES : (k + 1) * LANES] = one_hot(listed[k : k + 1, :], tall, base).astype(jnp.bfloat16)
        emit(i, halves(jnp.dot(hot[...], ret_both[...], preferred_element_type=jnp.float32)))
        return 0

    lax.fori_loop(0, rows // tall, chunk, 0)


def side_join_kernel(lane, returned, listed, padded, own, own_degree, *refs):
    lanes = 4
    outs, (acc, ret_both, hot, landed, arrival) = refs[:lanes], refs[lanes:]
    come = pltpu.make_async_copy(returned, landed, arrival)
    come.start()
    blocks = returned.shape[0]
    rows = own.shape[0]
    width = listed.shape[0] * LANES // blocks
    share = rows // lanes
    come.wait()
    for c in range(blocks):
        put_split(ret_both, slice(c * width, (c + 1) * width), landed[c, :width, :])

    def emit(i, got):
        at = pl.ds(pl.multiple_of(i * hot.shape[0], hot.shape[0]), hot.shape[0])
        acc[at, :] = own[at, :] + got

    scatter_back(ret_both, listed, hot, emit, rows)
    deg = own_degree[...] + factored(
        4,
        blocks,
        lambda k: lax.shift_right_arithmetic(padded[k : k + 1, :], 7),
        lambda k: padded[k : k + 1, :] & (LANES - 1),
        lambda k: landed[k, width : width + 1, :],
        rows // LANES,
    )
    deg_rows = share // LANES
    for s in range(lanes):
        q = lax.rem(lane[0] + s, lanes)
        outs[s][:share, :] = acc[pl.ds(pl.multiple_of(q * share, share), share), :]
        row = jnp.zeros((8, LANES), jnp.float32)
        place = lax.broadcasted_iota(jnp.int32, (8, LANES), 0)
        for p in range(lanes):
            for d in range(deg_rows):
                one = jnp.broadcast_to(deg[p * deg_rows + d : p * deg_rows + d + 1, :], (8, LANES))
                row = jnp.where((place == d) & (q == p), one, row)
        outs[s][share : share + 8, :] = row


def far_list_kernel(begin, end, count, order, mass, code, heavy, size):
    def step(i, at):
        e = begin + i * 8
        given = [order[e + u] for u in range(8)]
        loads = [mass[e + u] for u in range(8)]
        for u in range(8):
            code[at] = given[u]
            heavy[at] = loads[u]
            at = at + 1 + lax.shift_right_arithmetic(given[u], 31)
        return at

    live = jnp.clip(count[0] - begin, 0, end - begin)
    at = lax.fori_loop(0, lax.div(live + 7, 8), step, 0)
    for u in range(UNROLL):
        code[at + u] = 0
        heavy[at + u] = 0.0
    size[0] = at


def trips(n):
    return lax.div(n + UNROLL - 1, UNROLL)


def clear(banks):
    for a in banks:
        a[...] = jnp.zeros_like(a)


def far_rows(lists, take, give, banks):
    for code, heavy, size in lists:

        def step(i, _):
            for u in range(0, UNROLL, BANKS):
                at = i * UNROLL + u
                given = [code[at + k] for k in range(BANKS)]
                rows = [take(given[k]) * heavy[at + k] for k in range(BANKS)]
                to = [pl.ds(give(given[k]), 1) for k in range(BANKS)]
                new = [banks[k][to[k], :] + rows[k] for k in range(BANKS)]
                for k in range(BANKS):
                    banks[k][to[k], :] = new[k]
            return 0

        lax.fori_loop(0, trips(size[0]), step, 0)


def source_of(given):
    return given & 4095


def target_of(given):
    return lax.shift_right_logical(given, 12)


def assemble(lane, lanes, shares, field):
    share = shares[0].shape[0]
    for s in range(lanes):
        q = lax.rem(lane[0] - s + lanes, lanes)
        field[pl.ds(pl.multiple_of(q * share, share), share), :] = shares[s][...]


def pack(lists, field, out, width):
    def step(c, _):
        for r in range(width):
            out[c, pl.ds(r, 1), :] = field[pl.ds(lists[c * width + r], 1), :]
        return 0

    lax.fori_loop(0, out.shape[0], step, 0)


def field_kernel(lane, rows_a, mass_a, size_a, rows_b, mass_b, size_b, lists, *refs):
    lanes = 4
    shares, (field, sent), refs = refs[:lanes], refs[lanes : lanes + 2], refs[lanes + 2 :]
    out, sums, leave, leave_more = refs[:4]
    banks = refs[4:]
    blocks, width, _ = out.shape
    assemble(lane, lanes, shares, field)
    pack(lists, field, out, width)
    go = pltpu.make_async_copy(out, sent.at[:, :width, :], leave)
    go.start()
    clear(banks)
    far_rows(
        ((rows_a, mass_a, size_a), (rows_b, mass_b, size_b)),
        lambda given: field[pl.ds(source_of(given), 1), :],
        target_of,
        banks,
    )
    total = banks[0][...]
    for a in banks[1:]:
        total = total + a[...]
    for c in range(blocks):
        sums[c] = total[c * width : (c + 1) * width]
    more = pltpu.make_async_copy(sums, sent.at[:, width:, :], leave_more)
    more.start()
    go.wait()
    more.wait()


def near_kernel(count, order, heavy, field, out, *banks):
    clear(banks)

    def step(i, _):
        for u in range(0, UNROLL, BANKS):
            at = i * UNROLL + u
            code = [order[at + k] for k in range(BANKS)]
            mass = [heavy[at + k] for k in range(BANKS)]
            one = [pl.ds(source_of(code[k]), 1) for k in range(BANKS)]
            two = [pl.ds(target_of(code[k]), 1) for k in range(BANKS)]
            from_one = [field[one[k], :] * mass[k] for k in range(BANKS)]
            from_two = [field[two[k], :] * mass[k] for k in range(BANKS)]
            new = [banks[k][one[k], :] + from_two[k] for k in range(BANKS)]
            for k in range(BANKS):
                banks[k][one[k], :] = new[k]
            new = [banks[k][two[k], :] + from_one[k] for k in range(BANKS)]
            for k in range(BANKS):
                banks[k][two[k], :] = new[k]
        return 0

    lax.fori_loop(0, trips(count[0]), step, 0)
    total = banks[0][...]
    for a in banks[1:]:
        total = total + a[...]
    out[...] = total


def share_block(q, listed, far, ret_both, hot, out):
    share = out.shape[0]
    for k in range(listed.shape[0]):
        hot[:, k * LANES : (k + 1) * LANES] = one_hot(listed[k : k + 1, :], share, q * share).astype(jnp.bfloat16)
    got = halves(jnp.dot(hot[...], ret_both[...], preferred_element_type=jnp.float32))
    out[...] = far[pl.ds(pl.multiple_of(q * share, share), share), :] + got


def first_join_kernel(
    shift, lanes, lane, rows_a, mass_a, size_a, rows_b, mass_b, size_b, listed, near, arrived, *refs
):
    out, far, ret_both, hot, halo, ret, come_halo, come_ret = refs[:8]
    banks = refs[8:]
    blocks, width, _ = halo.shape
    first = pltpu.make_async_copy(arrived.at[:, :width, :], halo, come_halo)
    second = pltpu.make_async_copy(arrived.at[:, width:, :], ret, come_ret)
    first.start()
    second.start()
    clear(banks)
    first.wait()
    flat = halo.reshape(blocks * width, LANES)
    far_rows(
        ((rows_a, mass_a, size_a), (rows_b, mass_b, size_b)),
        lambda given: flat[pl.ds(target_of(given), 1), :],
        source_of,
        banks,
    )
    total = near[...]
    for a in banks:
        total = total + a[...]
    far[...] = total
    second.wait()
    for c in range(blocks):
        put_split(ret_both, slice(c * width, (c + 1) * width), ret[c])
    share_block(lax.rem(lane[0] + shift, lanes), listed, far, ret_both, hot, out)


def join_kernel(shifts, lanes, lane, listed, far, ret_both, *refs):
    outs, hot = refs[:-1], refs[-1]
    for s, out in zip(shifts, outs):
        share_block(lax.rem(lane[0] + s, lanes), listed, far, ret_both, hot, out)


def solution_kernel(lane, lists, *refs):
    lanes = 4
    shares, (field, sent, out, leave) = refs[:lanes], refs[lanes:]
    assemble(lane, lanes, shares, field)
    pack(lists, field, out, out.shape[1])
    go = pltpu.make_async_copy(out, sent, leave)
    go.start()
    go.wait()


def near_gap_kernel(count, order, field, gaps, more):
    rows = field.shape[0]
    more[:rows, :] = field[...]
    more[rows:, :] = jnp.zeros((more.shape[0] - rows, LANES), jnp.float32)

    def step(i, _):
        for u in range(UNROLL):
            e = i * UNROLL + u
            code = order[e]
            gaps[pl.ds(e, 1), :] = (
                field[pl.ds(code & 4095, 1), :] - more[pl.ds(lax.shift_right_logical(code, 12), 1), :]
            )
        return 0

    lax.fori_loop(0, trips(count[0]), step, 0)


def far_gap_kernel(count, slot, gaps, arrived, live, out, halo, taken, come):
    blocks, width, _ = arrived.shape
    groups = live.shape[0]
    first = pltpu.make_async_copy(arrived, halo.at[:blocks], come)
    first.start()
    halo[blocks] = jnp.zeros((width, LANES), jnp.float32)
    first.wait()
    flat = halo.reshape((blocks + 1) * width, LANES)

    def step(i, _):
        for u in range(4 * UNROLL):
            e = i * 4 * UNROLL + u
            taken[pl.ds(e, 1), :] = flat[pl.ds(slot[e], 1), :]
        return 0

    lax.fori_loop(0, lax.div(count[0] + 4 * UNROLL - 1, 4 * UNROLL), step, 0)
    for k in range(groups):
        at = slice(k * LANES, (k + 1) * LANES)
        gap = gaps[at, :] - taken[at, :]
        total = jnp.sum((gap * gap).T, axis=0, keepdims=True)
        alive = live[k : k + 1, :]
        out[k : k + 1, :] = jnp.where(alive > 0, total * (alive / LANES), 0.0)


def passed_round(blocks, lanes, sign):
    return [blocks[0]] + [
        lax.ppermute(blocks[s], "edg", [(i, (i + sign * s) % lanes) for i in range(lanes)]) for s in (2, 1, 3)
    ]


def summed(blocks, lanes):
    home, two, one, three = passed_round(blocks, lanes, 1)
    return (home + one) + (two + three)


def to_all(mine, lanes):
    home, two, one, three = passed_round([mine] * lanes, lanes, 1)
    return [home, one, two, three]


def across(x):
    return lax.all_to_all(x, "vtx", split_axis=0, concat_axis=0, tiled=True)


def local(sketch_cols, edge_weight, ground, src_local, dst_index, send_rows, edge_count):
    blocks = lax.axis_size("vtx")
    lanes = lax.axis_size("edg")
    rows = ground.shape[0]
    edges = edge_weight.shape[0]
    width = send_rows.shape[2]
    slots = blocks * width
    share = rows // lanes
    groups = edges // LANES
    f32, i32, bf16 = jnp.float32, jnp.int32, jnp.bfloat16
    lane = lax.axis_index("edg").astype(i32).reshape(1)
    lists = send_rows[0].reshape(-1)
    listed = lists.reshape(slots // LANES, LANES)
    padded = jnp.pad(send_rows[0], ((0, 0), (0, LANES - width)), constant_values=-1)
    live = (jnp.arange(edges, dtype=i32) < edge_count[0]).astype(f32)
    weight = edge_weight * live
    root = jnp.sqrt(edge_weight) * live
    terms = root[:, None] * sketch_cols.astype(f32)
    live_rows = live.reshape(groups, LANES)
    weight_rows = weight.reshape(groups, LANES)
    source_rows = src_local.reshape(groups, LANES)
    target_rows = dst_index.reshape(groups, LANES)

    outgoing = call(
        functools.partial(halo_side_kernel, rows, slots, width),
        [((blocks, width + 8, LANES), f32, ANY)],
        [VMEM] * 3,
        [pltpu.VMEM((edges, 2 * LANES), bf16), pltpu.VMEM((8 * width, edges), bf16)]
        + [pltpu.VMEM((blocks, width + 8, LANES), f32), pltpu.SemaphoreType.DMA],
        "halo_side",
        flops=2 * slots * edges * 2 * LANES,
    )(terms, target_rows, weight_rows)[0]
    returned = across(outgoing)
    own, own_degree = call(
        own_side_kernel,
        [((rows, LANES), f32, VMEM), ((rows // LANES, LANES), f32, VMEM)],
        [VMEM] * 4,
        [pltpu.VMEM((edges, 2 * LANES), bf16), pltpu.VMEM((256, edges), bf16)],
        "own_side",
        flops=2 * rows * edges * 2 * LANES,
    )(terms, source_rows, target_rows, weight_rows)
    sides = call(
        side_join_kernel,
        [((share + 8, LANES), f32, VMEM)] * lanes,
        [SMEM, ANY] + [VMEM] * 4,
        [pltpu.VMEM((rows, LANES), f32), pltpu.VMEM((slots, 2 * LANES), bf16), pltpu.VMEM((256, slots), bf16)]
        + [pltpu.VMEM((blocks, width + 8, LANES), f32), pltpu.SemaphoreType.DMA],
        "side_join",
        flops=2 * rows * slots * 2 * LANES,
    )(lane, returned, listed, padded, own, own_degree)
    begin, *sides = lax.optimization_barrier((edge_count, *sides))
    away = dst_index >= rows
    near_weight = jnp.where(away, 0.0, weight)
    near_order = src_local | (jnp.where(away, 0, dst_index) << 12)
    gap_order = src_local | (jnp.minimum(dst_index, rows) << 12)
    gap_slot = jnp.where(away, dst_index - rows, slots)
    far_order = jnp.where(away, src_local | ((dst_index - rows) << 12), -1)

    def far_list(start, stop, count):
        room = stop - start + LANES
        return call(
            functools.partial(far_list_kernel, start, stop),
            [((room,), i32, SMEM), ((room,), f32, SMEM), ((1,), i32, SMEM)],
            [SMEM] * 3,
            [],
            "far_list",
            moved=2**25,
        )(count, far_order, weight)

    middle = edges // 2
    list_a = far_list(0, middle, begin)
    side = summed(sides, lanes)
    side, size_a = lax.optimization_barrier((side, list_a[2]))
    later, side = lax.optimization_barrier((edge_count, side))
    list_b = far_list(middle, edges, later)
    far = (list_a[0], list_a[1], size_a, *list_b)
    right_share = side[:share]
    degree_share = side[share : share + share // LANES].reshape(share)
    ground_share = lax.dynamic_slice_in_dim(ground, lane[0] * share, share)
    diagonal = (degree_share + ground_share)[:, None]
    inverse = 1.0 / diagonal

    first, pairs = chebyshev_terms(ITERS)
    residual = right_share
    direction = first * inverse * right_share
    solution_share = direction
    for keep, push in pairs:
        field, message = call(
            field_kernel,
            [((rows, LANES), f32, VMEM), ((blocks, 2 * width, LANES), f32, ANY)],
            [SMEM] * 8 + [VMEM] * lanes,
            [pltpu.VMEM((blocks, width, LANES), f32)] * 2
            + [pltpu.SemaphoreType.DMA] * 2
            + [pltpu.VMEM((slots, LANES), f32)] * BANKS,
            "field",
        )(lane, *far, lists, *to_all(direction, lanes))
        arrived = across(message)
        near = call(
            near_kernel,
            [((rows, LANES), f32, VMEM)],
            [SMEM] * 3 + [VMEM],
            [pltpu.VMEM((rows, LANES), f32)] * BANKS,
            "near",
            moved=2**25,
        )(edge_count, near_order, near_weight, field)[0]
        two, sums, ret_both = call(
            functools.partial(first_join_kernel, 2, lanes),
            [((share, LANES), f32, VMEM), ((rows, LANES), f32, VMEM), ((slots, 2 * LANES), bf16, VMEM)],
            [SMEM] * 7 + [VMEM, VMEM, ANY],
            [pltpu.VMEM((share, slots), bf16)]
            + [pltpu.VMEM((blocks, width, LANES), f32)] * 2
            + [pltpu.SemaphoreType.DMA] * 2
            + [pltpu.VMEM((rows, LANES), f32)] * BANKS,
            "join_two",
        )(lane, *far, listed, near, arrived)
        one, three = call(
            functools.partial(join_kernel, (1, 3), lanes),
            [((share, LANES), f32, VMEM)] * 2,
            [SMEM] + [VMEM] * 3,
            [pltpu.VMEM((share, slots), bf16)],
            "join_one_three",
        )(lane, listed, sums, ret_both)
        home = call(
            functools.partial(join_kernel, (0,), lanes),
            [((share, LANES), f32, VMEM)],
            [SMEM] + [VMEM] * 3,
            [pltpu.VMEM((share, slots), bf16)],
            "join_home",
            moved=2**25,
        )(lane, listed, sums, ret_both)[0]
        flows = summed((home, one, two, three), lanes)
        residual = residual - (diagonal * direction - flows)
        direction = keep * direction + push * inverse * residual
        solution_share = solution_share + direction
    field, message = call(
        solution_kernel,
        [((rows, LANES), f32, VMEM), ((blocks, width, LANES), f32, ANY)],
        [SMEM] * 2 + [VMEM] * lanes,
        [pltpu.VMEM((blocks, width, LANES), f32), pltpu.SemaphoreType.DMA],
        "solution_rows",
    )(lane, lists, *to_all(solution_share, lanes))
    halo = across(message)
    gaps = call(
        near_gap_kernel,
        [((edges, LANES), f32, VMEM)],
        [SMEM] * 2 + [VMEM],
        [pltpu.VMEM((rows + 8, LANES), f32)],
        "near_gap",
        moved=2**25,
    )(edge_count, gap_order, field)[0]
    resistance = call(
        far_gap_kernel,
        [((groups, LANES), f32, VMEM)],
        [SMEM] * 2 + [VMEM, ANY, VMEM],
        [pltpu.VMEM((blocks + 1, width, LANES), f32), pltpu.VMEM((edges, LANES), f32), pltpu.SemaphoreType.DMA],
        "far_gap",
    )(edge_count, gap_slot, gaps, halo, live_rows)[0]
    return (field, resistance.reshape(edges))


def solution(mesh):
    in_specs = (
        P(("vtx", "edg"), None),
        P(("vtx", "edg")),
        P("vtx"),
        P(("vtx", "edg")),
        P(("vtx", "edg")),
        P(("vtx", "edg"), None, None),
        P(("vtx", "edg")),
    )
    out_specs = (P("vtx", None), P(("vtx", "edg")))
    return jax.shard_map(local, mesh=mesh, in_specs=in_specs, out_specs=out_specs, check_vma=False)
```

```python
import functools

import jax
import jax.numpy as jnp
from jax import lax
from jax.experimental import pallas as pl
from jax.experimental.pallas import tpu as pltpu
from jax.sharding import PartitionSpec as P

ITERS = 3
LANES = 128
UNROLL = 16
BANKS = 4
QUARTERS = 4
SPARE = 1536

lam_low = 0.05
lam_high = 2.0

SMEM = pl.BlockSpec(memory_space=pltpu.SMEM)
VMEM = pl.BlockSpec(memory_space=pltpu.VMEM)
HBM = pl.BlockSpec(memory_space=pltpu.HBM)
LIMIT = 24 * 2**20


def chebyshev_terms(steps):
    centre = (lam_high + lam_low) / 2.0
    half_width = (lam_high - lam_low) / 2.0
    sigma_val = centre / half_width
    rho_prev = 1.0 / sigma_val
    pairs = []
    for count_idx in range(steps - 1):
        rho_next = 1.0 / (2.0 * sigma_val - rho_prev)
        pairs.append((rho_next * rho_prev, 2.0 * rho_next / half_width))
        rho_prev = rho_next
    return (1.0 / centre, pairs)


def call(kernel, outs, ins, scratch, name, flops=0, moved=2**22):
    return pl.pallas_call(
        kernel,
        out_shape=[
            pltpu.HBM(shape, dtype) if space is HBM else jax.ShapeDtypeStruct(shape, dtype) for shape, dtype, space in outs
        ],
        in_specs=ins,
        out_specs=[space for _, _, space in outs],
        scratch_shapes=scratch,
        compiler_params=pltpu.CompilerParams(vmem_limit_bytes=LIMIT),
        cost_estimate=pl.CostEstimate(flops=flops, bytes_accessed=moved, transcendentals=0),
        name=name,
    )


def split(x):
    high = x.astype(jnp.bfloat16)
    return high, (x - high.astype(jnp.float32)).astype(jnp.bfloat16)


def put_split(ref, rows, x):
    high, low = split(x)
    ref[rows, :LANES] = high
    ref[rows, LANES:] = low


def halves(x):
    return x[:, :LANES] + x[:, LANES:]


def one_hot(row, height, base):
    place = lax.broadcasted_iota(jnp.int32, (height, row.shape[1]), 0) + base
    return jnp.where(place == row, 1.0, 0.0)


def factored(pick, groups, high_of, low_of, weight_of, height):
    total = jnp.zeros((2 * height, LANES), jnp.float32)
    for k0 in range(0, groups, pick):
        left, right = [], []
        for k in range(k0, k0 + pick):
            member = one_hot(high_of(k), height, 0) * weight_of(k)
            high, low = split(member)
            left.append(jnp.concatenate([high, low], axis=0))
            right.append(one_hot(low_of(k), LANES, 0).astype(jnp.bfloat16))
        total = total + lax.dot_general(
            jnp.concatenate(left, axis=1),
            jnp.concatenate(right, axis=1),
            (((1,), (1,)), ((), ())),
            preferred_element_type=jnp.float32,
        )
    return total[:height] + total[height:]


def halo_side_kernel(rows, slots, width, terms, target, weight, sent, both, hot, out, leave):
    groups = target.shape[0]
    tall = hot.shape[0]
    per = tall // width
    blocks = slots // width
    chunks = slots // tall

    def slot(k):
        return target[k : k + 1, :] - rows

    def block_of(k):
        return jnp.where(slot(k) < 0, -1, lax.shift_right_arithmetic(slot(k) * 1366, 16))

    def within(k):
        return slot(k) - block_of(k) * width

    deg = factored(4, groups, block_of, within, lambda k: weight[k : k + 1, :], blocks)
    for c in range(blocks):
        out[c, width : width + 8, :] = jnp.broadcast_to(deg[c : c + 1, :], (8, LANES))
    put_split(both, slice(None), terms[...])

    def part(i):
        at = pl.ds(i * per, per)
        return pltpu.make_async_copy(out.at[at], sent.at[at], leave.at[i])

    def chunk(i, _):
        base = rows + i * tall
        for k in range(groups):
            hot[:, k * LANES : (k + 1) * LANES] = one_hot(target[k : k + 1, :], tall, base).astype(jnp.bfloat16)
        got = halves(jnp.dot(hot[...], both[...], preferred_element_type=jnp.float32))
        for c in range(per):
            out[i * per + c, :width, :] = -got[c * width : (c + 1) * width]
        part(i).start()
        return 0

    lax.fori_loop(0, chunks, chunk, 0)
    for i in range(chunks):
        part(i).wait()


def own_side_kernel(terms, source, target, weight, kept, degree, both, hot, out, leave):
    groups = target.shape[0]
    rows = out.shape[0]
    put_split(both, slice(None), terms[...])
    tall = hot.shape[0]

    def part(i):
        at = pl.ds(pl.multiple_of(i * tall, tall), tall)
        return pltpu.make_async_copy(out.at[at, :], kept.at[at, :], leave.at[i])

    def chunk(i, _):
        base = i * tall
        for k in range(groups):
            plus = one_hot(source[k : k + 1, :], tall, base)
            minus = one_hot(target[k : k + 1, :], tall, base)
            hot[:, k * LANES : (k + 1) * LANES] = (plus - minus).astype(jnp.bfloat16)
        out[pl.ds(pl.multiple_of(i * tall, tall), tall), :] = halves(
            jnp.dot(hot[...], both[...], preferred_element_type=jnp.float32)
        )
        part(i).start()
        return 0

    lax.fori_loop(0, rows // tall, chunk, 0)

    def total(ref):
        return factored(
            4,
            groups,
            lambda k: lax.shift_right_logical(ref[k : k + 1, :], 7),
            lambda k: ref[k : k + 1, :] & (LANES - 1),
            lambda k: weight[k : k + 1, :],
            rows // LANES,
        )

    degree[...] = total(source) + total(target)
    for i in range(rows // tall):
        part(i).wait()


def scatter_back(ret_both, listed, hot, emit, rows):
    tall = hot.shape[0]
    groups = listed.shape[0]

    def chunk(i, _):
        base = i * tall
        for k in range(groups):
            hot[:, k * LANES : (k + 1) * LANES] = one_hot(listed[k : k + 1, :], tall, base).astype(jnp.bfloat16)
        emit(i, halves(jnp.dot(hot[...], ret_both[...], preferred_element_type=jnp.float32)))
        return 0

    lax.fori_loop(0, rows // tall, chunk, 0)


def side_join_kernel(lane, returned, listed, padded, own, own_degree, *refs):
    lanes = 4
    outs, (acc, ret_both, hot, landed, arrival, arrival_own) = refs[:lanes], refs[lanes:]
    come = pltpu.make_async_copy(returned, landed, arrival)
    come.start()
    mine = pltpu.make_async_copy(own, acc, arrival_own)
    mine.start()
    blocks = returned.shape[0]
    rows = own.shape[0]
    width = listed.shape[0] * LANES // blocks
    share = rows // lanes
    come.wait()
    for c in range(blocks):
        put_split(ret_both, slice(c * width, (c + 1) * width), landed[c, :width, :])

    def emit(i, got):
        at = pl.ds(pl.multiple_of(i * hot.shape[0], hot.shape[0]), hot.shape[0])
        acc[at, :] = acc[at, :] + got

    mine.wait()
    scatter_back(ret_both, listed, hot, emit, rows)
    deg = own_degree[...] + factored(
        4,
        blocks,
        lambda k: lax.shift_right_arithmetic(padded[k : k + 1, :], 7),
        lambda k: padded[k : k + 1, :] & (LANES - 1),
        lambda k: landed[k, width : width + 1, :],
        rows // LANES,
    )
    deg_rows = share // LANES
    for s in range(lanes):
        q = lax.rem(lane[0] + s, lanes)
        outs[s][:share, :] = acc[pl.ds(pl.multiple_of(q * share, share), share), :]
        row = jnp.zeros((8, LANES), jnp.float32)
        place = lax.broadcasted_iota(jnp.int32, (8, LANES), 0)
        for p in range(lanes):
            for d in range(deg_rows):
                one = jnp.broadcast_to(deg[p * deg_rows + d : p * deg_rows + d + 1, :], (8, LANES))
                row = jnp.where((place == d) & (q == p), one, row)
        outs[s][share : share + 8, :] = row


def far_list_kernel(first, room, count, lane, order, code, sizes):
    quarter = order.shape[0] // QUARTERS
    across = lax.rem(lane[0] + 2, 4)
    for c in range(2):
        begin = (first + c) * quarter
        zero = 2 * c * room

        def step(i, at):
            e = begin + i * 8
            given = [order[e + u] for u in range(8)]
            early, late = at
            for u in range(8):
                far = jnp.where(lax.shift_right_arithmetic(given[u], 21) == -1, 0, 1)
                after = (lax.shift_right_logical(given[u], 19) & 3) == across
                code[jnp.where(after, late, early)] = given[u]
                early = early + jnp.where(after, 0, far)
                late = late + jnp.where(after, far, 0)
            return early, late

        live = jnp.clip(count[0] - begin, 0, quarter)
        early, late = lax.fori_loop(0, lax.div(live + 7, 8), step, (zero, zero + room))
        nothing = jnp.int32(SPARE - 2048) << 21
        for u in range(UNROLL):
            code[early + u] = nothing
            code[late + u] = nothing
        sizes[2 * c] = early - zero
        sizes[2 * c + 1] = late - zero - room


def trips(n):
    return lax.div(n + UNROLL - 1, UNROLL)


def clear(banks):
    for a in banks:
        a[...] = jnp.zeros_like(a)


def far_rows(kind, lists, mass, take, give, banks):
    quarter = mass.shape[0] // QUARTERS
    many = len(banks)
    for h, (code, sizes) in enumerate(lists):
        room = code.shape[0] // 4
        for c in range(2):
            start = (2 * c + kind) * room
            base = (2 * h + c) * quarter

            def step(i, _):
                for u in range(0, UNROLL, many):
                    at = start + i * UNROLL + u
                    given = [code[at + k] for k in range(many)]
                    rows = [take(given[k]) * mass[base + (given[k] & 1023)] for k in range(many)]
                    to = [pl.ds(give(given[k]), 1) for k in range(many)]
                    new = [banks[k][to[k], :] + rows[k] for k in range(many)]
                    for k in range(many):
                        banks[k][to[k], :] = new[k]
                return 0

            lax.fori_loop(0, trips(sizes[2 * c + kind]), step, 0)


def far_source(given):
    return lax.shift_right_logical(given, 10) & 2047


def far_slot(given):
    return lax.shift_right_logical(given, 21)


def source_of(given):
    return given & 4095


def target_of(given):
    return lax.shift_right_logical(given, 12)


def place(lane, lanes, shift, share, field):
    q = lax.rem(lane[0] - shift + lanes, lanes)
    rows = share.shape[0]
    field[pl.ds(pl.multiple_of(q * rows, rows), rows), :] = share[...]


def assemble(lane, lanes, shares, field):
    for s in range(lanes):
        place(lane, lanes, s, shares[s], field)


def pack(lists, field, out, width):
    def step(c, _):
        for r in range(width):
            out[c, pl.ds(r, 1), :] = field[pl.ds(lists[c * width + r], 1), :]
        return 0

    lax.fori_loop(0, out.shape[0], step, 0)


def early_field_kernel(lanes, lane, code_a, sizes_a, code_b, sizes_b, mass, home, one, three, out, field, *banks):
    for s, share in ((0, home), (1, one), (3, three)):
        place(lane, lanes, s, share, field)
    clear(banks)
    far_rows(
        0,
        ((code_a, sizes_a), (code_b, sizes_b)),
        mass,
        lambda given: field[pl.ds(far_source(given), 1), :],
        far_slot,
        banks,
    )
    total = banks[0][...]
    for a in banks[1:]:
        total = total + a[...]
    out[...] = total


def field_kernel(lanes, lane, code_a, sizes_a, code_b, sizes_b, mass, lists, part, *refs):
    shares, (kept, sent), refs = refs[:lanes], refs[lanes : lanes + 2], refs[lanes + 2 :]
    field, out, sums, leave_field, leave, leave_sums = refs[:6]
    banks = refs[6:]
    blocks, width, _ = out.shape
    assemble(lane, lanes, shares, field)
    keep = pltpu.make_async_copy(field, kept, leave_field)
    keep.start()
    banks[0][...] = part[...]
    clear(banks[1:])
    far_rows(
        1,
        ((code_a, sizes_a), (code_b, sizes_b)),
        mass,
        lambda given: field[pl.ds(far_source(given), 1), :],
        far_slot,
        banks,
    )
    for c in range(blocks):
        at = slice(c * width, (c + 1) * width)
        total = banks[0][at, :]
        for a in banks[1:]:
            total = total + a[at, :]
        sums[c] = total
    more = pltpu.make_async_copy(sums, sent.at[:, width:, :], leave_sums)
    more.start()
    pack(lists, field, out, width)
    go = pltpu.make_async_copy(out, sent.at[:, :width, :], leave)
    go.start()
    keep.wait()
    more.wait()
    go.wait()


def near_kernel(count, order, heavy, kept, out, field, come, *banks):
    bring = pltpu.make_async_copy(kept, field, come)
    bring.start()
    clear(banks)
    bring.wait()

    def step(i, _):
        for u in range(0, UNROLL, BANKS):
            at = i * UNROLL + u
            code = [order[at + k] for k in range(BANKS)]
            mass = [heavy[at + k] for k in range(BANKS)]
            one = [pl.ds(source_of(code[k]), 1) for k in range(BANKS)]
            two = [pl.ds(target_of(code[k]), 1) for k in range(BANKS)]
            from_one = [field[one[k], :] * mass[k] for k in range(BANKS)]
            from_two = [field[two[k], :] * mass[k] for k in range(BANKS)]
            new = [banks[k][one[k], :] + from_two[k] for k in range(BANKS)]
            for k in range(BANKS):
                banks[k][one[k], :] = new[k]
            new = [banks[k][two[k], :] + from_one[k] for k in range(BANKS)]
            for k in range(BANKS):
                banks[k][two[k], :] = new[k]
        return 0

    lax.fori_loop(0, trips(count[0]), step, 0)
    total = banks[0][...]
    for a in banks[1:]:
        total = total + a[...]
    out[...] = total


def listed_rows(q, share, listed, ret_both, hot):
    for k in range(listed.shape[0]):
        hot[:, k * LANES : (k + 1) * LANES] = one_hot(listed[k : k + 1, :], share, q * share).astype(jnp.bfloat16)
    return halves(jnp.dot(hot[...], ret_both[...], preferred_element_type=jnp.float32))


def late_join_kernel(lanes, lane, code_a, sizes_a, code_b, sizes_b, mass, listed, near, arrived, *refs):
    out, halo, ret_both, hot, ret, come_halo, come_ret = refs[:7]
    banks = refs[7:]
    blocks, width, _ = ret.shape
    share = out.shape[0]
    first = pltpu.make_async_copy(arrived.at[:, :width, :], halo.at[:blocks], come_halo)
    second = pltpu.make_async_copy(arrived.at[:, width:, :], ret, come_ret)
    first.start()
    second.start()
    halo[blocks] = jnp.zeros((width, LANES), jnp.float32)
    clear(banks)
    q = lax.rem(lane[0] + 2, lanes)
    first.wait()
    flat = halo.reshape((blocks + 1) * width, LANES)
    far_rows(
        1,
        ((code_a, sizes_a), (code_b, sizes_b)),
        mass,
        lambda given: flat[pl.ds(far_slot(given), 1), :],
        lambda given: far_source(given) & (share - 1),
        banks,
    )
    second.wait()
    for c in range(blocks):
        put_split(ret_both, slice(c * width, (c + 1) * width), ret[c])
    total = near[pl.ds(pl.multiple_of(q * share, share), share), :]
    for a in banks:
        total = total + a[...]
    out[...] = total + listed_rows(q, share, listed, ret_both, hot)


def join_kernel(lanes, lane, code_a, sizes_a, code_b, sizes_b, mass, listed, near, halo, ret_both, *refs):
    outs, hot, banks = refs[:3], refs[3], refs[4:]
    share = outs[0].shape[0]
    clear(banks)
    flat = halo.reshape(halo.shape[0] * halo.shape[1], LANES)
    far_rows(
        0,
        ((code_a, sizes_a), (code_b, sizes_b)),
        mass,
        lambda given: flat[pl.ds(far_slot(given), 1), :],
        far_source,
        banks,
    )
    for s, out in zip((1, 3, 0), outs):
        q = lax.rem(lane[0] + s, lanes)
        at = pl.ds(pl.multiple_of(q * share, share), share)
        total = near[at, :]
        for a in banks:
            total = total + a[at, :]
        out[...] = total + listed_rows(q, share, listed, ret_both, hot)


def solution_kernel(lane, lists, *refs):
    lanes = 4
    shares, (field, sent, out, leave) = refs[:lanes], refs[lanes:]
    assemble(lane, lanes, shares, field)
    pack(lists, field, out, out.shape[1])
    go = pltpu.make_async_copy(out, sent, leave)
    go.start()
    go.wait()


def near_gap_kernel(count, order, field, gaps, more):
    rows = field.shape[0]
    more[:rows, :] = field[...]
    more[rows:, :] = jnp.zeros((more.shape[0] - rows, LANES), jnp.float32)

    def step(i, _):
        for u in range(UNROLL):
            e = i * UNROLL + u
            code = order[e]
            gaps[pl.ds(e, 1), :] = (
                field[pl.ds(code & 4095, 1), :] - more[pl.ds(lax.shift_right_logical(code, 12), 1), :]
            )
        return 0

    lax.fori_loop(0, trips(count[0]), step, 0)


def far_gap_kernel(count, slot, gaps, arrived, live, out, halo, taken, come):
    blocks, width, _ = arrived.shape
    groups = live.shape[0]
    first = pltpu.make_async_copy(arrived, halo.at[:blocks], come)
    first.start()
    halo[blocks] = jnp.zeros((width, LANES), jnp.float32)
    first.wait()
    flat = halo.reshape((blocks + 1) * width, LANES)

    def step(i, _):
        for u in range(4 * UNROLL):
            e = i * 4 * UNROLL + u
            taken[pl.ds(e, 1), :] = flat[pl.ds(slot[e], 1), :]
        return 0

    lax.fori_loop(0, lax.div(count[0] + 4 * UNROLL - 1, 4 * UNROLL), step, 0)
    for k in range(groups):
        at = slice(k * LANES, (k + 1) * LANES)
        gap = gaps[at, :] - taken[at, :]
        total = jnp.sum((gap * gap).T, axis=0, keepdims=True)
        alive = live[k : k + 1, :]
        out[k : k + 1, :] = jnp.where(alive > 0, total * (alive / LANES), 0.0)


def moved_by(x, shift, lanes):
    return lax.ppermute(x, "edg", [(i, (i + shift) % lanes) for i in range(lanes)])


def passed_round(blocks, lanes):
    return [blocks[0]] + [moved_by(blocks[s], s, lanes) for s in (2, 1, 3)]


def summed(blocks, lanes):
    home, two, one, three = passed_round(blocks, lanes)
    return (home + one) + (two + three)


def to_all(mine, lanes):
    home, two, one, three = passed_round([mine] * lanes, lanes)
    return [home, one, two, three]


def across(x):
    return lax.all_to_all(x, "vtx", split_axis=0, concat_axis=0, tiled=True)


def local(sketch_cols, edge_weight, ground, src_local, dst_index, send_rows, edge_count):
    blocks = lax.axis_size("vtx")
    lanes = lax.axis_size("edg")
    rows = ground.shape[0]
    edges = edge_weight.shape[0]
    width = send_rows.shape[2]
    slots = blocks * width
    share = rows // lanes
    groups = edges // LANES
    f32, i32, bf16 = jnp.float32, jnp.int32, jnp.bfloat16
    lane = lax.axis_index("edg").astype(i32).reshape(1)
    lists = send_rows[0].reshape(-1)
    listed = lists.reshape(slots // LANES, LANES)
    padded = jnp.pad(send_rows[0], ((0, 0), (0, LANES - width)), constant_values=-1)
    live = (jnp.arange(edges, dtype=i32) < edge_count[0]).astype(f32)
    weight = edge_weight * live
    root = jnp.sqrt(edge_weight) * live
    terms = root[:, None] * sketch_cols.astype(f32)
    live_rows = live.reshape(groups, LANES)
    weight_rows = weight.reshape(groups, LANES)
    source_rows = src_local.reshape(groups, LANES)
    target_rows = dst_index.reshape(groups, LANES)

    outgoing = call(
        functools.partial(halo_side_kernel, rows, slots, width),
        [((blocks, width + 8, LANES), f32, HBM)],
        [VMEM] * 3,
        [pltpu.VMEM((edges, 2 * LANES), bf16), pltpu.VMEM((8 * width, edges), bf16)]
        + [pltpu.VMEM((blocks, width + 8, LANES), f32), pltpu.SemaphoreType.DMA((slots // (8 * width),))],
        "halo_side",
        flops=2 * slots * edges * 2 * LANES,
    )(terms, target_rows, weight_rows)[0]
    returned = across(outgoing)
    own, own_degree = call(
        own_side_kernel,
        [((rows, LANES), f32, HBM), ((rows // LANES, LANES), f32, VMEM)],
        [VMEM] * 4,
        [pltpu.VMEM((edges, 2 * LANES), bf16), pltpu.VMEM((256, edges), bf16)]
        + [pltpu.VMEM((rows, LANES), f32), pltpu.SemaphoreType.DMA((rows // 256,))],
        "own_side",
        flops=2 * rows * edges * 2 * LANES,
    )(terms, source_rows, target_rows, weight_rows)
    sides = call(
        side_join_kernel,
        [((share + 8, LANES), f32, VMEM)] * lanes,
        [SMEM, HBM, VMEM, VMEM, HBM, VMEM],
        [pltpu.VMEM((rows, LANES), f32), pltpu.VMEM((slots, 2 * LANES), bf16), pltpu.VMEM((256, slots), bf16)]
        + [pltpu.VMEM((blocks, width + 8, LANES), f32)]
        + [pltpu.SemaphoreType.DMA] * 2,
        "side_join",
        flops=2 * rows * slots * 2 * LANES,
    )(lane, returned, listed, padded, own, own_degree)
    begin, *sides = lax.optimization_barrier((edge_count, *sides))
    away = dst_index >= rows
    near_weight = jnp.where(away, 0.0, weight)
    near_order = src_local | (jnp.where(away, 0, dst_index) << 12)
    gap_order = src_local | (jnp.minimum(dst_index, rows) << 12)
    gap_slot = jnp.where(away, dst_index - rows, slots)
    quarter = edges // QUARTERS
    number = jnp.arange(edges, dtype=i32) & (quarter - 1)
    far_order = (jnp.where(away, dst_index - rows, 2047) << 21) | (src_local << 10) | number

    def far_list(first, count):
        room = quarter + LANES // 4
        return call(
            functools.partial(far_list_kernel, first, room),
            [((4 * room,), i32, SMEM), ((4,), i32, SMEM)],
            [SMEM] * 3,
            [],
            "far_list",
            moved=2**25,
        )(count, lane, far_order)

    code_a, sizes_a = far_list(0, begin)
    side = summed(sides, lanes)
    side, sizes_a = lax.optimization_barrier((side, sizes_a))
    later, side = lax.optimization_barrier((edge_count, side))
    code_b, sizes_b = far_list(2, later)
    far = (code_a, sizes_a, code_b, sizes_b, weight)
    right_share = side[:share]
    degree_share = side[share : share + share // LANES].reshape(share)
    ground_share = lax.dynamic_slice_in_dim(ground, lane[0] * share, share)
    diagonal = (degree_share + ground_share)[:, None]
    inverse = 1.0 / diagonal

    first, pairs = chebyshev_terms(ITERS)
    residual = right_share
    direction = first * inverse * right_share
    solution_share = direction
    for keep, push in pairs:
        shares = to_all(direction, lanes)
        early = call(
            functools.partial(early_field_kernel, lanes),
            [((slots + 8, LANES), f32, VMEM)],
            [SMEM] * 6 + [VMEM] * 3,
            [pltpu.VMEM((rows, LANES), f32)] + [pltpu.VMEM((slots + 8, LANES), f32)] * BANKS,
            "early_field",
            moved=2**25,
        )(lane, *far, shares[0], shares[1], shares[3])[0]
        field, message = call(
            functools.partial(field_kernel, lanes),
            [((rows, LANES), f32, HBM), ((blocks, 2 * width, LANES), f32, HBM)],
            [SMEM] * 7 + [VMEM] * (1 + lanes),
            [pltpu.VMEM((rows, LANES), f32)]
            + [pltpu.VMEM((blocks, width, LANES), f32)] * 2
            + [pltpu.SemaphoreType.DMA] * 3
            + [pltpu.VMEM((slots + 8, LANES), f32)] * 2,
            "field",
        )(lane, *far, lists, early, *shares)
        arrived = across(message)
        near = call(
            near_kernel,
            [((rows, LANES), f32, VMEM)],
            [SMEM] * 3 + [HBM],
            [pltpu.VMEM((rows, LANES), f32), pltpu.SemaphoreType.DMA] + [pltpu.VMEM((rows, LANES), f32)] * BANKS,
            "near",
            moved=2**25,
        )(edge_count, near_order, near_weight, field)[0]
        two, halo, ret_both = call(
            functools.partial(late_join_kernel, lanes),
            [((share, LANES), f32, VMEM), ((blocks + 1, width, LANES), f32, VMEM), ((slots, 2 * LANES), bf16, VMEM)],
            [SMEM] * 6 + [VMEM, VMEM, HBM],
            [pltpu.VMEM((share, slots), bf16), pltpu.VMEM((blocks, width, LANES), f32)]
            + [pltpu.SemaphoreType.DMA] * 2
            + [pltpu.VMEM((share, LANES), f32)] * BANKS,
            "late_join",
        )(lane, *far, listed, near, arrived)
        one, three, home = call(
            functools.partial(join_kernel, lanes),
            [((share, LANES), f32, VMEM)] * 3,
            [SMEM] * 6 + [VMEM] * 4,
            [pltpu.VMEM((share, slots), bf16)] + [pltpu.VMEM((rows, LANES), f32)] * BANKS,
            "join",
            moved=2**25,
        )(lane, *far, listed, near, halo, ret_both)
        two = moved_by(two, 2, lanes)
        two, one, three = lax.optimization_barrier((two, one, three))
        flows = (home + two) + (moved_by(one, 1, lanes) + moved_by(three, 3, lanes))
        residual = residual - (diagonal * direction - flows)
        direction = keep * direction + push * inverse * residual
        solution_share = solution_share + direction
    field, message = call(
        solution_kernel,
        [((rows, LANES), f32, VMEM), ((blocks, width, LANES), f32, HBM)],
        [SMEM] * 2 + [VMEM] * lanes,
        [pltpu.VMEM((blocks, width, LANES), f32), pltpu.SemaphoreType.DMA],
        "solution_rows",
    )(lane, lists, *to_all(solution_share, lanes))
    halo = across(message)
    gaps = call(
        near_gap_kernel,
        [((edges, LANES), f32, VMEM)],
        [SMEM] * 2 + [VMEM],
        [pltpu.VMEM((rows + 8, LANES), f32)],
        "near_gap",
        moved=2**25,
    )(edge_count, gap_order, field)[0]
    resistance = call(
        far_gap_kernel,
        [((groups, LANES), f32, VMEM)],
        [SMEM] * 2 + [VMEM, HBM, VMEM],
        [pltpu.VMEM((blocks + 1, width, LANES), f32), pltpu.VMEM((edges, LANES), f32), pltpu.SemaphoreType.DMA],
        "far_gap",
    )(edge_count, gap_slot, gaps, halo, live_rows)[0]
    return (field, resistance.reshape(edges))


def solution(mesh):
    in_specs = (
        P(("vtx", "edg"), None),
        P(("vtx", "edg")),
        P("vtx"),
        P(("vtx", "edg")),
        P(("vtx", "edg")),
        P(("vtx", "edg"), None, None),
        P(("vtx", "edg")),
    )
    out_specs = (P("vtx", None), P(("vtx", "edg")))
    return jax.shard_map(local, mesh=mesh, in_specs=in_specs, out_specs=out_specs, check_vma=False)
```

```python
import functools

import jax
import jax.numpy as jnp
from jax import lax
from jax.experimental import pallas as pl
from jax.experimental.pallas import tpu as pltpu
from jax.sharding import PartitionSpec as P

ITERS = 3
LANES = 128
UNROLL = 16
BANKS = 4
QUARTERS = 4
SPARE = 1536

lam_low = 0.05
lam_high = 2.0

SMEM = pl.BlockSpec(memory_space=pltpu.SMEM)
VMEM = pl.BlockSpec(memory_space=pltpu.VMEM)
HBM = pl.BlockSpec(memory_space=pltpu.HBM)
LIMIT = 24 * 2**20


def chebyshev_terms(steps):
    centre = (lam_high + lam_low) / 2.0
    half_width = (lam_high - lam_low) / 2.0
    sigma_val = centre / half_width
    rho_prev = 1.0 / sigma_val
    pairs = []
    for count_idx in range(steps - 1):
        rho_next = 1.0 / (2.0 * sigma_val - rho_prev)
        pairs.append((rho_next * rho_prev, 2.0 * rho_next / half_width))
        rho_prev = rho_next
    return (1.0 / centre, pairs)


def call(kernel, outs, ins, scratch, name, flops=0, moved=2**22):
    return pl.pallas_call(
        kernel,
        out_shape=[
            pltpu.HBM(shape, dtype) if space is HBM else jax.ShapeDtypeStruct(shape, dtype) for shape, dtype, space in outs
        ],
        in_specs=ins,
        out_specs=[space for _, _, space in outs],
        scratch_shapes=scratch,
        compiler_params=pltpu.CompilerParams(vmem_limit_bytes=LIMIT),
        cost_estimate=pl.CostEstimate(flops=flops, bytes_accessed=moved, transcendentals=0),
        name=name,
    )


def split(x):
    high = x.astype(jnp.bfloat16)
    return high, (x - high.astype(jnp.float32)).astype(jnp.bfloat16)


def put_split(ref, rows, x):
    high, low = split(x)
    ref[rows, :LANES] = high
    ref[rows, LANES:] = low


def halves(x):
    return x[:, :LANES] + x[:, LANES:]


def one_hot(row, height, base):
    place = lax.broadcasted_iota(jnp.int32, (height, row.shape[1]), 0) + base
    return jnp.where(place == row, 1.0, 0.0)


def factored(pick, groups, high_of, low_of, weight_of, height):
    total = jnp.zeros((2 * height, LANES), jnp.float32)
    for k0 in range(0, groups, pick):
        left, right = [], []
        for k in range(k0, k0 + pick):
            member = one_hot(high_of(k), height, 0) * weight_of(k)
            high, low = split(member)
            left.append(jnp.concatenate([high, low], axis=0))
            right.append(one_hot(low_of(k), LANES, 0).astype(jnp.bfloat16))
        total = total + lax.dot_general(
            jnp.concatenate(left, axis=1),
            jnp.concatenate(right, axis=1),
            (((1,), (1,)), ((), ())),
            preferred_element_type=jnp.float32,
        )
    return total[:height] + total[height:]


def halo_side_kernel(rows, slots, width, terms, target, weight, sent, both, hot, out, leave):
    groups = target.shape[0]
    tall = hot.shape[0]
    per = tall // width
    blocks = slots // width
    chunks = slots // tall

    def slot(k):
        return target[k : k + 1, :] - rows

    def block_of(k):
        return jnp.where(slot(k) < 0, -1, lax.shift_right_arithmetic(slot(k) * 1366, 16))

    def within(k):
        return slot(k) - block_of(k) * width

    deg = factored(4, groups, block_of, within, lambda k: weight[k : k + 1, :], blocks)
    for c in range(blocks):
        out[c, width : width + 8, :] = jnp.broadcast_to(deg[c : c + 1, :], (8, LANES))
    put_split(both, slice(None), terms[...])

    def part(i):
        at = pl.ds(i * per, per)
        return pltpu.make_async_copy(out.at[at], sent.at[at], leave.at[i])

    def chunk(i, _):
        base = rows + i * tall
        for k in range(groups):
            hot[:, k * LANES : (k + 1) * LANES] = one_hot(target[k : k + 1, :], tall, base).astype(jnp.bfloat16)
        got = halves(jnp.dot(hot[...], both[...], preferred_element_type=jnp.float32))
        for c in range(per):
            out[i * per + c, :width, :] = -got[c * width : (c + 1) * width]
        part(i).start()
        return 0

    lax.fori_loop(0, chunks, chunk, 0)
    for i in range(chunks):
        part(i).wait()


def own_side_kernel(terms, source, target, weight, kept, degree, both, hot, out, leave):
    groups = target.shape[0]
    rows = out.shape[0]
    put_split(both, slice(None), terms[...])
    tall = hot.shape[0]

    def part(i):
        at = pl.ds(pl.multiple_of(i * tall, tall), tall)
        return pltpu.make_async_copy(out.at[at, :], kept.at[at, :], leave.at[i])

    def chunk(i, _):
        base = i * tall
        for k in range(groups):
            plus = one_hot(source[k : k + 1, :], tall, base)
            minus = one_hot(target[k : k + 1, :], tall, base)
            hot[:, k * LANES : (k + 1) * LANES] = (plus - minus).astype(jnp.bfloat16)
        out[pl.ds(pl.multiple_of(i * tall, tall), tall), :] = halves(
            jnp.dot(hot[...], both[...], preferred_element_type=jnp.float32)
        )
        part(i).start()
        return 0

    lax.fori_loop(0, rows // tall, chunk, 0)

    def total(ref):
        return factored(
            4,
            groups,
            lambda k: lax.shift_right_logical(ref[k : k + 1, :], 7),
            lambda k: ref[k : k + 1, :] & (LANES - 1),
            lambda k: weight[k : k + 1, :],
            rows // LANES,
        )

    degree[...] = total(source) + total(target)
    for i in range(rows // tall):
        part(i).wait()


def scatter_back(ret_both, listed, hot, emit, rows):
    tall = hot.shape[0]
    groups = listed.shape[0]

    def chunk(i, _):
        base = i * tall
        for k in range(groups):
            hot[:, k * LANES : (k + 1) * LANES] = one_hot(listed[k : k + 1, :], tall, base).astype(jnp.bfloat16)
        emit(i, halves(jnp.dot(hot[...], ret_both[...], preferred_element_type=jnp.float32)))
        return 0

    lax.fori_loop(0, rows // tall, chunk, 0)


def side_join_kernel(lane, returned, listed, padded, own, own_degree, *refs):
    lanes = 4
    outs, (acc, ret_both, hot, landed, arrival, arrival_own) = refs[:lanes], refs[lanes:]
    come = pltpu.make_async_copy(returned, landed, arrival)
    come.start()
    mine = pltpu.make_async_copy(own, acc, arrival_own)
    mine.start()
    blocks = returned.shape[0]
    rows = own.shape[0]
    width = listed.shape[0] * LANES // blocks
    share = rows // lanes
    come.wait()
    for c in range(blocks):
        put_split(ret_both, slice(c * width, (c + 1) * width), landed[c, :width, :])

    def emit(i, got):
        at = pl.ds(pl.multiple_of(i * hot.shape[0], hot.shape[0]), hot.shape[0])
        acc[at, :] = acc[at, :] + got

    mine.wait()
    scatter_back(ret_both, listed, hot, emit, rows)
    deg = own_degree[...] + factored(
        4,
        blocks,
        lambda k: lax.shift_right_arithmetic(padded[k : k + 1, :], 7),
        lambda k: padded[k : k + 1, :] & (LANES - 1),
        lambda k: landed[k, width : width + 1, :],
        rows // LANES,
    )
    deg_rows = share // LANES
    for s in range(lanes):
        q = lax.rem(lane[0] + s, lanes)
        outs[s][:share, :] = acc[pl.ds(pl.multiple_of(q * share, share), share), :]
        row = jnp.zeros((8, LANES), jnp.float32)
        place = lax.broadcasted_iota(jnp.int32, (8, LANES), 0)
        for p in range(lanes):
            for d in range(deg_rows):
                one = jnp.broadcast_to(deg[p * deg_rows + d : p * deg_rows + d + 1, :], (8, LANES))
                row = jnp.where((place == d) & (q == p), one, row)
        outs[s][share : share + 8, :] = row


def edge_code_kernel(
    rows, slots, room, count, lane, source, target, weight, far_code, spot, totals, mass, near_code, near_mass, gap_code, gap_slot
):
    groups = source.shape[0]
    per = groups // QUARTERS
    s, t = source[...], target[...]
    row = lax.broadcasted_iota(jnp.int32, s.shape, 0)
    number = row * LANES + lax.broadcasted_iota(jnp.int32, s.shape, 1)
    live = number < count[0]
    away = t >= rows
    load = jnp.where(live, weight[...], 0.0)
    mass[...] = load
    near_mass[...] = jnp.where(away, 0.0, load)
    near_code[...] = s | (jnp.where(away, 0, t) << 12)
    gap_code[...] = s | (jnp.minimum(t, rows) << 12)
    gap_slot[...] = jnp.where(away, t - rows, slots)
    far_code[...] = (jnp.where(away, t - rows, 0) << 21) | (s << 10) | (number & (per * LANES - 1))
    left = lax.broadcasted_iota(jnp.int32, (LANES, LANES), 0)
    right = lax.broadcasted_iota(jnp.int32, (LANES, LANES), 1)
    before = jnp.where(left < right, 1.0, 0.0).astype(jnp.bfloat16)
    ones = jnp.ones((LANES, LANES), jnp.bfloat16)
    down = lax.broadcasted_iota(jnp.int32, (groups, groups), 0)
    over = lax.broadcasted_iota(jnp.int32, (groups, groups), 1)
    same = lax.shift_right_logical(down, 3) == lax.shift_right_logical(over, 3)
    above = jnp.where(same & (over < down), 1.0, 0.0).astype(jnp.bfloat16)
    late = lax.shift_right_logical(s, 9) == lax.rem(lane[0] + 2, 4)
    region = (lax.shift_right_logical(row, 3) & 1) * 2 * room
    where = jnp.zeros_like(row) + 4 * room
    for kind in range(2):
        counted = away & live & (late if kind else ~late)
        flags = jnp.where(counted, 1.0, 0.0).astype(jnp.bfloat16)
        within = jnp.dot(flags, before, preferred_element_type=jnp.float32)
        total = jnp.dot(flags, ones, preferred_element_type=jnp.float32)
        base = jnp.dot(above, total.astype(jnp.bfloat16), preferred_element_type=jnp.float32)
        where = jnp.where(counted, region + kind * room + (within + base).astype(jnp.int32), where)
        through = (base + total).astype(jnp.int32)
        for c in range(QUARTERS):
            totals[kind * QUARTERS + c : kind * QUARTERS + c + 1, :] = through[(c + 1) * per - 1 : (c + 1) * per, :]
    spot[...] = where


def far_list_kernel(first, room, count, order, spot, totals, code):
    half = order.shape[0] // 2
    begin = first * order.shape[0] // QUARTERS

    def step(i, _):
        e = begin + i * 8
        given = [order[e + u] for u in range(8)]
        to = [spot[e + u] for u in range(8)]
        for u in range(8):
            code[to[u]] = given[u]
        return 0

    live = jnp.clip(count[0] - begin, 0, half)
    lax.fori_loop(0, lax.div(live + 7, 8), step, 0)
    nothing = jnp.int32(SPARE - 2048) << 21
    for c in range(2):
        for kind in range(2):
            end = (2 * c + kind) * room + totals[kind * QUARTERS + first + c, 0]
            for u in range(UNROLL):
                code[end + u] = nothing


def trips(n):
    return lax.div(n + UNROLL - 1, UNROLL)


def clear(banks):
    for a in banks:
        a[...] = jnp.zeros_like(a)


def far_rows(kind, lists, totals, mass, take, give, banks):
    quarter = mass.shape[0] // QUARTERS
    many = len(banks)
    for h, code in enumerate(lists):
        room = (code.shape[0] - LANES) // 4
        for c in range(2):
            start = (2 * c + kind) * room
            base = (2 * h + c) * quarter

            def step(i, _):
                for u in range(0, UNROLL, many):
                    at = start + i * UNROLL + u
                    given = [code[at + k] for k in range(many)]
                    rows = [take(given[k]) * mass[base + (given[k] & 1023)] for k in range(many)]
                    to = [pl.ds(give(given[k]), 1) for k in range(many)]
                    new = [banks[k][to[k], :] + rows[k] for k in range(many)]
                    for k in range(many):
                        banks[k][to[k], :] = new[k]
                return 0

            lax.fori_loop(0, trips(totals[kind * QUARTERS + 2 * h + c, 0]), step, 0)


def far_source(given):
    return lax.shift_right_logical(given, 10) & 2047


def far_slot(given):
    return lax.shift_right_logical(given, 21)


def source_of(given):
    return given & 4095


def target_of(given):
    return lax.shift_right_logical(given, 12)


def place(lane, lanes, shift, share, field):
    q = lax.rem(lane[0] - shift + lanes, lanes)
    rows = share.shape[0]
    field[pl.ds(pl.multiple_of(q * rows, rows), rows), :] = share[...]


def assemble(lane, lanes, shares, field):
    for s in range(lanes):
        place(lane, lanes, s, shares[s], field)


def pack(lists, field, out, width):
    def step(c, _):
        for r in range(width):
            out[c, pl.ds(r, 1), :] = field[pl.ds(lists[c * width + r], 1), :]
        return 0

    lax.fori_loop(0, out.shape[0], step, 0)


def field_kernel(lanes, lane, code_a, code_b, totals, mass, lists, *refs):
    shares, (kept, sent), refs = refs[:lanes], refs[lanes : lanes + 2], refs[lanes + 2 :]
    field, out, sums, leave_field, leave, leave_sums = refs[:6]
    banks = refs[6:]
    blocks, width, _ = out.shape
    assemble(lane, lanes, shares, field)
    keep = pltpu.make_async_copy(field, kept, leave_field)
    keep.start()
    clear(banks)
    for kind in range(2):
        far_rows(
            kind,
            (code_a, code_b),
            totals,
            mass,
            lambda given: field[pl.ds(far_source(given), 1), :],
            far_slot,
            banks,
        )
    for c in range(blocks):
        at = slice(c * width, (c + 1) * width)
        total = banks[0][at, :]
        for a in banks[1:]:
            total = total + a[at, :]
        sums[c] = total
    more = pltpu.make_async_copy(sums, sent.at[:, width:, :], leave_sums)
    more.start()
    pack(lists, field, out, width)
    go = pltpu.make_async_copy(out, sent.at[:, :width, :], leave)
    go.start()
    keep.wait()
    more.wait()
    go.wait()


def near_kernel(count, order, heavy, kept, out, field, come, *banks):
    bring = pltpu.make_async_copy(kept, field, come)
    bring.start()
    clear(banks)
    bring.wait()

    def step(i, _):
        for u in range(0, UNROLL, BANKS):
            at = i * UNROLL + u
            code = [order[at + k] for k in range(BANKS)]
            mass = [heavy[at + k] for k in range(BANKS)]
            one = [pl.ds(source_of(code[k]), 1) for k in range(BANKS)]
            two = [pl.ds(target_of(code[k]), 1) for k in range(BANKS)]
            from_one = [field[one[k], :] * mass[k] for k in range(BANKS)]
            from_two = [field[two[k], :] * mass[k] for k in range(BANKS)]
            new = [banks[k][one[k], :] + from_two[k] for k in range(BANKS)]
            for k in range(BANKS):
                banks[k][one[k], :] = new[k]
            new = [banks[k][two[k], :] + from_one[k] for k in range(BANKS)]
            for k in range(BANKS):
                banks[k][two[k], :] = new[k]
        return 0

    lax.fori_loop(0, trips(count[0]), step, 0)
    total = banks[0][...]
    for a in banks[1:]:
        total = total + a[...]
    out[...] = total


def listed_rows(q, share, listed, ret_both, hot):
    for k in range(listed.shape[0]):
        hot[:, k * LANES : (k + 1) * LANES] = one_hot(listed[k : k + 1, :], share, q * share).astype(jnp.bfloat16)
    return halves(jnp.dot(hot[...], ret_both[...], preferred_element_type=jnp.float32))


def late_join_kernel(lanes, lane, code_a, code_b, totals, mass, listed, near, arrived, *refs):
    out, halo, ret_both, hot, ret, come_halo, come_ret = refs[:7]
    banks = refs[7:]
    blocks, width, _ = ret.shape
    share = out.shape[0]
    first = pltpu.make_async_copy(arrived.at[:, :width, :], halo.at[:blocks], come_halo)
    second = pltpu.make_async_copy(arrived.at[:, width:, :], ret, come_ret)
    first.start()
    second.start()
    halo[blocks] = jnp.zeros((width, LANES), jnp.float32)
    clear(banks)
    q = lax.rem(lane[0] + 2, lanes)
    first.wait()
    flat = halo.reshape((blocks + 1) * width, LANES)
    far_rows(
        1,
        (code_a, code_b),
        totals,
        mass,
        lambda given: flat[pl.ds(far_slot(given), 1), :],
        lambda given: far_source(given) & (share - 1),
        banks,
    )
    second.wait()
    for c in range(blocks):
        put_split(ret_both, slice(c * width, (c + 1) * width), ret[c])
    total = near[pl.ds(pl.multiple_of(q * share, share), share), :]
    for a in banks:
        total = total + a[...]
    out[...] = total + listed_rows(q, share, listed, ret_both, hot)


def join_kernel(lanes, lane, code_a, code_b, totals, mass, listed, near, halo, ret_both, *refs):
    outs, hot, banks = refs[:3], refs[3], refs[4:]
    share = outs[0].shape[0]
    banks[0][...] = near[...]
    clear(banks[1:])
    flat = halo.reshape(halo.shape[0] * halo.shape[1], LANES)
    far_rows(
        0,
        (code_a, code_b),
        totals,
        mass,
        lambda given: flat[pl.ds(far_slot(given), 1), :],
        far_source,
        banks,
    )
    for s, out in zip((1, 3, 0), outs):
        q = lax.rem(lane[0] + s, lanes)
        at = pl.ds(pl.multiple_of(q * share, share), share)
        total = banks[0][at, :]
        for a in banks[1:]:
            total = total + a[at, :]
        out[...] = total + listed_rows(q, share, listed, ret_both, hot) if s else total


def home_kernel(lane, listed, part, ret_both, out, hot):
    out[...] = part[...] + listed_rows(lane[0], out.shape[0], listed, ret_both, hot)


def solution_kernel(lane, lists, *refs):
    lanes = 4
    shares, (field, sent, out, leave) = refs[:lanes], refs[lanes:]
    assemble(lane, lanes, shares, field)
    pack(lists, field, out, out.shape[1])
    go = pltpu.make_async_copy(out, sent, leave)
    go.start()
    go.wait()


def near_gap_kernel(count, order, field, gaps, more):
    rows = field.shape[0]
    more[:rows, :] = field[...]
    more[rows:, :] = jnp.zeros((more.shape[0] - rows, LANES), jnp.float32)

    def step(i, _):
        for u in range(UNROLL):
            e = i * UNROLL + u
            code = order[e]
            gaps[pl.ds(e, 1), :] = (
                field[pl.ds(code & 4095, 1), :] - more[pl.ds(lax.shift_right_logical(code, 12), 1), :]
            )
        return 0

    lax.fori_loop(0, trips(count[0]), step, 0)


def far_gap_kernel(count, slot, gaps, arrived, live, out, halo, taken, come):
    blocks, width, _ = arrived.shape
    groups = live.shape[0]
    first = pltpu.make_async_copy(arrived, halo.at[:blocks], come)
    first.start()
    halo[blocks] = jnp.zeros((width, LANES), jnp.float32)
    first.wait()
    flat = halo.reshape((blocks + 1) * width, LANES)

    def step(i, _):
        for u in range(4 * UNROLL):
            e = i * 4 * UNROLL + u
            taken[pl.ds(e, 1), :] = flat[pl.ds(slot[e], 1), :]
        return 0

    lax.fori_loop(0, lax.div(count[0] + 4 * UNROLL - 1, 4 * UNROLL), step, 0)
    for k in range(groups):
        at = slice(k * LANES, (k + 1) * LANES)
        gap = gaps[at, :] - taken[at, :]
        total = jnp.sum((gap * gap).T, axis=0, keepdims=True)
        alive = live[k : k + 1, :]
        out[k : k + 1, :] = jnp.where(alive > 0, total * (alive / LANES), 0.0)


def moved_by(x, shift, lanes):
    return lax.ppermute(x, "edg", [(i, (i + shift) % lanes) for i in range(lanes)])


def passed_round(blocks, lanes):
    return [blocks[0]] + [moved_by(blocks[s], s, lanes) for s in (2, 1, 3)]


def summed(blocks, lanes):
    home, two, one, three = passed_round(blocks, lanes)
    return (home + one) + (two + three)


def to_all(mine, lanes):
    home, two, one, three = passed_round([mine] * lanes, lanes)
    return [home, one, two, three]


def across(x):
    return lax.all_to_all(x, "vtx", split_axis=0, concat_axis=0, tiled=True)


def local(sketch_cols, edge_weight, ground, src_local, dst_index, send_rows, edge_count):
    blocks = lax.axis_size("vtx")
    lanes = lax.axis_size("edg")
    rows = ground.shape[0]
    edges = edge_weight.shape[0]
    width = send_rows.shape[2]
    slots = blocks * width
    share = rows // lanes
    groups = edges // LANES
    f32, i32, bf16 = jnp.float32, jnp.int32, jnp.bfloat16
    lane = lax.axis_index("edg").astype(i32).reshape(1)
    lists = send_rows[0].reshape(-1)
    listed = lists.reshape(slots // LANES, LANES)
    padded = jnp.pad(send_rows[0], ((0, 0), (0, LANES - width)), constant_values=-1)
    live = (jnp.arange(edges, dtype=i32) < edge_count[0]).astype(f32)
    weight = edge_weight * live
    root = jnp.sqrt(edge_weight) * live
    terms = root[:, None] * sketch_cols.astype(f32)
    live_rows = live.reshape(groups, LANES)
    weight_rows = weight.reshape(groups, LANES)
    source_rows = src_local.reshape(groups, LANES)
    target_rows = dst_index.reshape(groups, LANES)

    outgoing = call(
        functools.partial(halo_side_kernel, rows, slots, width),
        [((blocks, width + 8, LANES), f32, HBM)],
        [VMEM] * 3,
        [pltpu.VMEM((edges, 2 * LANES), bf16), pltpu.VMEM((8 * width, edges), bf16)]
        + [pltpu.VMEM((blocks, width + 8, LANES), f32), pltpu.SemaphoreType.DMA((slots // (8 * width),))],
        "halo_side",
        flops=2 * slots * edges * 2 * LANES,
    )(terms, target_rows, weight_rows)[0]
    returned = across(outgoing)
    own, own_degree = call(
        own_side_kernel,
        [((rows, LANES), f32, HBM), ((rows // LANES, LANES), f32, VMEM)],
        [VMEM] * 4,
        [pltpu.VMEM((edges, 2 * LANES), bf16), pltpu.VMEM((256, edges), bf16)]
        + [pltpu.VMEM((rows, LANES), f32), pltpu.SemaphoreType.DMA((rows // 256,))],
        "own_side",
        flops=2 * rows * edges * 2 * LANES,
    )(terms, source_rows, target_rows, weight_rows)
    sides = call(
        side_join_kernel,
        [((share + 8, LANES), f32, VMEM)] * lanes,
        [SMEM, HBM, VMEM, VMEM, HBM, VMEM],
        [pltpu.VMEM((rows, LANES), f32), pltpu.VMEM((slots, 2 * LANES), bf16), pltpu.VMEM((256, slots), bf16)]
        + [pltpu.VMEM((blocks, width + 8, LANES), f32)]
        + [pltpu.SemaphoreType.DMA] * 2,
        "side_join",
        flops=2 * rows * slots * 2 * LANES,
    )(lane, returned, listed, padded, own, own_degree)
    late = lax.optimization_barrier((edge_count, source_rows, target_rows, edge_weight, *sides))
    begin, source_late, target_late, weight_late, *sides = late
    quarter = edges // QUARTERS
    room = quarter + LANES // 4
    per_edge = ((groups, LANES), i32, VMEM)
    per_edge_f32 = ((groups, LANES), f32, VMEM)
    coded = list(call(
        functools.partial(edge_code_kernel, rows, slots, room),
        [per_edge, per_edge, ((2 * QUARTERS, LANES), i32, VMEM), per_edge_f32, per_edge, per_edge_f32, per_edge, per_edge],
        [SMEM] * 2 + [VMEM] * 3,
        [],
        "edge_code",
    )(begin, lane, source_late, target_late, weight_late.reshape(groups, LANES)))
    totals = coded.pop(2)
    far_order, spot, mass, near_order, near_weight, gap_order, gap_slot = (x.reshape(edges) for x in coded)

    def far_list(first, count):
        return call(
            functools.partial(far_list_kernel, first, room),
            [((4 * room + LANES,), i32, SMEM)],
            [SMEM] * 4,
            [],
            "far_list",
            moved=2**25,
        )(count, far_order, spot, totals)[0]

    code_a = far_list(0, begin)
    side = summed(sides, lanes)
    side, code_a = lax.optimization_barrier((side, code_a))
    later, side = lax.optimization_barrier((begin, side))
    code_b = far_list(2, later)
    far = (code_a, code_b, totals, mass)
    right_share = side[:share]
    degree_share = side[share : share + share // LANES].reshape(share)
    ground_share = lax.dynamic_slice_in_dim(ground, lane[0] * share, share)
    diagonal = (degree_share + ground_share)[:, None]
    inverse = 1.0 / diagonal

    first, pairs = chebyshev_terms(ITERS)
    residual = right_share
    direction = first * inverse * right_share
    solution_share = direction
    for keep, push in pairs:
        shares = to_all(direction, lanes)
        field, message = call(
            functools.partial(field_kernel, lanes),
            [((rows, LANES), f32, HBM), ((blocks, 2 * width, LANES), f32, HBM)],
            [SMEM] * 6 + [VMEM] * lanes,
            [pltpu.VMEM((rows, LANES), f32)]
            + [pltpu.VMEM((blocks, width, LANES), f32)] * 2
            + [pltpu.SemaphoreType.DMA] * 3
            + [pltpu.VMEM((slots + 8, LANES), f32)] * BANKS,
            "field",
        )(lane, *far, lists, *shares)
        arrived = across(message)
        near = call(
            near_kernel,
            [((rows, LANES), f32, VMEM)],
            [SMEM] * 3 + [HBM],
            [pltpu.VMEM((rows, LANES), f32), pltpu.SemaphoreType.DMA] + [pltpu.VMEM((rows, LANES), f32)] * BANKS,
            "near",
            moved=2**25,
        )(edge_count, near_order, near_weight, field)[0]
        two, halo, ret_both = call(
            functools.partial(late_join_kernel, lanes),
            [((share, LANES), f32, VMEM), ((blocks + 1, width, LANES), f32, VMEM), ((slots, 2 * LANES), bf16, VMEM)],
            [SMEM] * 5 + [VMEM, VMEM, HBM],
            [pltpu.VMEM((share, slots), bf16), pltpu.VMEM((blocks, width, LANES), f32)]
            + [pltpu.SemaphoreType.DMA] * 2
            + [pltpu.VMEM((share, LANES), f32)] * BANKS,
            "late_join",
        )(lane, *far, listed, near, arrived)
        one, three, home = call(
            functools.partial(join_kernel, lanes),
            [((share, LANES), f32, VMEM)] * 3,
            [SMEM] * 5 + [VMEM] * 4,
            [pltpu.VMEM((share, slots), bf16)] + [pltpu.VMEM((rows, LANES), f32)] * BANKS,
            "join",
            moved=2**25,
        )(lane, *far, listed, near, halo, ret_both)
        home = call(
            home_kernel,
            [((share, LANES), f32, VMEM)],
            [SMEM] + [VMEM] * 3,
            [pltpu.VMEM((share, slots), bf16)],
            "home",
            moved=2**25,
        )(lane, listed, home, ret_both)[0]
        two = moved_by(two, 2, lanes)
        two, one, three = lax.optimization_barrier((two, one, three))
        flows = (home + two) + (moved_by(one, 1, lanes) + moved_by(three, 3, lanes))
        residual = residual - (diagonal * direction - flows)
        direction = keep * direction + push * inverse * residual
        solution_share = solution_share + direction
    field, message = call(
        solution_kernel,
        [((rows, LANES), f32, VMEM), ((blocks, width, LANES), f32, HBM)],
        [SMEM] * 2 + [VMEM] * lanes,
        [pltpu.VMEM((blocks, width, LANES), f32), pltpu.SemaphoreType.DMA],
        "solution_rows",
    )(lane, lists, *to_all(solution_share, lanes))
    halo = across(message)
    gaps = call(
        near_gap_kernel,
        [((edges, LANES), f32, VMEM)],
        [SMEM] * 2 + [VMEM],
        [pltpu.VMEM((rows + 8, LANES), f32)],
        "near_gap",
        moved=2**25,
    )(edge_count, gap_order, field)[0]
    resistance = call(
        far_gap_kernel,
        [((groups, LANES), f32, VMEM)],
        [SMEM] * 2 + [VMEM, HBM, VMEM],
        [pltpu.VMEM((blocks + 1, width, LANES), f32), pltpu.VMEM((edges, LANES), f32), pltpu.SemaphoreType.DMA],
        "far_gap",
    )(edge_count, gap_slot, gaps, halo, live_rows)[0]
    return (field, resistance.reshape(edges))


def solution(mesh):
    in_specs = (
        P(("vtx", "edg"), None),
        P(("vtx", "edg")),
        P("vtx"),
        P(("vtx", "edg")),
        P(("vtx", "edg")),
        P(("vtx", "edg"), None, None),
        P(("vtx", "edg")),
    )
    out_specs = (P("vtx", None), P(("vtx", "edg")))
    return jax.shard_map(local, mesh=mesh, in_specs=in_specs, out_specs=out_specs, check_vma=False)
```

```python
import functools

import jax
import jax.numpy as jnp
from jax import lax
from jax.experimental import pallas as pl
from jax.experimental.pallas import tpu as pltpu
from jax.sharding import PartitionSpec as P

ITERS = 3
LANES = 128
UNROLL = 16
BANKS = 4
QUARTERS = 4
SPARE = 1536
BESIDE, OPPOSITE, HOME = range(3)
KINDS = 3
PARTS = 8

lam_low = 0.05
lam_high = 2.0

SMEM = pl.BlockSpec(memory_space=pltpu.SMEM)
VMEM = pl.BlockSpec(memory_space=pltpu.VMEM)
HBM = pl.BlockSpec(memory_space=pltpu.HBM)
LIMIT = 24 * 2**20


def chebyshev_terms(steps):
    centre = (lam_high + lam_low) / 2.0
    half_width = (lam_high - lam_low) / 2.0
    sigma_val = centre / half_width
    rho_prev = 1.0 / sigma_val
    pairs = []
    for count_idx in range(steps - 1):
        rho_next = 1.0 / (2.0 * sigma_val - rho_prev)
        pairs.append((rho_next * rho_prev, 2.0 * rho_next / half_width))
        rho_prev = rho_next
    return (1.0 / centre, pairs)


def call(kernel, outs, ins, scratch, name, flops=0, moved=2**22):
    return pl.pallas_call(
        kernel,
        out_shape=[
            pltpu.HBM(shape, dtype) if space is HBM else jax.ShapeDtypeStruct(shape, dtype) for shape, dtype, space in outs
        ],
        in_specs=ins,
        out_specs=[space for _, _, space in outs],
        scratch_shapes=scratch,
        compiler_params=pltpu.CompilerParams(vmem_limit_bytes=LIMIT),
        cost_estimate=pl.CostEstimate(flops=flops, bytes_accessed=moved, transcendentals=0),
        name=name,
    )


def split(x):
    high = x.astype(jnp.bfloat16)
    return high, (x - high.astype(jnp.float32)).astype(jnp.bfloat16)


def put_split(ref, rows, x):
    high, low = split(x)
    ref[rows, :LANES] = high
    ref[rows, LANES:] = low


def halves(x):
    return x[:, :LANES] + x[:, LANES:]


def one_hot(row, height, base):
    place = lax.broadcasted_iota(jnp.int32, (height, row.shape[1]), 0) + base
    return jnp.where(place == row, 1.0, 0.0)


def factored(pick, groups, high_of, low_of, weight_of, height):
    total = jnp.zeros((2 * height, LANES), jnp.float32)
    for k0 in range(0, groups, pick):
        left, right = [], []
        for k in range(k0, k0 + pick):
            member = one_hot(high_of(k), height, 0) * weight_of(k)
            high, low = split(member)
            left.append(jnp.concatenate([high, low], axis=0))
            right.append(one_hot(low_of(k), LANES, 0).astype(jnp.bfloat16))
        total = total + lax.dot_general(
            jnp.concatenate(left, axis=1),
            jnp.concatenate(right, axis=1),
            (((1,), (1,)), ((), ())),
            preferred_element_type=jnp.float32,
        )
    return total[:height] + total[height:]


def halo_side_kernel(rows, slots, width, terms, target, weight, sent, both, hot, out, leave):
    groups = target.shape[0]
    tall = hot.shape[0]
    per = tall // width
    blocks = slots // width
    chunks = slots // tall

    def slot(k):
        return target[k : k + 1, :] - rows

    def block_of(k):
        return jnp.where(slot(k) < 0, -1, lax.shift_right_arithmetic(slot(k) * 1366, 16))

    def within(k):
        return slot(k) - block_of(k) * width

    deg = factored(4, groups, block_of, within, lambda k: weight[k : k + 1, :], blocks)
    for c in range(blocks):
        out[c, width : width + 8, :] = jnp.broadcast_to(deg[c : c + 1, :], (8, LANES))
    put_split(both, slice(None), terms[...])

    def part(i):
        at = pl.ds(i * per, per)
        return pltpu.make_async_copy(out.at[at], sent.at[at], leave.at[i])

    def chunk(i, _):
        base = rows + i * tall
        for k in range(groups):
            hot[:, k * LANES : (k + 1) * LANES] = one_hot(target[k : k + 1, :], tall, base).astype(jnp.bfloat16)
        got = halves(jnp.dot(hot[...], both[...], preferred_element_type=jnp.float32))
        for c in range(per):
            out[i * per + c, :width, :] = -got[c * width : (c + 1) * width]
        part(i).start()
        return 0

    lax.fori_loop(0, chunks, chunk, 0)
    for i in range(chunks):
        part(i).wait()


def own_side_kernel(terms, source, target, weight, kept, degree, both, hot, out, leave):
    groups = target.shape[0]
    rows = out.shape[0]
    put_split(both, slice(None), terms[...])
    tall = hot.shape[0]

    def part(i):
        at = pl.ds(pl.multiple_of(i * tall, tall), tall)
        return pltpu.make_async_copy(out.at[at, :], kept.at[at, :], leave.at[i])

    def chunk(i, _):
        base = i * tall
        for k in range(groups):
            plus = one_hot(source[k : k + 1, :], tall, base)
            minus = one_hot(target[k : k + 1, :], tall, base)
            hot[:, k * LANES : (k + 1) * LANES] = (plus - minus).astype(jnp.bfloat16)
        out[pl.ds(pl.multiple_of(i * tall, tall), tall), :] = halves(
            jnp.dot(hot[...], both[...], preferred_element_type=jnp.float32)
        )
        part(i).start()
        return 0

    lax.fori_loop(0, rows // tall, chunk, 0)

    def total(ref):
        return factored(
            4,
            groups,
            lambda k: lax.shift_right_logical(ref[k : k + 1, :], 7),
            lambda k: ref[k : k + 1, :] & (LANES - 1),
            lambda k: weight[k : k + 1, :],
            rows // LANES,
        )

    degree[...] = total(source) + total(target)
    for i in range(rows // tall):
        part(i).wait()


def scatter_back(ret_both, listed, hot, emit, rows):
    tall = hot.shape[0]
    groups = listed.shape[0]

    def chunk(i, _):
        base = i * tall
        for k in range(groups):
            hot[:, k * LANES : (k + 1) * LANES] = one_hot(listed[k : k + 1, :], tall, base).astype(jnp.bfloat16)
        emit(i, halves(jnp.dot(hot[...], ret_both[...], preferred_element_type=jnp.float32)))
        return 0

    lax.fori_loop(0, rows // tall, chunk, 0)


def side_join_kernel(lane, returned, listed, padded, own, own_degree, *refs):
    lanes = 4
    outs, (acc, ret_both, hot, landed, arrival, arrival_own) = refs[:lanes], refs[lanes:]
    come = pltpu.make_async_copy(returned, landed, arrival)
    come.start()
    mine = pltpu.make_async_copy(own, acc, arrival_own)
    mine.start()
    blocks = returned.shape[0]
    rows = own.shape[0]
    width = listed.shape[0] * LANES // blocks
    share = rows // lanes
    come.wait()
    for c in range(blocks):
        put_split(ret_both, slice(c * width, (c + 1) * width), landed[c, :width, :])

    def emit(i, got):
        at = pl.ds(pl.multiple_of(i * hot.shape[0], hot.shape[0]), hot.shape[0])
        acc[at, :] = acc[at, :] + got

    mine.wait()
    scatter_back(ret_both, listed, hot, emit, rows)
    deg = own_degree[...] + factored(
        4,
        blocks,
        lambda k: lax.shift_right_arithmetic(padded[k : k + 1, :], 7),
        lambda k: padded[k : k + 1, :] & (LANES - 1),
        lambda k: landed[k, width : width + 1, :],
        rows // LANES,
    )
    deg_rows = share // LANES
    for s in range(lanes):
        q = lax.rem(lane[0] + s, lanes)
        outs[s][:share, :] = acc[pl.ds(pl.multiple_of(q * share, share), share), :]
        row = jnp.zeros((8, LANES), jnp.float32)
        place = lax.broadcasted_iota(jnp.int32, (8, LANES), 0)
        for p in range(lanes):
            for d in range(deg_rows):
                one = jnp.broadcast_to(deg[p * deg_rows + d : p * deg_rows + d + 1, :], (8, LANES))
                row = jnp.where((place == d) & (q == p), one, row)
        outs[s][share : share + 8, :] = row


def edge_code_kernel(
    rows, slots, room, count, lane, source, target, weight, far_code, spot, totals, mass, near_code, near_mass, gap_code, gap_slot
):
    groups = source.shape[0]
    per = groups // QUARTERS
    s, t = source[...], target[...]
    row = lax.broadcasted_iota(jnp.int32, s.shape, 0)
    number = row * LANES + lax.broadcasted_iota(jnp.int32, s.shape, 1)
    live = number < count[0]
    away = t >= rows
    load = jnp.where(live, weight[...], 0.0)
    mass[...] = load
    near_mass[...] = jnp.where(away, 0.0, load)
    near_code[...] = s | (jnp.where(away, 0, t) << 12)
    gap_code[...] = s | (jnp.minimum(t, rows) << 12)
    gap_slot[...] = jnp.where(away, t - rows, slots)
    far_code[...] = (jnp.where(away, t - rows, 0) << 21) | (s << 10) | (number & (per * LANES - 1))
    left = lax.broadcasted_iota(jnp.int32, (LANES, LANES), 0)
    right = lax.broadcasted_iota(jnp.int32, (LANES, LANES), 1)
    before = jnp.where(left < right, 1.0, 0.0).astype(jnp.bfloat16)
    ones = jnp.ones((LANES, LANES), jnp.bfloat16)
    down = lax.broadcasted_iota(jnp.int32, (groups, groups), 0)
    over = lax.broadcasted_iota(jnp.int32, (groups, groups), 1)
    same = lax.shift_right_logical(down, 3) == lax.shift_right_logical(over, 3)
    above = jnp.where(same & (over < down), 1.0, 0.0).astype(jnp.bfloat16)
    apart = (lax.shift_right_logical(s, 9) - lane[0]) & 3
    kinds = jnp.where(apart == 0, HOME, jnp.where(apart == 2, OPPOSITE, BESIDE))
    region = (lax.shift_right_logical(row, 3) & 1) * KINDS * room
    where = jnp.zeros_like(row) + 2 * KINDS * room
    for kind in range(KINDS):
        counted = away & live & (kinds == kind)
        flags = jnp.where(counted, 1.0, 0.0).astype(jnp.bfloat16)
        within = jnp.dot(flags, before, preferred_element_type=jnp.float32)
        total = jnp.dot(flags, ones, preferred_element_type=jnp.float32)
        base = jnp.dot(above, total.astype(jnp.bfloat16), preferred_element_type=jnp.float32)
        where = jnp.where(counted, region + kind * room + (within + base).astype(jnp.int32), where)
        through = (base + total).astype(jnp.int32)
        for c in range(QUARTERS):
            totals[kind * QUARTERS + c : kind * QUARTERS + c + 1, :] = through[(c + 1) * per - 1 : (c + 1) * per, :]
    spot[...] = where


def far_list_kernel(first, room, count, order, spot, totals, code):
    half = order.shape[0] // 2
    begin = first * order.shape[0] // QUARTERS

    def step(i, _):
        e = begin + i * 8
        given = [order[e + u] for u in range(8)]
        to = [spot[e + u] for u in range(8)]
        for u in range(8):
            code[to[u]] = given[u]
        return 0

    live = jnp.clip(count[0] - begin, 0, half)
    lax.fori_loop(0, lax.div(live + 7, 8), step, 0)
    nothing = jnp.int32(SPARE - 2048) << 21
    for c in range(2):
        for kind in range(KINDS):
            end = (KINDS * c + kind) * room + totals[kind * QUARTERS + first + c, 0]
            for u in range(UNROLL):
                code[end + u] = nothing


def trips(n):
    return lax.div(n + UNROLL - 1, UNROLL)


def clear(banks):
    for a in banks:
        a[...] = jnp.zeros_like(a)


def far_rows(kind, lists, totals, mass, take, give, banks):
    quarter = mass.shape[0] // QUARTERS
    many = len(banks)
    for h, code in enumerate(lists):
        room = (code.shape[0] - LANES) // (2 * KINDS)
        for c in range(2):
            start = (KINDS * c + kind) * room
            base = (2 * h + c) * quarter

            def step(i, _):
                for u in range(0, UNROLL, many):
                    at = start + i * UNROLL + u
                    given = [code[at + k] for k in range(many)]
                    rows = [take(given[k]) * mass[base + (given[k] & 1023)] for k in range(many)]
                    to = [pl.ds(give(given[k]), 1) for k in range(many)]
                    new = [banks[k][to[k], :] + rows[k] for k in range(many)]
                    for k in range(many):
                        banks[k][to[k], :] = new[k]
                return 0

            lax.fori_loop(0, trips(totals[kind * QUARTERS + 2 * h + c, 0]), step, 0)


def far_source(given):
    return lax.shift_right_logical(given, 10) & 2047


def far_slot(given):
    return lax.shift_right_logical(given, 21)


def source_of(given):
    return given & 4095


def target_of(given):
    return lax.shift_right_logical(given, 12)


def place(lane, lanes, shift, share, field):
    q = lax.rem(lane[0] - shift + lanes, lanes)
    rows = share.shape[0]
    field[pl.ds(pl.multiple_of(q * rows, rows), rows), :] = share[...]


def assemble(lane, lanes, shares, field):
    for s in range(lanes):
        place(lane, lanes, s, shares[s], field)


def pack(lists, field, out, width, part):
    per = out.shape[0] // PARTS

    def step(i, _):
        for c in range(per):
            for r in range(width):
                out[i * per + c, pl.ds(r, 1), :] = field[pl.ds(lists[(i * per + c) * width + r], 1), :]
        part(i).start()
        return 0

    lax.fori_loop(0, PARTS, step, 0)


def early_field_kernel(lanes, lane, code_a, code_b, totals, mass, home, opposite, out, field, *banks):
    place(lane, lanes, 0, home, field)
    place(lane, lanes, 2, opposite, field)
    clear(banks)
    for kind in (HOME, OPPOSITE):
        far_rows(
            kind,
            (code_a, code_b),
            totals,
            mass,
            lambda given: field[pl.ds(far_source(given), 1), :],
            far_slot,
            banks,
        )
    total = banks[0][...]
    for a in banks[1:]:
        total = total + a[...]
    out[...] = total


def field_kernel(lanes, lane, code_a, code_b, totals, mass, lists, early, *refs):
    shares, (kept, sent), refs = refs[:lanes], refs[lanes : lanes + 2], refs[lanes + 2 :]
    field, out, sums, leave_field, leave, leave_sums = refs[:6]
    banks = refs[6:]
    blocks, width, _ = out.shape
    assemble(lane, lanes, shares, field)
    keep = pltpu.make_async_copy(field, kept, leave_field)
    keep.start()
    banks[0][...] = early[...]
    clear(banks[1:])
    far_rows(
        BESIDE,
        (code_a, code_b),
        totals,
        mass,
        lambda given: field[pl.ds(far_source(given), 1), :],
        far_slot,
        banks,
    )
    for c in range(blocks):
        at = slice(c * width, (c + 1) * width)
        total = banks[0][at, :]
        for a in banks[1:]:
            total = total + a[at, :]
        sums[c] = total
    more = pltpu.make_async_copy(sums, sent.at[:, width:, :], leave_sums)
    more.start()
    per = blocks // PARTS

    def part(i):
        at = pl.ds(i * per, per)
        return pltpu.make_async_copy(out.at[at], sent.at[at, :width, :], leave.at[i])

    pack(lists, field, out, width, part)
    keep.wait()
    more.wait()
    for i in range(PARTS):
        part(i).wait()


def near_kernel(count, order, heavy, kept, out, field, come, *banks):
    bring = pltpu.make_async_copy(kept, field, come)
    bring.start()
    clear(banks)
    bring.wait()

    def step(i, _):
        for u in range(0, UNROLL, BANKS):
            at = i * UNROLL + u
            code = [order[at + k] for k in range(BANKS)]
            mass = [heavy[at + k] for k in range(BANKS)]
            one = [pl.ds(source_of(code[k]), 1) for k in range(BANKS)]
            two = [pl.ds(target_of(code[k]), 1) for k in range(BANKS)]
            from_one = [field[one[k], :] * mass[k] for k in range(BANKS)]
            from_two = [field[two[k], :] * mass[k] for k in range(BANKS)]
            new = [banks[k][one[k], :] + from_two[k] for k in range(BANKS)]
            for k in range(BANKS):
                banks[k][one[k], :] = new[k]
            new = [banks[k][two[k], :] + from_one[k] for k in range(BANKS)]
            for k in range(BANKS):
                banks[k][two[k], :] = new[k]
        return 0

    lax.fori_loop(0, trips(count[0]), step, 0)
    total = banks[0][...]
    for a in banks[1:]:
        total = total + a[...]
    out[...] = total


def listed_rows(q, share, listed, ret_both, hot):
    for k in range(listed.shape[0]):
        hot[:, k * LANES : (k + 1) * LANES] = one_hot(listed[k : k + 1, :], share, q * share).astype(jnp.bfloat16)
    return halves(jnp.dot(hot[...], ret_both[...], preferred_element_type=jnp.float32))


def late_join_kernel(lanes, lane, code_a, code_b, totals, mass, listed, near, arrived, *refs):
    out, halo, ret_both, hot, ret, come_halo, come_ret = refs[:7]
    banks = refs[7:]
    blocks, width, _ = ret.shape
    share = out.shape[0]
    first = pltpu.make_async_copy(arrived.at[:, :width, :], halo.at[:blocks], come_halo)
    second = pltpu.make_async_copy(arrived.at[:, width:, :], ret, come_ret)
    first.start()
    second.start()
    halo[blocks] = jnp.zeros((width, LANES), jnp.float32)
    clear(banks)
    q = lax.rem(lane[0] + 2, lanes)
    first.wait()
    flat = halo.reshape((blocks + 1) * width, LANES)
    far_rows(
        OPPOSITE,
        (code_a, code_b),
        totals,
        mass,
        lambda given: flat[pl.ds(far_slot(given), 1), :],
        lambda given: far_source(given) & (share - 1),
        banks,
    )
    second.wait()
    for c in range(blocks):
        put_split(ret_both, slice(c * width, (c + 1) * width), ret[c])
    total = near[pl.ds(pl.multiple_of(q * share, share), share), :]
    for a in banks:
        total = total + a[...]
    out[...] = total + listed_rows(q, share, listed, ret_both, hot)


def join_kernel(lanes, lane, code_a, code_b, totals, mass, listed, near, halo, ret_both, *refs):
    outs, hot, banks = refs[:2], refs[2], refs[3:]
    share = outs[0].shape[0]
    spots = []
    for s in (1, 3):
        q = lax.rem(lane[0] + s, lanes)
        at = pl.ds(pl.multiple_of(q * share, share), share)
        banks[0][at, :] = near[at, :]
        for a in banks[1:]:
            a[at, :] = jnp.zeros((share, LANES), jnp.float32)
        spots.append((q, at))
    flat = halo.reshape(halo.shape[0] * halo.shape[1], LANES)
    far_rows(
        BESIDE,
        (code_a, code_b),
        totals,
        mass,
        lambda given: flat[pl.ds(far_slot(given), 1), :],
        far_source,
        banks,
    )
    for (q, at), out in zip(spots, outs):
        total = banks[0][at, :]
        for a in banks[1:]:
            total = total + a[at, :]
        out[...] = total + listed_rows(q, share, listed, ret_both, hot)


def home_kernel(lane, code_a, code_b, totals, mass, listed, near, halo, ret_both, out, hot, *banks):
    share = out.shape[0]
    clear(banks)
    flat = halo.reshape(halo.shape[0] * halo.shape[1], LANES)
    far_rows(
        HOME,
        (code_a, code_b),
        totals,
        mass,
        lambda given: flat[pl.ds(far_slot(given), 1), :],
        lambda given: far_source(given) & (share - 1),
        banks,
    )
    total = near[pl.ds(pl.multiple_of(lane[0] * share, share), share), :]
    for a in banks:
        total = total + a[...]
    out[...] = total + listed_rows(lane[0], share, listed, ret_both, hot)


def solution_kernel(lane, lists, *refs):
    lanes = 4
    shares, (field, sent, out, leave) = refs[:lanes], refs[lanes:]
    assemble(lane, lanes, shares, field)
    per = out.shape[0] // PARTS

    def part(i):
        at = pl.ds(i * per, per)
        return pltpu.make_async_copy(out.at[at], sent.at[at], leave.at[i])

    pack(lists, field, out, out.shape[1], part)
    for i in range(PARTS):
        part(i).wait()


def near_gap_kernel(count, order, field, gaps, more):
    rows = field.shape[0]
    more[:rows, :] = field[...]
    more[rows:, :] = jnp.zeros((more.shape[0] - rows, LANES), jnp.float32)

    def step(i, _):
        for u in range(UNROLL):
            e = i * UNROLL + u
            code = order[e]
            gaps[pl.ds(e, 1), :] = (
                field[pl.ds(code & 4095, 1), :] - more[pl.ds(lax.shift_right_logical(code, 12), 1), :]
            )
        return 0

    lax.fori_loop(0, trips(count[0]), step, 0)


def far_gap_kernel(count, slot, gaps, arrived, live, out, halo, taken, come):
    blocks, width, _ = arrived.shape
    groups = live.shape[0]
    first = pltpu.make_async_copy(arrived, halo.at[:blocks], come)
    first.start()
    halo[blocks] = jnp.zeros((width, LANES), jnp.float32)
    first.wait()
    flat = halo.reshape((blocks + 1) * width, LANES)

    def step(i, _):
        for u in range(4 * UNROLL):
            e = i * 4 * UNROLL + u
            taken[pl.ds(e, 1), :] = flat[pl.ds(slot[e], 1), :]
        return 0

    lax.fori_loop(0, lax.div(count[0] + 4 * UNROLL - 1, 4 * UNROLL), step, 0)
    for k in range(groups):
        at = slice(k * LANES, (k + 1) * LANES)
        gap = gaps[at, :] - taken[at, :]
        total = jnp.sum((gap * gap).T, axis=0, keepdims=True)
        alive = live[k : k + 1, :]
        out[k : k + 1, :] = jnp.where(alive > 0, total * (alive / LANES), 0.0)


def moved_by(x, shift, lanes):
    return lax.ppermute(x, "edg", [(i, (i + shift) % lanes) for i in range(lanes)])


def passed_round(blocks, lanes):
    return [blocks[0]] + [moved_by(blocks[s], s, lanes) for s in (2, 1, 3)]


def summed(blocks, lanes):
    home, two, one, three = passed_round(blocks, lanes)
    return (home + one) + (two + three)


def to_all(mine, lanes):
    home, two, one, three = passed_round([mine] * lanes, lanes)
    return [home, one, two, three]


def across(x):
    return lax.all_to_all(x, "vtx", split_axis=0, concat_axis=0, tiled=True)


def local(sketch_cols, edge_weight, ground, src_local, dst_index, send_rows, edge_count):
    blocks = lax.axis_size("vtx")
    lanes = lax.axis_size("edg")
    rows = ground.shape[0]
    edges = edge_weight.shape[0]
    width = send_rows.shape[2]
    slots = blocks * width
    share = rows // lanes
    groups = edges // LANES
    f32, i32, bf16 = jnp.float32, jnp.int32, jnp.bfloat16
    lane = lax.axis_index("edg").astype(i32).reshape(1)
    lists = send_rows[0].reshape(-1)
    listed = lists.reshape(slots // LANES, LANES)
    padded = jnp.pad(send_rows[0], ((0, 0), (0, LANES - width)), constant_values=-1)
    live = (jnp.arange(edges, dtype=i32) < edge_count[0]).astype(f32)
    weight = edge_weight * live
    root = jnp.sqrt(edge_weight) * live
    terms = root[:, None] * sketch_cols.astype(f32)
    live_rows = live.reshape(groups, LANES)
    weight_rows = weight.reshape(groups, LANES)
    source_rows = src_local.reshape(groups, LANES)
    target_rows = dst_index.reshape(groups, LANES)

    outgoing = call(
        functools.partial(halo_side_kernel, rows, slots, width),
        [((blocks, width + 8, LANES), f32, HBM)],
        [VMEM] * 3,
        [pltpu.VMEM((edges, 2 * LANES), bf16), pltpu.VMEM((8 * width, edges), bf16)]
        + [pltpu.VMEM((blocks, width + 8, LANES), f32), pltpu.SemaphoreType.DMA((slots // (8 * width),))],
        "halo_side",
        flops=2 * slots * edges * 2 * LANES,
    )(terms, target_rows, weight_rows)[0]
    returned = across(outgoing)
    own, own_degree = call(
        own_side_kernel,
        [((rows, LANES), f32, HBM), ((rows // LANES, LANES), f32, VMEM)],
        [VMEM] * 4,
        [pltpu.VMEM((edges, 2 * LANES), bf16), pltpu.VMEM((256, edges), bf16)]
        + [pltpu.VMEM((rows, LANES), f32), pltpu.SemaphoreType.DMA((rows // 256,))],
        "own_side",
        flops=2 * rows * edges * 2 * LANES,
    )(terms, source_rows, target_rows, weight_rows)
    sides = call(
        side_join_kernel,
        [((share + 8, LANES), f32, VMEM)] * lanes,
        [SMEM, HBM, VMEM, VMEM, HBM, VMEM],
        [pltpu.VMEM((rows, LANES), f32), pltpu.VMEM((slots, 2 * LANES), bf16), pltpu.VMEM((256, slots), bf16)]
        + [pltpu.VMEM((blocks, width + 8, LANES), f32)]
        + [pltpu.SemaphoreType.DMA] * 2,
        "side_join",
        flops=2 * rows * slots * 2 * LANES,
    )(lane, returned, listed, padded, own, own_degree)
    late = lax.optimization_barrier((edge_count, source_rows, target_rows, edge_weight, *sides))
    begin, source_late, target_late, weight_late, *sides = late
    quarter = edges // QUARTERS
    room = quarter + LANES // 2
    per_edge = ((groups, LANES), i32, VMEM)
    per_edge_f32 = ((groups, LANES), f32, VMEM)
    coded = list(call(
        functools.partial(edge_code_kernel, rows, slots, room),
        [per_edge, per_edge, ((4 * QUARTERS, LANES), i32, VMEM), per_edge_f32, per_edge, per_edge_f32, per_edge, per_edge],
        [SMEM] * 2 + [VMEM] * 3,
        [],
        "edge_code",
    )(begin, lane, source_late, target_late, weight_late.reshape(groups, LANES)))
    totals = coded.pop(2)
    far_order, spot, mass, near_order, near_weight, gap_order, gap_slot = (x.reshape(edges) for x in coded)

    def far_list(first, count):
        return call(
            functools.partial(far_list_kernel, first, room),
            [((2 * KINDS * room + LANES,), i32, SMEM)],
            [SMEM] * 4,
            [],
            "far_list",
            moved=2**25,
        )(count, far_order, spot, totals)[0]

    code_a = far_list(0, begin)
    side = summed(sides, lanes)
    side, code_a = lax.optimization_barrier((side, code_a))
    later, side = lax.optimization_barrier((begin, side))
    code_b = far_list(2, later)
    far = (code_a, code_b, totals, mass)
    right_share = side[:share]
    degree_share = side[share : share + share // LANES].reshape(share)
    ground_share = lax.dynamic_slice_in_dim(ground, lane[0] * share, share)
    diagonal = (degree_share + ground_share)[:, None]
    inverse = 1.0 / diagonal

    first, pairs = chebyshev_terms(ITERS)
    residual = right_share
    direction = first * inverse * right_share
    solution_share = direction
    for keep, push in pairs:
        shares = to_all(direction, lanes)
        early = call(
            functools.partial(early_field_kernel, lanes),
            [((slots + 8, LANES), f32, VMEM)],
            [SMEM] * 5 + [VMEM] * 2,
            [pltpu.VMEM((rows, LANES), f32)] + [pltpu.VMEM((slots + 8, LANES), f32)] * BANKS,
            "early_field",
            moved=2**25,
        )(lane, *far, shares[0], shares[2])[0]
        field, message = call(
            functools.partial(field_kernel, lanes),
            [((rows, LANES), f32, HBM), ((blocks, 2 * width, LANES), f32, HBM)],
            [SMEM] * 6 + [VMEM] * (1 + lanes),
            [pltpu.VMEM((rows, LANES), f32)]
            + [pltpu.VMEM((blocks, width, LANES), f32)] * 2
            + [pltpu.SemaphoreType.DMA, pltpu.SemaphoreType.DMA((PARTS,)), pltpu.SemaphoreType.DMA]
            + [pltpu.VMEM((slots + 8, LANES), f32)] * BANKS,
            "field",
        )(lane, *far, lists, early, *shares)
        arrived = across(message)
        near = call(
            near_kernel,
            [((rows, LANES), f32, VMEM)],
            [SMEM] * 3 + [HBM],
            [pltpu.VMEM((rows, LANES), f32), pltpu.SemaphoreType.DMA] + [pltpu.VMEM((rows, LANES), f32)] * BANKS,
            "near",
            moved=2**25,
        )(edge_count, near_order, near_weight, field)[0]
        two, halo, ret_both = call(
            functools.partial(late_join_kernel, lanes),
            [((share, LANES), f32, VMEM), ((blocks + 1, width, LANES), f32, VMEM), ((slots, 2 * LANES), bf16, VMEM)],
            [SMEM] * 5 + [VMEM, VMEM, HBM],
            [pltpu.VMEM((share, slots), bf16), pltpu.VMEM((blocks, width, LANES), f32)]
            + [pltpu.SemaphoreType.DMA] * 2
            + [pltpu.VMEM((share, LANES), f32)] * BANKS,
            "late_join",
        )(lane, *far, listed, near, arrived)
        one, three = call(
            functools.partial(join_kernel, lanes),
            [((share, LANES), f32, VMEM)] * 2,
            [SMEM] * 5 + [VMEM] * 4,
            [pltpu.VMEM((share, slots), bf16)] + [pltpu.VMEM((rows, LANES), f32)] * BANKS,
            "join",
            moved=2**25,
        )(lane, *far, listed, near, halo, ret_both)
        home = call(
            home_kernel,
            [((share, LANES), f32, VMEM)],
            [SMEM] * 5 + [VMEM] * 4,
            [pltpu.VMEM((share, slots), bf16)] + [pltpu.VMEM((share, LANES), f32)] * BANKS,
            "home",
            moved=2**25,
        )(lane, *far, listed, near, halo, ret_both)[0]
        two = moved_by(two, 2, lanes)
        two, one, three = lax.optimization_barrier((two, one, three))
        flows = (home + two) + (moved_by(one, 1, lanes) + moved_by(three, 3, lanes))
        residual = residual - (diagonal * direction - flows)
        direction = keep * direction + push * inverse * residual
        solution_share = solution_share + direction
    field, message = call(
        solution_kernel,
        [((rows, LANES), f32, VMEM), ((blocks, width, LANES), f32, HBM)],
        [SMEM] * 2 + [VMEM] * lanes,
        [pltpu.VMEM((blocks, width, LANES), f32), pltpu.SemaphoreType.DMA((PARTS,))],
        "solution_rows",
    )(lane, lists, *to_all(solution_share, lanes))
    halo = across(message)
    gaps = call(
        near_gap_kernel,
        [((edges, LANES), f32, VMEM)],
        [SMEM] * 2 + [VMEM],
        [pltpu.VMEM((rows + 8, LANES), f32)],
        "near_gap",
        moved=2**25,
    )(edge_count, gap_order, field)[0]
    resistance = call(
        far_gap_kernel,
        [((groups, LANES), f32, VMEM)],
        [SMEM] * 2 + [VMEM, HBM, VMEM],
        [pltpu.VMEM((blocks + 1, width, LANES), f32), pltpu.VMEM((edges, LANES), f32), pltpu.SemaphoreType.DMA],
        "far_gap",
    )(edge_count, gap_slot, gaps, halo, live_rows)[0]
    return (field, resistance.reshape(edges))


def solution(mesh):
    in_specs = (
        P(("vtx", "edg"), None),
        P(("vtx", "edg")),
        P("vtx"),
        P(("vtx", "edg")),
        P(("vtx", "edg")),
        P(("vtx", "edg"), None, None),
        P(("vtx", "edg")),
    )
    out_specs = (P("vtx", None), P(("vtx", "edg")))
    return jax.shard_map(local, mesh=mesh, in_specs=in_specs, out_specs=out_specs, check_vma=False)
```

```python
import functools

import jax
import jax.numpy as jnp
from jax import lax
from jax.experimental import pallas as pl
from jax.experimental.pallas import tpu as pltpu
from jax.sharding import PartitionSpec as P

ITERS = 3
LANES = 128
UNROLL = 16
BANKS = 4
QUARTERS = 4
SPARE = 1536
BESIDE, OPPOSITE, HOME = range(3)
KINDS = 3
PARTS = 8

lam_low = 0.05
lam_high = 2.0

SMEM = pl.BlockSpec(memory_space=pltpu.SMEM)
VMEM = pl.BlockSpec(memory_space=pltpu.VMEM)
HBM = pl.BlockSpec(memory_space=pltpu.HBM)
LIMIT = 24 * 2**20


def chebyshev_terms(steps):
    centre = (lam_high + lam_low) / 2.0
    half_width = (lam_high - lam_low) / 2.0
    sigma_val = centre / half_width
    rho_prev = 1.0 / sigma_val
    pairs = []
    for count_idx in range(steps - 1):
        rho_next = 1.0 / (2.0 * sigma_val - rho_prev)
        pairs.append((rho_next * rho_prev, 2.0 * rho_next / half_width))
        rho_prev = rho_next
    return (1.0 / centre, pairs)


def call(kernel, outs, ins, scratch, name, flops=0, moved=2**22):
    return pl.pallas_call(
        kernel,
        out_shape=[
            pltpu.HBM(shape, dtype) if space is HBM else jax.ShapeDtypeStruct(shape, dtype) for shape, dtype, space in outs
        ],
        in_specs=ins,
        out_specs=[space for _, _, space in outs],
        scratch_shapes=scratch,
        compiler_params=pltpu.CompilerParams(vmem_limit_bytes=LIMIT),
        cost_estimate=pl.CostEstimate(flops=flops, bytes_accessed=moved, transcendentals=0),
        name=name,
    )


def split(x):
    high = x.astype(jnp.bfloat16)
    return high, (x - high.astype(jnp.float32)).astype(jnp.bfloat16)


def put_split(ref, rows, x):
    high, low = split(x)
    ref[rows, :LANES] = high
    ref[rows, LANES:] = low


def halves(x):
    return x[:, :LANES] + x[:, LANES:]


def one_hot(row, height, base):
    place = lax.broadcasted_iota(jnp.int32, (height, row.shape[1]), 0) + base
    return jnp.where(place == row, 1.0, 0.0)


def factored(pick, groups, high_of, low_of, weight_of, height):
    total = jnp.zeros((2 * height, LANES), jnp.float32)
    for k0 in range(0, groups, pick):
        left, right = [], []
        for k in range(k0, k0 + pick):
            member = one_hot(high_of(k), height, 0) * weight_of(k)
            high, low = split(member)
            left.append(jnp.concatenate([high, low], axis=0))
            right.append(one_hot(low_of(k), LANES, 0).astype(jnp.bfloat16))
        total = total + lax.dot_general(
            jnp.concatenate(left, axis=1),
            jnp.concatenate(right, axis=1),
            (((1,), (1,)), ((), ())),
            preferred_element_type=jnp.float32,
        )
    return total[:height] + total[height:]


def halo_side_kernel(rows, slots, width, terms, target, weight, sent, both, hot, other, out, leave):
    groups = target.shape[0]
    tall = hot.shape[0]
    per = tall // width
    blocks = slots // width
    chunks = slots // tall

    def slot(k):
        return target[k : k + 1, :] - rows

    def block_of(k):
        return jnp.where(slot(k) < 0, -1, lax.shift_right_arithmetic(slot(k) * 1366, 16))

    def within(k):
        return slot(k) - block_of(k) * width

    deg = factored(4, groups, block_of, within, lambda k: weight[k : k + 1, :], blocks)
    for c in range(blocks):
        out[c, width : width + 8, :] = jnp.broadcast_to(deg[c : c + 1, :], (8, LANES))
    put_split(both, slice(None), terms[...])

    def part(i):
        at = pl.ds(i * per, per)
        return pltpu.make_async_copy(out.at[at], sent.at[at], leave.at[i])

    def build(i):
        to = (hot, other)[i % 2]
        for k in range(groups):
            to[:, k * LANES : (k + 1) * LANES] = one_hot(target[k : k + 1, :], tall, rows + i * tall).astype(jnp.bfloat16)

    build(0)
    for i in range(chunks):
        if i + 1 < chunks:
            build(i + 1)
        got = halves(jnp.dot((hot, other)[i % 2][...], both[...], preferred_element_type=jnp.float32))
        for c in range(per):
            out[i * per + c, :width, :] = -got[c * width : (c + 1) * width]
        part(i).start()
    for i in range(chunks):
        part(i).wait()


def own_side_kernel(terms, source, target, weight, kept, degree, both, hot, out, leave):
    groups = target.shape[0]
    rows = out.shape[0]
    put_split(both, slice(None), terms[...])
    tall = hot.shape[0]

    def part(i):
        at = pl.ds(pl.multiple_of(i * tall, tall), tall)
        return pltpu.make_async_copy(out.at[at, :], kept.at[at, :], leave.at[i])

    def chunk(i, _):
        base = i * tall
        for k in range(groups):
            plus = one_hot(source[k : k + 1, :], tall, base)
            minus = one_hot(target[k : k + 1, :], tall, base)
            hot[:, k * LANES : (k + 1) * LANES] = (plus - minus).astype(jnp.bfloat16)
        out[pl.ds(pl.multiple_of(i * tall, tall), tall), :] = halves(
            jnp.dot(hot[...], both[...], preferred_element_type=jnp.float32)
        )
        part(i).start()
        return 0

    lax.fori_loop(0, rows // tall, chunk, 0)

    def total(ref):
        return factored(
            4,
            groups,
            lambda k: lax.shift_right_logical(ref[k : k + 1, :], 7),
            lambda k: ref[k : k + 1, :] & (LANES - 1),
            lambda k: weight[k : k + 1, :],
            rows // LANES,
        )

    degree[...] = total(source) + total(target)
    for i in range(rows // tall):
        part(i).wait()


def scatter_back(ret_both, listed, hots, emit, rows):
    tall = hots[0].shape[0]

    def build(i):
        to = hots[i % 2]
        for k in range(listed.shape[0]):
            to[:, k * LANES : (k + 1) * LANES] = one_hot(listed[k : k + 1, :], tall, i * tall).astype(jnp.bfloat16)

    build(0)
    for i in range(rows // tall):
        if (i + 1) * tall < rows:
            build(i + 1)
        emit(i, halves(jnp.dot(hots[i % 2][...], ret_both[...], preferred_element_type=jnp.float32)))


def side_join_kernel(lane, returned, listed, padded, own, own_degree, *refs):
    lanes = 4
    outs, (acc, ret_both, hot, other, landed, arrival, arrival_own) = refs[:lanes], refs[lanes:]
    come = pltpu.make_async_copy(returned, landed, arrival)
    come.start()
    mine = pltpu.make_async_copy(own, acc, arrival_own)
    mine.start()
    blocks = returned.shape[0]
    rows = own.shape[0]
    width = listed.shape[0] * LANES // blocks
    share = rows // lanes
    come.wait()
    for c in range(blocks):
        put_split(ret_both, slice(c * width, (c + 1) * width), landed[c, :width, :])

    def emit(i, got):
        at = slice(i * hot.shape[0], (i + 1) * hot.shape[0])
        acc[at, :] = acc[at, :] + got

    mine.wait()
    scatter_back(ret_both, listed, (hot, other), emit, rows)
    deg = own_degree[...] + factored(
        4,
        blocks,
        lambda k: lax.shift_right_arithmetic(padded[k : k + 1, :], 7),
        lambda k: padded[k : k + 1, :] & (LANES - 1),
        lambda k: landed[k, width : width + 1, :],
        rows // LANES,
    )
    deg_rows = share // LANES
    for s in range(lanes):
        q = lax.rem(lane[0] + s, lanes)
        outs[s][:share, :] = acc[pl.ds(pl.multiple_of(q * share, share), share), :]
        row = jnp.zeros((8, LANES), jnp.float32)
        place = lax.broadcasted_iota(jnp.int32, (8, LANES), 0)
        for p in range(lanes):
            for d in range(deg_rows):
                one = jnp.broadcast_to(deg[p * deg_rows + d : p * deg_rows + d + 1, :], (8, LANES))
                row = jnp.where((place == d) & (q == p), one, row)
        outs[s][share : share + 8, :] = row


def edge_code_kernel(
    rows, slots, room, count, lane, source, target, weight, far_code, spot, totals, mass, near_code, near_mass, gap_code, gap_slot
):
    groups = source.shape[0]
    per = groups // QUARTERS
    s, t = source[...], target[...]
    row = lax.broadcasted_iota(jnp.int32, s.shape, 0)
    number = row * LANES + lax.broadcasted_iota(jnp.int32, s.shape, 1)
    live = number < count[0]
    away = t >= rows
    load = jnp.where(live, weight[...], 0.0)
    mass[...] = load
    near_mass[...] = jnp.where(away, 0.0, load)
    near_code[...] = s | (jnp.where(away, 0, t) << 12)
    gap_code[...] = s | (jnp.minimum(t, rows) << 12)
    gap_slot[...] = jnp.where(away, t - rows, slots)
    far_code[...] = (jnp.where(away, t - rows, 0) << 21) | (s << 10) | (number & (per * LANES - 1))
    left = lax.broadcasted_iota(jnp.int32, (LANES, LANES), 0)
    right = lax.broadcasted_iota(jnp.int32, (LANES, LANES), 1)
    before = jnp.where(left < right, 1.0, 0.0).astype(jnp.bfloat16)
    ones = jnp.ones((LANES, LANES), jnp.bfloat16)
    down = lax.broadcasted_iota(jnp.int32, (groups, groups), 0)
    over = lax.broadcasted_iota(jnp.int32, (groups, groups), 1)
    same = lax.shift_right_logical(down, 3) == lax.shift_right_logical(over, 3)
    above = jnp.where(same & (over < down), 1.0, 0.0).astype(jnp.bfloat16)
    apart = (lax.shift_right_logical(s, 9) - lane[0]) & 3
    kinds = jnp.where(apart == 0, HOME, jnp.where(apart == 2, OPPOSITE, BESIDE))
    region = (lax.shift_right_logical(row, 3) & 1) * KINDS * room
    where = jnp.zeros_like(row) + 2 * KINDS * room
    for kind in range(KINDS):
        counted = away & live & (kinds == kind)
        flags = jnp.where(counted, 1.0, 0.0).astype(jnp.bfloat16)
        within = jnp.dot(flags, before, preferred_element_type=jnp.float32)
        total = jnp.dot(flags, ones, preferred_element_type=jnp.float32)
        base = jnp.dot(above, total.astype(jnp.bfloat16), preferred_element_type=jnp.float32)
        where = jnp.where(counted, region + kind * room + (within + base).astype(jnp.int32), where)
        through = (base + total).astype(jnp.int32)
        for c in range(QUARTERS):
            totals[kind * QUARTERS + c : kind * QUARTERS + c + 1, :] = through[(c + 1) * per - 1 : (c + 1) * per, :]
    spot[...] = where


def far_list_kernel(first, room, count, order, spot, totals, code):
    half = order.shape[0] // 2
    begin = first * order.shape[0] // QUARTERS

    def step(i, _):
        e = begin + i * 8
        given = [order[e + u] for u in range(8)]
        to = [spot[e + u] for u in range(8)]
        for u in range(8):
            code[to[u]] = given[u]
        return 0

    live = jnp.clip(count[0] - begin, 0, half)
    lax.fori_loop(0, lax.div(live + 7, 8), step, 0)
    nothing = jnp.int32(SPARE - 2048) << 21
    for c in range(2):
        for kind in range(KINDS):
            end = (KINDS * c + kind) * room + totals[kind * QUARTERS + first + c, 0]
            for u in range(UNROLL):
                code[end + u] = nothing


def trips(n):
    return lax.div(n + UNROLL - 1, UNROLL)


def clear(banks):
    for a in banks:
        a[...] = jnp.zeros_like(a)


def far_rows(kind, lists, totals, mass, take, give, banks):
    quarter = mass.shape[0] // QUARTERS
    many = len(banks)
    for h, code in enumerate(lists):
        room = (code.shape[0] - LANES) // (2 * KINDS)
        for c in range(2):
            start = (KINDS * c + kind) * room
            base = (2 * h + c) * quarter

            def step(i, _):
                for u in range(0, UNROLL, many):
                    at = start + i * UNROLL + u
                    given = [code[at + k] for k in range(many)]
                    rows = [take(given[k]) * mass[base + (given[k] & 1023)] for k in range(many)]
                    to = [pl.ds(give(given[k]), 1) for k in range(many)]
                    new = [banks[k][to[k], :] + rows[k] for k in range(many)]
                    for k in range(many):
                        banks[k][to[k], :] = new[k]
                return 0

            lax.fori_loop(0, trips(totals[kind * QUARTERS + 2 * h + c, 0]), step, 0)


def far_source(given):
    return lax.shift_right_logical(given, 10) & 2047


def far_slot(given):
    return lax.shift_right_logical(given, 21)


def source_of(given):
    return given & 4095


def target_of(given):
    return lax.shift_right_logical(given, 12)


def place(lane, lanes, shift, share, field):
    q = lax.rem(lane[0] - shift + lanes, lanes)
    rows = share.shape[0]
    field[pl.ds(pl.multiple_of(q * rows, rows), rows), :] = share[...]


def assemble(lane, lanes, shares, field):
    for s in range(lanes):
        place(lane, lanes, s, shares[s], field)


def pack(lists, field, out, width, part):
    per = out.shape[0] // PARTS

    def step(i, _):
        for c in range(per):
            for r in range(width):
                out[i * per + c, pl.ds(r, 1), :] = field[pl.ds(lists[(i * per + c) * width + r], 1), :]
        part(i).start()
        return 0

    lax.fori_loop(0, PARTS, step, 0)


def early_field_kernel(lanes, lane, code_a, code_b, totals, mass, home, opposite, out, field, *banks):
    place(lane, lanes, 0, home, field)
    place(lane, lanes, 2, opposite, field)
    clear(banks)
    for kind in (HOME, OPPOSITE):
        far_rows(
            kind,
            (code_a, code_b),
            totals,
            mass,
            lambda given: field[pl.ds(far_source(given), 1), :],
            far_slot,
            banks,
        )
    total = banks[0][...]
    for a in banks[1:]:
        total = total + a[...]
    out[...] = total


def field_kernel(lanes, lane, code_a, code_b, totals, mass, lists, early, *refs):
    shares, (kept, sent), refs = refs[:lanes], refs[lanes : lanes + 2], refs[lanes + 2 :]
    field, out, sums, leave_field, leave, leave_sums = refs[:6]
    banks = refs[6:]
    blocks, width, _ = out.shape
    assemble(lane, lanes, shares, field)
    keep = pltpu.make_async_copy(field, kept, leave_field)
    keep.start()
    banks[0][...] = early[...]
    clear(banks[1:])
    far_rows(
        BESIDE,
        (code_a, code_b),
        totals,
        mass,
        lambda given: field[pl.ds(far_source(given), 1), :],
        far_slot,
        banks,
    )
    for c in range(blocks):
        at = slice(c * width, (c + 1) * width)
        total = banks[0][at, :]
        for a in banks[1:]:
            total = total + a[at, :]
        sums[c] = total
    more = pltpu.make_async_copy(sums, sent.at[:, width:, :], leave_sums)
    more.start()
    per = blocks // PARTS

    def part(i):
        at = pl.ds(i * per, per)
        return pltpu.make_async_copy(out.at[at], sent.at[at, :width, :], leave.at[i])

    pack(lists, field, out, width, part)
    keep.wait()
    more.wait()
    for i in range(PARTS):
        part(i).wait()


def near_kernel(count, order, heavy, kept, out, field, come, *banks):
    bring = pltpu.make_async_copy(kept, field, come)
    bring.start()
    clear(banks)
    bring.wait()

    def step(i, _):
        for u in range(0, UNROLL, BANKS):
            at = i * UNROLL + u
            code = [order[at + k] for k in range(BANKS)]
            mass = [heavy[at + k] for k in range(BANKS)]
            one = [pl.ds(source_of(code[k]), 1) for k in range(BANKS)]
            two = [pl.ds(target_of(code[k]), 1) for k in range(BANKS)]
            from_one = [field[one[k], :] * mass[k] for k in range(BANKS)]
            from_two = [field[two[k], :] * mass[k] for k in range(BANKS)]
            new = [banks[k][one[k], :] + from_two[k] for k in range(BANKS)]
            for k in range(BANKS):
                banks[k][one[k], :] = new[k]
            new = [banks[k][two[k], :] + from_one[k] for k in range(BANKS)]
            for k in range(BANKS):
                banks[k][two[k], :] = new[k]
        return 0

    lax.fori_loop(0, trips(count[0]), step, 0)
    total = banks[0][...]
    for a in banks[1:]:
        total = total + a[...]
    out[...] = total


def listed_rows(q, share, listed, ret_both, hot):
    for k in range(listed.shape[0]):
        hot[:, k * LANES : (k + 1) * LANES] = one_hot(listed[k : k + 1, :], share, q * share).astype(jnp.bfloat16)
    return halves(jnp.dot(hot[...], ret_both[...], preferred_element_type=jnp.float32))


def late_join_kernel(lanes, lane, code_a, code_b, totals, mass, listed, near, arrived, *refs):
    out, halo, ret_both, hot, ret, come_halo, come_ret = refs[:7]
    banks = refs[7:]
    blocks, width, _ = ret.shape
    share = out.shape[0]
    first = pltpu.make_async_copy(arrived.at[:, :width, :], halo.at[:blocks], come_halo)
    second = pltpu.make_async_copy(arrived.at[:, width:, :], ret, come_ret)
    second.start()
    first.start()
    halo[blocks] = jnp.zeros((width, LANES), jnp.float32)
    clear(banks)
    q = lax.rem(lane[0] + 2, lanes)
    second.wait()
    for c in range(blocks):
        put_split(ret_both, slice(c * width, (c + 1) * width), ret[c])
    total = near[pl.ds(pl.multiple_of(q * share, share), share), :]
    out[...] = total + listed_rows(q, share, listed, ret_both, hot)
    first.wait()
    flat = halo.reshape((blocks + 1) * width, LANES)
    far_rows(
        OPPOSITE,
        (code_a, code_b),
        totals,
        mass,
        lambda given: flat[pl.ds(far_slot(given), 1), :],
        lambda given: far_source(given) & (share - 1),
        banks,
    )
    total = out[...]
    for a in banks:
        total = total + a[...]
    out[...] = total


def join_kernel(lanes, lane, code_a, code_b, totals, mass, listed, near, halo, ret_both, *refs):
    outs, hot, banks = refs[:2], refs[2], refs[3:]
    share = outs[0].shape[0]
    spots = []
    for s in (1, 3):
        q = lax.rem(lane[0] + s, lanes)
        at = pl.ds(pl.multiple_of(q * share, share), share)
        banks[0][at, :] = near[at, :]
        for a in banks[1:]:
            a[at, :] = jnp.zeros((share, LANES), jnp.float32)
        spots.append((q, at))
    flat = halo.reshape(halo.shape[0] * halo.shape[1], LANES)
    far_rows(
        BESIDE,
        (code_a, code_b),
        totals,
        mass,
        lambda given: flat[pl.ds(far_slot(given), 1), :],
        far_source,
        banks,
    )
    for (q, at), out in zip(spots, outs):
        total = banks[0][at, :]
        for a in banks[1:]:
            total = total + a[at, :]
        out[...] = total + listed_rows(q, share, listed, ret_both, hot)


def home_kernel(lane, code_a, code_b, totals, mass, listed, near, halo, ret_both, out, hot, *banks):
    share = out.shape[0]
    clear(banks)
    flat = halo.reshape(halo.shape[0] * halo.shape[1], LANES)
    far_rows(
        HOME,
        (code_a, code_b),
        totals,
        mass,
        lambda given: flat[pl.ds(far_slot(given), 1), :],
        lambda given: far_source(given) & (share - 1),
        banks,
    )
    total = near[pl.ds(pl.multiple_of(lane[0] * share, share), share), :]
    for a in banks:
        total = total + a[...]
    out[...] = total + listed_rows(lane[0], share, listed, ret_both, hot)


def solution_kernel(lane, lists, *refs):
    lanes = 4
    shares, (field, sent, out, leave) = refs[:lanes], refs[lanes:]
    assemble(lane, lanes, shares, field)
    per = out.shape[0] // PARTS

    def part(i):
        at = pl.ds(i * per, per)
        return pltpu.make_async_copy(out.at[at], sent.at[at], leave.at[i])

    pack(lists, field, out, out.shape[1], part)
    for i in range(PARTS):
        part(i).wait()


def near_gap_kernel(count, order, field, gaps, more):
    rows = field.shape[0]
    more[:rows, :] = field[...]
    more[rows:, :] = jnp.zeros((more.shape[0] - rows, LANES), jnp.float32)

    def step(i, _):
        for u in range(UNROLL):
            e = i * UNROLL + u
            code = order[e]
            gaps[pl.ds(e, 1), :] = (
                field[pl.ds(code & 4095, 1), :] - more[pl.ds(lax.shift_right_logical(code, 12), 1), :]
            )
        return 0

    lax.fori_loop(0, trips(count[0]), step, 0)


def far_gap_kernel(count, slot, gaps, arrived, live, out, halo, taken, come):
    blocks, width, _ = arrived.shape
    groups = live.shape[0]
    first = pltpu.make_async_copy(arrived, halo.at[:blocks], come)
    first.start()
    halo[blocks] = jnp.zeros((width, LANES), jnp.float32)
    first.wait()
    flat = halo.reshape((blocks + 1) * width, LANES)

    def gather(k):
        for u in range(LANES):
            e = k * LANES + u
            taken[pl.ds(e, 1), :] = flat[pl.ds(slot[e], 1), :]

    def finish(k):
        at = pl.ds(pl.multiple_of(k * LANES, LANES), LANES)
        gap = gaps[at, :] - taken[at, :]
        total = jnp.sum((gap * gap).T, axis=0, keepdims=True)
        alive = live[pl.ds(k, 1), :]
        out[pl.ds(k, 1), :] = jnp.where(alive > 0, total * (alive / LANES), 0.0)

    def step(k, _):
        finish(k - 1)
        gather(k)
        return 0

    out[...] = jnp.zeros((groups, LANES), jnp.float32)
    many = lax.div(count[0] + LANES - 1, LANES)
    gather(0)
    lax.fori_loop(1, many, step, 0)
    finish(many - 1)


def moved_by(x, shift, lanes):
    return lax.ppermute(x, "edg", [(i, (i + shift) % lanes) for i in range(lanes)])


def passed_round(blocks, lanes):
    return [blocks[0]] + [moved_by(blocks[s], s, lanes) for s in (2, 1, 3)]


def summed(blocks, lanes):
    home, two, one, three = passed_round(blocks, lanes)
    return (home + one) + (two + three)


def to_all(mine, lanes):
    home, two, one, three = passed_round([mine] * lanes, lanes)
    return [home, one, two, three]


def across(x):
    return lax.all_to_all(x, "vtx", split_axis=0, concat_axis=0, tiled=True)


def local(sketch_cols, edge_weight, ground, src_local, dst_index, send_rows, edge_count):
    blocks = lax.axis_size("vtx")
    lanes = lax.axis_size("edg")
    rows = ground.shape[0]
    edges = edge_weight.shape[0]
    width = send_rows.shape[2]
    slots = blocks * width
    share = rows // lanes
    groups = edges // LANES
    f32, i32, bf16 = jnp.float32, jnp.int32, jnp.bfloat16
    lane = lax.axis_index("edg").astype(i32).reshape(1)
    lists = send_rows[0].reshape(-1)
    listed = lists.reshape(slots // LANES, LANES)
    padded = jnp.pad(send_rows[0], ((0, 0), (0, LANES - width)), constant_values=-1)
    live = (jnp.arange(edges, dtype=i32) < edge_count[0]).astype(f32)
    weight = edge_weight * live
    root = jnp.sqrt(edge_weight) * live
    terms = root[:, None] * sketch_cols.astype(f32)
    live_rows = live.reshape(groups, LANES)
    weight_rows = weight.reshape(groups, LANES)
    source_rows = src_local.reshape(groups, LANES)
    target_rows = dst_index.reshape(groups, LANES)

    outgoing = call(
        functools.partial(halo_side_kernel, rows, slots, width),
        [((blocks, width + 8, LANES), f32, HBM)],
        [VMEM] * 3,
        [pltpu.VMEM((edges, 2 * LANES), bf16)]
        + [pltpu.VMEM((8 * width, edges), bf16)] * 2
        + [pltpu.VMEM((blocks, width + 8, LANES), f32), pltpu.SemaphoreType.DMA((slots // (8 * width),))],
        "halo_side",
        flops=2 * slots * edges * 2 * LANES,
    )(terms, target_rows, weight_rows)[0]
    returned = across(outgoing)
    own, own_degree = call(
        own_side_kernel,
        [((rows, LANES), f32, HBM), ((rows // LANES, LANES), f32, VMEM)],
        [VMEM] * 4,
        [pltpu.VMEM((edges, 2 * LANES), bf16), pltpu.VMEM((256, edges), bf16)]
        + [pltpu.VMEM((rows, LANES), f32), pltpu.SemaphoreType.DMA((rows // 256,))],
        "own_side",
        flops=2 * rows * edges * 2 * LANES,
    )(terms, source_rows, target_rows, weight_rows)
    sides = call(
        side_join_kernel,
        [((share + 8, LANES), f32, VMEM)] * lanes,
        [SMEM, HBM, VMEM, VMEM, HBM, VMEM],
        [pltpu.VMEM((rows, LANES), f32), pltpu.VMEM((slots, 2 * LANES), bf16)]
        + [pltpu.VMEM((256, slots), bf16)] * 2
        + [pltpu.VMEM((blocks, width + 8, LANES), f32)]
        + [pltpu.SemaphoreType.DMA] * 2,
        "side_join",
        flops=2 * rows * slots * 2 * LANES,
    )(lane, returned, listed, padded, own, own_degree)
    late = lax.optimization_barrier((edge_count, source_rows, target_rows, edge_weight, *sides))
    begin, source_late, target_late, weight_late, *sides = late
    quarter = edges // QUARTERS
    room = quarter + LANES // 2
    per_edge = ((groups, LANES), i32, VMEM)
    per_edge_f32 = ((groups, LANES), f32, VMEM)
    coded = list(call(
        functools.partial(edge_code_kernel, rows, slots, room),
        [per_edge, per_edge, ((4 * QUARTERS, LANES), i32, VMEM), per_edge_f32, per_edge, per_edge_f32, per_edge, per_edge],
        [SMEM] * 2 + [VMEM] * 3,
        [],
        "edge_code",
    )(begin, lane, source_late, target_late, weight_late.reshape(groups, LANES)))
    totals = coded.pop(2)
    far_order, spot, mass, near_order, near_weight, gap_order, gap_slot = (x.reshape(edges) for x in coded)

    def far_list(first, count):
        return call(
            functools.partial(far_list_kernel, first, room),
            [((2 * KINDS * room + LANES,), i32, SMEM)],
            [SMEM] * 4,
            [],
            "far_list",
            moved=2**25,
        )(count, far_order, spot, totals)[0]

    code_a = far_list(0, begin)
    side = summed(sides, lanes)
    side, code_a = lax.optimization_barrier((side, code_a))
    later, side = lax.optimization_barrier((begin, side))
    code_b = far_list(2, later)
    far = (code_a, code_b, totals, mass)
    right_share = side[:share]
    degree_share = side[share : share + share // LANES].reshape(share)
    ground_share = lax.dynamic_slice_in_dim(ground, lane[0] * share, share)
    diagonal = (degree_share + ground_share)[:, None]
    inverse = 1.0 / diagonal

    first, pairs = chebyshev_terms(ITERS)
    residual = right_share
    direction = first * inverse * right_share
    solution_share = direction
    for keep, push in pairs:
        shares = to_all(direction, lanes)
        early = call(
            functools.partial(early_field_kernel, lanes),
            [((slots + 8, LANES), f32, VMEM)],
            [SMEM] * 5 + [VMEM] * 2,
            [pltpu.VMEM((rows, LANES), f32)] + [pltpu.VMEM((slots + 8, LANES), f32)] * BANKS,
            "early_field",
            moved=2**25,
        )(lane, *far, shares[0], shares[2])[0]
        field, message = call(
            functools.partial(field_kernel, lanes),
            [((rows, LANES), f32, HBM), ((blocks, 2 * width, LANES), f32, HBM)],
            [SMEM] * 6 + [VMEM] * (1 + lanes),
            [pltpu.VMEM((rows, LANES), f32)]
            + [pltpu.VMEM((blocks, width, LANES), f32)] * 2
            + [pltpu.SemaphoreType.DMA, pltpu.SemaphoreType.DMA((PARTS,)), pltpu.SemaphoreType.DMA]
            + [pltpu.VMEM((slots + 8, LANES), f32)] * BANKS,
            "field",
        )(lane, *far, lists, early, *shares)
        arrived = across(message)
        near = call(
            near_kernel,
            [((rows, LANES), f32, VMEM)],
            [SMEM] * 3 + [HBM],
            [pltpu.VMEM((rows, LANES), f32), pltpu.SemaphoreType.DMA] + [pltpu.VMEM((rows, LANES), f32)] * BANKS,
            "near",
            moved=2**25,
        )(edge_count, near_order, near_weight, field)[0]
        two, halo, ret_both = call(
            functools.partial(late_join_kernel, lanes),
            [((share, LANES), f32, VMEM), ((blocks + 1, width, LANES), f32, VMEM), ((slots, 2 * LANES), bf16, VMEM)],
            [SMEM] * 5 + [VMEM, VMEM, HBM],
            [pltpu.VMEM((share, slots), bf16), pltpu.VMEM((blocks, width, LANES), f32)]
            + [pltpu.SemaphoreType.DMA] * 2
            + [pltpu.VMEM((share, LANES), f32)] * BANKS,
            "late_join",
        )(lane, *far, listed, near, arrived)
        one, three = call(
            functools.partial(join_kernel, lanes),
            [((share, LANES), f32, VMEM)] * 2,
            [SMEM] * 5 + [VMEM] * 4,
            [pltpu.VMEM((share, slots), bf16)] + [pltpu.VMEM((rows, LANES), f32)] * BANKS,
            "join",
            moved=2**25,
        )(lane, *far, listed, near, halo, ret_both)
        home = call(
            home_kernel,
            [((share, LANES), f32, VMEM)],
            [SMEM] * 5 + [VMEM] * 4,
            [pltpu.VMEM((share, slots), bf16)] + [pltpu.VMEM((share, LANES), f32)] * BANKS,
            "home",
            moved=2**25,
        )(lane, *far, listed, near, halo, ret_both)[0]
        two = moved_by(two, 2, lanes)
        two, one, three = lax.optimization_barrier((two, one, three))
        flows = (home + two) + (moved_by(one, 1, lanes) + moved_by(three, 3, lanes))
        residual = residual - (diagonal * direction - flows)
        direction = keep * direction + push * inverse * residual
        solution_share = solution_share + direction
    field, message = call(
        solution_kernel,
        [((rows, LANES), f32, VMEM), ((blocks, width, LANES), f32, HBM)],
        [SMEM] * 2 + [VMEM] * lanes,
        [pltpu.VMEM((blocks, width, LANES), f32), pltpu.SemaphoreType.DMA((PARTS,))],
        "solution_rows",
    )(lane, lists, *to_all(solution_share, lanes))
    halo = across(message)
    gaps = call(
        near_gap_kernel,
        [((edges, LANES), f32, VMEM)],
        [SMEM] * 2 + [VMEM],
        [pltpu.VMEM((rows + 8, LANES), f32)],
        "near_gap",
        moved=2**25,
    )(edge_count, gap_order, field)[0]
    resistance = call(
        far_gap_kernel,
        [((groups, LANES), f32, VMEM)],
        [SMEM] * 2 + [VMEM, HBM, VMEM],
        [pltpu.VMEM((blocks + 1, width, LANES), f32), pltpu.VMEM((edges, LANES), f32), pltpu.SemaphoreType.DMA],
        "far_gap",
    )(edge_count, gap_slot, gaps, halo, live_rows)[0]
    return (field, resistance.reshape(edges))


def solution(mesh):
    in_specs = (
        P(("vtx", "edg"), None),
        P(("vtx", "edg")),
        P("vtx"),
        P(("vtx", "edg")),
        P(("vtx", "edg")),
        P(("vtx", "edg"), None, None),
        P(("vtx", "edg")),
    )
    out_specs = (P("vtx", None), P(("vtx", "edg")))
    return jax.shard_map(local, mesh=mesh, in_specs=in_specs, out_specs=out_specs, check_vma=False)
```

```python
import functools

import jax
import jax.numpy as jnp
from jax import lax
from jax.experimental import pallas as pl
from jax.experimental.pallas import tpu as pltpu
from jax.sharding import PartitionSpec as P

ITERS = 3
LANES = 128
UNROLL = 16
BANKS = 4
QUARTERS = 4
SPARE = 1536
BESIDE, OPPOSITE, HOME = range(3)
KINDS = 3
PARTS = 8
ROOMY = 32

lam_low = 0.05
lam_high = 2.0

SMEM = pl.BlockSpec(memory_space=pltpu.SMEM)
VMEM = pl.BlockSpec(memory_space=pltpu.VMEM)
HBM = pl.BlockSpec(memory_space=pltpu.HBM)
LIMIT = 24 * 2**20


def chebyshev_terms(steps):
    centre = (lam_high + lam_low) / 2.0
    half_width = (lam_high - lam_low) / 2.0
    sigma_val = centre / half_width
    rho_prev = 1.0 / sigma_val
    pairs = []
    for count_idx in range(steps - 1):
        rho_next = 1.0 / (2.0 * sigma_val - rho_prev)
        pairs.append((rho_next * rho_prev, 2.0 * rho_next / half_width))
        rho_prev = rho_next
    return (1.0 / centre, pairs)


def call(kernel, outs, ins, scratch, name, flops=0, moved=2**22):
    return pl.pallas_call(
        kernel,
        out_shape=[
            pltpu.HBM(shape, dtype) if space is HBM else jax.ShapeDtypeStruct(shape, dtype) for shape, dtype, space in outs
        ],
        in_specs=ins,
        out_specs=[space for _, _, space in outs],
        scratch_shapes=scratch,
        compiler_params=pltpu.CompilerParams(vmem_limit_bytes=LIMIT),
        cost_estimate=pl.CostEstimate(flops=flops, bytes_accessed=moved, transcendentals=0),
        name=name,
    )


def split(x):
    high = x.astype(jnp.bfloat16)
    return high, (x - high.astype(jnp.float32)).astype(jnp.bfloat16)


def put_split(ref, rows, x):
    high, low = split(x)
    ref[rows, :LANES] = high
    ref[rows, LANES:] = low


def halves(x):
    return x[:, :LANES] + x[:, LANES:]


def one_hot(row, height, base):
    place = lax.broadcasted_iota(jnp.int32, (height, row.shape[1]), 0) + base
    return jnp.where(place == row, 1.0, 0.0)


def factored(pick, groups, high_of, low_of, weight_of, height):
    total = jnp.zeros((2 * height, LANES), jnp.float32)
    for k0 in range(0, groups, pick):
        left, right = [], []
        for k in range(k0, k0 + pick):
            member = one_hot(high_of(k), height, 0) * weight_of(k)
            high, low = split(member)
            left.append(jnp.concatenate([high, low], axis=0))
            right.append(one_hot(low_of(k), LANES, 0).astype(jnp.bfloat16))
        total = total + lax.dot_general(
            jnp.concatenate(left, axis=1),
            jnp.concatenate(right, axis=1),
            (((1,), (1,)), ((), ())),
            preferred_element_type=jnp.float32,
        )
    return total[:height] + total[height:]


def halo_side_kernel(rows, slots, width, terms, target, weight, sent, both, hot, out, leave):
    groups = target.shape[0]
    tall = hot.shape[0]
    per = tall // width
    blocks = slots // width
    chunks = slots // tall

    def slot(k):
        return target[k : k + 1, :] - rows

    def block_of(k):
        return jnp.where(slot(k) < 0, -1, lax.shift_right_arithmetic(slot(k) * 1366, 16))

    def within(k):
        return slot(k) - block_of(k) * width

    deg = factored(4, groups, block_of, within, lambda k: weight[k : k + 1, :], blocks)
    for c in range(blocks):
        out[c, width : width + 8, :] = jnp.broadcast_to(deg[c : c + 1, :], (8, LANES))
    put_split(both, slice(None), terms[...])

    def part(i):
        at = pl.ds(i * per, per)
        return pltpu.make_async_copy(out.at[at], sent.at[at], leave.at[i])

    def chunk(i, _):
        base = rows + i * tall
        for k in range(groups):
            hot[:, k * LANES : (k + 1) * LANES] = one_hot(target[k : k + 1, :], tall, base).astype(jnp.bfloat16)
        got = halves(jnp.dot(hot[...], both[...], preferred_element_type=jnp.float32))
        for c in range(per):
            out[i * per + c, :width, :] = -got[c * width : (c + 1) * width]
        part(i).start()
        return 0

    lax.fori_loop(0, chunks, chunk, 0)
    for i in range(chunks):
        part(i).wait()


def own_side_kernel(terms, source, target, weight, kept, degree, both, hot, out, leave):
    groups = target.shape[0]
    rows = out.shape[0]
    put_split(both, slice(None), terms[...])
    tall = hot.shape[0]

    def part(i):
        at = pl.ds(pl.multiple_of(i * tall, tall), tall)
        return pltpu.make_async_copy(out.at[at, :], kept.at[0, at, :], leave.at[i])

    def chunk(i, _):
        base = i * tall
        for k in range(groups):
            plus = one_hot(source[k : k + 1, :], tall, base)
            minus = one_hot(target[k : k + 1, :], tall, base)
            hot[:, k * LANES : (k + 1) * LANES] = (plus - minus).astype(jnp.bfloat16)
        out[pl.ds(pl.multiple_of(i * tall, tall), tall), :] = halves(
            jnp.dot(hot[...], both[...], preferred_element_type=jnp.float32)
        )
        part(i).start()
        return 0

    lax.fori_loop(0, rows // tall, chunk, 0)

    def total(ref):
        return factored(
            4,
            groups,
            lambda k: lax.shift_right_logical(ref[k : k + 1, :], 7),
            lambda k: ref[k : k + 1, :] & (LANES - 1),
            lambda k: weight[k : k + 1, :],
            rows // LANES,
        )

    degree[...] = total(source) + total(target)
    for i in range(rows // tall):
        part(i).wait()


def scatter_back(ret_both, listed, hots, emit, rows):
    tall = hots[0].shape[0]

    def build(i):
        to = hots[i % 2]
        for k in range(listed.shape[0]):
            to[:, k * LANES : (k + 1) * LANES] = one_hot(listed[k : k + 1, :], tall, i * tall).astype(jnp.bfloat16)

    build(0)
    for i in range(rows // tall):
        if (i + 1) * tall < rows:
            build(i + 1)
        emit(i, halves(jnp.dot(hots[i % 2][...], ret_both[...], preferred_element_type=jnp.float32)))


def side_join_kernel(lane, returned, listed, padded, own, own_degree, *refs):
    lanes = 4
    outs, (acc, ret_both, hot, other, landed, arrival, arrival_own) = refs[:lanes], refs[lanes:]
    come = pltpu.make_async_copy(returned, landed, arrival)
    come.start()
    mine = pltpu.make_async_copy(own.at[0], acc, arrival_own)
    mine.start()
    blocks = returned.shape[0]
    rows = own.shape[1]
    width = listed.shape[0] * LANES // blocks
    share = rows // lanes
    come.wait()
    for c in range(blocks):
        put_split(ret_both, slice(c * width, (c + 1) * width), landed[c, :width, :])

    def emit(i, got):
        at = slice(i * hot.shape[0], (i + 1) * hot.shape[0])
        acc[at, :] = acc[at, :] + got

    mine.wait()
    scatter_back(ret_both, listed, (hot, other), emit, rows)
    deg = own_degree[...] + factored(
        4,
        blocks,
        lambda k: lax.shift_right_arithmetic(padded[k : k + 1, :], 7),
        lambda k: padded[k : k + 1, :] & (LANES - 1),
        lambda k: landed[k, width : width + 1, :],
        rows // LANES,
    )
    deg_rows = share // LANES
    for s in range(lanes):
        q = lax.rem(lane[0] + s, lanes)
        outs[s][:share, :] = acc[pl.ds(pl.multiple_of(q * share, share), share), :]
        row = jnp.zeros((8, LANES), jnp.float32)
        place = lax.broadcasted_iota(jnp.int32, (8, LANES), 0)
        for p in range(lanes):
            for d in range(deg_rows):
                one = jnp.broadcast_to(deg[p * deg_rows + d : p * deg_rows + d + 1, :], (8, LANES))
                row = jnp.where((place == d) & (q == p), one, row)
        outs[s][share : share + 8, :] = row


def edge_code_kernel(
    rows, slots, room, count, lane, source, target, weight, far_code, spot, totals, mass, near_code, near_mass, gap_code, gap_slot
):
    groups = source.shape[0]
    per = groups // QUARTERS
    s, t = source[...], target[...]
    row = lax.broadcasted_iota(jnp.int32, s.shape, 0)
    number = row * LANES + lax.broadcasted_iota(jnp.int32, s.shape, 1)
    live = number < count[0]
    away = t >= rows
    load = jnp.where(live, weight[...], 0.0)
    mass[...] = load
    near_mass[...] = jnp.where(away, 0.0, load)
    near_code[...] = s | (jnp.where(away, 0, t) << 12)
    gap_code[...] = s | (jnp.minimum(t, rows) << 12)
    gap_slot[...] = jnp.where(away, t - rows, slots)
    far_code[...] = (jnp.where(away, t - rows, 0) << 21) | (s << 10) | (number & (per * LANES - 1))
    left = lax.broadcasted_iota(jnp.int32, (LANES, LANES), 0)
    right = lax.broadcasted_iota(jnp.int32, (LANES, LANES), 1)
    before = jnp.where(left < right, 1.0, 0.0).astype(jnp.bfloat16)
    ones = jnp.ones((LANES, LANES), jnp.bfloat16)
    down = lax.broadcasted_iota(jnp.int32, (groups, groups), 0)
    over = lax.broadcasted_iota(jnp.int32, (groups, groups), 1)
    same = lax.shift_right_logical(down, 3) == lax.shift_right_logical(over, 3)
    above = jnp.where(same & (over < down), 1.0, 0.0).astype(jnp.bfloat16)
    apart = (lax.shift_right_logical(s, 9) - lane[0]) & 3
    kinds = jnp.where(apart == 0, HOME, jnp.where(apart == 2, OPPOSITE, BESIDE))
    region = (lax.shift_right_logical(row, 3) & 1) * KINDS * room
    where = jnp.zeros_like(row) + 2 * KINDS * room
    for kind in range(KINDS):
        counted = away & live & (kinds == kind)
        flags = jnp.where(counted, 1.0, 0.0).astype(jnp.bfloat16)
        within = jnp.dot(flags, before, preferred_element_type=jnp.float32)
        total = jnp.dot(flags, ones, preferred_element_type=jnp.float32)
        base = jnp.dot(above, total.astype(jnp.bfloat16), preferred_element_type=jnp.float32)
        where = jnp.where(counted, region + kind * room + (within + base).astype(jnp.int32), where)
        through = (base + total).astype(jnp.int32)
        for c in range(QUARTERS):
            totals[kind * QUARTERS + c : kind * QUARTERS + c + 1, :] = through[(c + 1) * per - 1 : (c + 1) * per, :]
    spot[...] = where


def far_list_kernel(first, room, count, order, spot, totals, code):
    half = order.shape[0] // 2
    begin = first * order.shape[0] // QUARTERS

    def step(i, _):
        e = begin + i * 8
        given = [order[e + u] for u in range(8)]
        to = [spot[e + u] for u in range(8)]
        for u in range(8):
            code[to[u]] = given[u]
        return 0

    live = jnp.clip(count[0] - begin, 0, half)
    lax.fori_loop(0, lax.div(live + 7, 8), step, 0)
    nothing = jnp.int32(SPARE - 2048) << 21
    for c in range(2):
        for kind in range(KINDS):
            end = (KINDS * c + kind) * room + totals[kind * QUARTERS + first + c, 0]
            for u in range(UNROLL):
                code[end + u] = nothing


def trips(n):
    return lax.div(n + UNROLL - 1, UNROLL)


def clear(banks):
    for a in banks:
        a[...] = jnp.zeros_like(a)


def far_rows(kind, lists, totals, mass, take, give, banks):
    quarter = mass.shape[0] // QUARTERS
    many = len(banks)
    for h, code in enumerate(lists):
        room = (code.shape[0] - LANES) // (2 * KINDS)
        for c in range(2):
            start = (KINDS * c + kind) * room
            base = (2 * h + c) * quarter

            def step(i, _):
                for u in range(0, UNROLL, many):
                    at = start + i * UNROLL + u
                    given = [code[at + k] for k in range(many)]
                    rows = [take(given[k]) * mass[base + (given[k] & 1023)] for k in range(many)]
                    to = [pl.ds(give(given[k]), 1) for k in range(many)]
                    new = [banks[k][to[k], :] + rows[k] for k in range(many)]
                    for k in range(many):
                        banks[k][to[k], :] = new[k]
                return 0

            lax.fori_loop(0, trips(totals[kind * QUARTERS + 2 * h + c, 0]), step, 0)


def far_source(given):
    return lax.shift_right_logical(given, 10) & 2047


def far_slot(given):
    return lax.shift_right_logical(given, 21)


def source_of(given):
    return given & 4095


def target_of(given):
    return lax.shift_right_logical(given, 12)


def place(lane, lanes, shift, share, field):
    q = lax.rem(lane[0] - shift + lanes, lanes)
    rows = share.shape[0]
    field[pl.ds(pl.multiple_of(q * rows, rows), rows), :] = share[...]


def assemble(lane, lanes, shares, field):
    for s in range(lanes):
        place(lane, lanes, s, shares[s], field)


def pack(lists, field, out, width, part):
    per = out.shape[0] // PARTS

    def step(i, _):
        for c in range(per):
            for r in range(width):
                out[i * per + c, pl.ds(r, 1), :] = field[pl.ds(lists[(i * per + c) * width + r], 1), :]
        part(i).start()
        return 0

    lax.fori_loop(0, PARTS, step, 0)


def early_field_kernel(lanes, lane, code_a, code_b, totals, mass, home, opposite, out, field, *banks):
    place(lane, lanes, 0, home, field)
    place(lane, lanes, 2, opposite, field)
    clear(banks)
    for kind in (HOME, OPPOSITE):
        far_rows(
            kind,
            (code_a, code_b),
            totals,
            mass,
            lambda given: field[pl.ds(far_source(given), 1), :],
            far_slot,
            banks,
        )
    total = banks[0][...]
    for a in banks[1:]:
        total = total + a[...]
    out[...] = total


def field_kernel(lanes, lane, code_a, code_b, totals, mass, lists, early, *refs):
    shares, (kept, sent), refs = refs[:lanes], refs[lanes : lanes + 2], refs[lanes + 2 :]
    field, out, sums, leave_field, leave, leave_sums = refs[:6]
    banks = refs[6:]
    blocks, width, _ = out.shape
    assemble(lane, lanes, shares, field)
    keep = pltpu.make_async_copy(field, kept, leave_field)
    keep.start()
    banks[0][...] = early[...]
    clear(banks[1:])
    far_rows(
        BESIDE,
        (code_a, code_b),
        totals,
        mass,
        lambda given: field[pl.ds(far_source(given), 1), :],
        far_slot,
        banks,
    )
    for c in range(blocks):
        at = slice(c * width, (c + 1) * width)
        total = banks[0][at, :]
        for a in banks[1:]:
            total = total + a[at, :]
        sums[c] = total
    more = pltpu.make_async_copy(sums, sent.at[:, width:, :], leave_sums)
    more.start()
    per = blocks // PARTS

    def part(i):
        at = pl.ds(i * per, per)
        return pltpu.make_async_copy(out.at[at], sent.at[at, :width, :], leave.at[i])

    pack(lists, field, out, width, part)
    keep.wait()
    more.wait()
    for i in range(PARTS):
        part(i).wait()


def near_kernel(count, order, heavy, kept, out, field, come, *banks):
    bring = pltpu.make_async_copy(kept, field, come)
    bring.start()
    clear(banks)
    bring.wait()

    def step(i, _):
        for u in range(0, UNROLL, BANKS):
            at = i * UNROLL + u
            code = [order[at + k] for k in range(BANKS)]
            mass = [heavy[at + k] for k in range(BANKS)]
            one = [pl.ds(source_of(code[k]), 1) for k in range(BANKS)]
            two = [pl.ds(target_of(code[k]), 1) for k in range(BANKS)]
            from_one = [field[one[k], :] * mass[k] for k in range(BANKS)]
            from_two = [field[two[k], :] * mass[k] for k in range(BANKS)]
            new = [banks[k][one[k], :] + from_two[k] for k in range(BANKS)]
            for k in range(BANKS):
                banks[k][one[k], :] = new[k]
            new = [banks[k][two[k], :] + from_one[k] for k in range(BANKS)]
            for k in range(BANKS):
                banks[k][two[k], :] = new[k]
        return 0

    lax.fori_loop(0, trips(count[0]), step, 0)
    total = banks[0][...]
    for a in banks[1:]:
        total = total + a[...]
    out[...] = total


def listed_rows(q, share, listed, ret_both, hot):
    for k in range(listed.shape[0]):
        hot[:, k * LANES : (k + 1) * LANES] = one_hot(listed[k : k + 1, :], share, q * share).astype(jnp.bfloat16)
    return halves(jnp.dot(hot[...], ret_both[...], preferred_element_type=jnp.float32))


def late_join_kernel(lanes, lane, code_a, code_b, totals, mass, listed, near, arrived, *refs):
    out, halo, ret_both, hot, ret, come_halo, come_ret = refs[:7]
    banks = refs[7:]
    blocks, width, _ = ret.shape
    share = out.shape[0]
    first = pltpu.make_async_copy(arrived.at[:, :width, :], halo.at[:blocks], come_halo)
    second = pltpu.make_async_copy(arrived.at[:, width:, :], ret, come_ret)
    second.start()
    first.start()
    halo[blocks] = jnp.zeros((width, LANES), jnp.float32)
    clear(banks)
    q = lax.rem(lane[0] + 2, lanes)
    second.wait()
    for c in range(blocks):
        put_split(ret_both, slice(c * width, (c + 1) * width), ret[c])
    total = near[pl.ds(pl.multiple_of(q * share, share), share), :]
    out[...] = total + listed_rows(q, share, listed, ret_both, hot)
    first.wait()
    flat = halo.reshape((blocks + 1) * width, LANES)
    far_rows(
        OPPOSITE,
        (code_a, code_b),
        totals,
        mass,
        lambda given: flat[pl.ds(far_slot(given), 1), :],
        lambda given: far_source(given) & (share - 1),
        banks,
    )
    total = out[...]
    for a in banks:
        total = total + a[...]
    out[...] = total


def join_kernel(lanes, lane, code_a, code_b, totals, mass, listed, near, halo, ret_both, *refs):
    outs, hot, banks = refs[:2], refs[2], refs[3:]
    share = outs[0].shape[0]
    spots = []
    for s in (1, 3):
        q = lax.rem(lane[0] + s, lanes)
        at = pl.ds(pl.multiple_of(q * share, share), share)
        banks[0][at, :] = near[at, :]
        for a in banks[1:]:
            a[at, :] = jnp.zeros((share, LANES), jnp.float32)
        spots.append((q, at))
    flat = halo.reshape(halo.shape[0] * halo.shape[1], LANES)
    far_rows(
        BESIDE,
        (code_a, code_b),
        totals,
        mass,
        lambda given: flat[pl.ds(far_slot(given), 1), :],
        far_source,
        banks,
    )
    for (q, at), out in zip(spots, outs):
        total = banks[0][at, :]
        for a in banks[1:]:
            total = total + a[at, :]
        out[...] = total + listed_rows(q, share, listed, ret_both, hot)


def home_kernel(lane, code_a, code_b, totals, mass, listed, near, halo, ret_both, out, hot, *banks):
    share = out.shape[0]
    clear(banks)
    flat = halo.reshape(halo.shape[0] * halo.shape[1], LANES)
    far_rows(
        HOME,
        (code_a, code_b),
        totals,
        mass,
        lambda given: flat[pl.ds(far_slot(given), 1), :],
        lambda given: far_source(given) & (share - 1),
        banks,
    )
    total = near[pl.ds(pl.multiple_of(lane[0] * share, share), share), :]
    for a in banks:
        total = total + a[...]
    out[...] = total + listed_rows(lane[0], share, listed, ret_both, hot)


def solution_kernel(lane, lists, *refs):
    lanes = 4
    shares, (field, sent, out, leave) = refs[:lanes], refs[lanes:]
    assemble(lane, lanes, shares, field)
    per = out.shape[0] // PARTS

    def part(i):
        at = pl.ds(i * per, per)
        return pltpu.make_async_copy(out.at[at], sent.at[at], leave.at[i])

    pack(lists, field, out, out.shape[1], part)
    for i in range(PARTS):
        part(i).wait()


def near_gap_kernel(count, order, field, gaps, more):
    rows = field.shape[0]
    more[:rows, :] = field[...]
    more[rows:, :] = jnp.zeros((more.shape[0] - rows, LANES), jnp.float32)

    def step(i, _):
        for u in range(UNROLL):
            e = i * UNROLL + u
            code = order[e]
            gaps[pl.ds(e, 1), :] = (
                field[pl.ds(code & 4095, 1), :] - more[pl.ds(lax.shift_right_logical(code, 12), 1), :]
            )
        return 0

    lax.fori_loop(0, trips(count[0]), step, 0)


def far_gap_kernel(count, slot, gaps, arrived, live, out, halo, taken, come):
    blocks, width, _ = arrived.shape
    groups = live.shape[0]
    first = pltpu.make_async_copy(arrived, halo.at[:blocks], come)
    first.start()
    halo[blocks] = jnp.zeros((width, LANES), jnp.float32)
    first.wait()
    flat = halo.reshape((blocks + 1) * width, LANES)

    def gather(k):
        for u in range(LANES):
            e = k * LANES + u
            taken[pl.ds(e, 1), :] = flat[pl.ds(slot[e], 1), :]

    def finish(k):
        at = pl.ds(pl.multiple_of(k * LANES, LANES), LANES)
        gap = gaps[at, :] - taken[at, :]
        total = jnp.sum((gap * gap).T, axis=0, keepdims=True)
        alive = live[pl.ds(k, 1), :]
        out[pl.ds(k, 1), :] = jnp.where(alive > 0, total * (alive / LANES), 0.0)

    def step(k, _):
        finish(k - 1)
        gather(k)
        return 0

    out[...] = jnp.zeros((groups, LANES), jnp.float32)
    many = lax.div(count[0] + LANES - 1, LANES)
    gather(0)
    lax.fori_loop(1, many, step, 0)
    finish(many - 1)


def moved_by(x, shift, lanes):
    return lax.ppermute(x, "edg", [(i, (i + shift) % lanes) for i in range(lanes)])


def passed_round(blocks, lanes):
    return [blocks[0]] + [moved_by(blocks[s], s, lanes) for s in (2, 1, 3)]


def summed(blocks, lanes):
    home, two, one, three = passed_round(blocks, lanes)
    return (home + one) + (two + three)


def to_all(mine, lanes):
    home, two, one, three = passed_round([mine] * lanes, lanes)
    return [home, one, two, three]


def across(x):
    return lax.all_to_all(x, "vtx", split_axis=0, concat_axis=0, tiled=True)


def local(sketch_cols, edge_weight, ground, src_local, dst_index, send_rows, edge_count):
    blocks = lax.axis_size("vtx")
    lanes = lax.axis_size("edg")
    rows = ground.shape[0]
    edges = edge_weight.shape[0]
    width = send_rows.shape[2]
    slots = blocks * width
    share = rows // lanes
    groups = edges // LANES
    f32, i32, bf16 = jnp.float32, jnp.int32, jnp.bfloat16
    lane = lax.axis_index("edg").astype(i32).reshape(1)
    lists = send_rows[0].reshape(-1)
    listed = lists.reshape(slots // LANES, LANES)
    padded = jnp.pad(send_rows[0], ((0, 0), (0, LANES - width)), constant_values=-1)
    live = (jnp.arange(edges, dtype=i32) < edge_count[0]).astype(f32)
    weight = edge_weight * live
    root = jnp.sqrt(edge_weight) * live
    terms = root[:, None] * sketch_cols.astype(f32)
    live_rows = live.reshape(groups, LANES)
    weight_rows = weight.reshape(groups, LANES)
    source_rows = src_local.reshape(groups, LANES)
    target_rows = dst_index.reshape(groups, LANES)

    outgoing = call(
        functools.partial(halo_side_kernel, rows, slots, width),
        [((blocks, width + 8, LANES), f32, HBM)],
        [VMEM] * 3,
        [pltpu.VMEM((edges, 2 * LANES), bf16), pltpu.VMEM((8 * width, edges), bf16)]
        + [pltpu.VMEM((blocks, width + 8, LANES), f32), pltpu.SemaphoreType.DMA((slots // (8 * width),))],
        "halo_side",
        flops=2 * slots * edges * 2 * LANES,
    )(terms, target_rows, weight_rows)[0]
    returned = across(outgoing)
    own, own_degree = call(
        own_side_kernel,
        [((ROOMY, rows, LANES), f32, HBM), ((rows // LANES, LANES), f32, VMEM)],
        [VMEM] * 4,
        [pltpu.VMEM((edges, 2 * LANES), bf16), pltpu.VMEM((256, edges), bf16)]
        + [pltpu.VMEM((rows, LANES), f32), pltpu.SemaphoreType.DMA((rows // 256,))],
        "own_side",
        flops=2 * rows * edges * 2 * LANES,
    )(terms, source_rows, target_rows, weight_rows)
    sides = call(
        side_join_kernel,
        [((share + 8, LANES), f32, VMEM)] * lanes,
        [SMEM, HBM, VMEM, VMEM, HBM, VMEM],
        [pltpu.VMEM((rows, LANES), f32), pltpu.VMEM((slots, 2 * LANES), bf16)]
        + [pltpu.VMEM((256, slots), bf16)] * 2
        + [pltpu.VMEM((blocks, width + 8, LANES), f32)]
        + [pltpu.SemaphoreType.DMA] * 2,
        "side_join",
        flops=2 * rows * slots * 2 * LANES,
    )(lane, returned, listed, padded, own, own_degree)
    late = lax.optimization_barrier((edge_count, source_rows, target_rows, edge_weight, *sides))
    begin, source_late, target_late, weight_late, *sides = late
    quarter = edges // QUARTERS
    room = quarter + LANES // 2
    per_edge = ((groups, LANES), i32, VMEM)
    per_edge_f32 = ((groups, LANES), f32, VMEM)
    coded = list(call(
        functools.partial(edge_code_kernel, rows, slots, room),
        [per_edge, per_edge, ((4 * QUARTERS, LANES), i32, VMEM), per_edge_f32, per_edge, per_edge_f32, per_edge, per_edge],
        [SMEM] * 2 + [VMEM] * 3,
        [],
        "edge_code",
    )(begin, lane, source_late, target_late, weight_late.reshape(groups, LANES)))
    totals = coded.pop(2)
    far_order, spot, mass, near_order, near_weight, gap_order, gap_slot = (x.reshape(edges) for x in coded)

    def far_list(first, count):
        return call(
            functools.partial(far_list_kernel, first, room),
            [((2 * KINDS * room + LANES,), i32, SMEM)],
            [SMEM] * 4,
            [],
            "far_list",
            moved=2**25,
        )(count, far_order, spot, totals)[0]

    code_a = far_list(0, begin)
    side = summed(sides, lanes)
    side, code_a = lax.optimization_barrier((side, code_a))
    later, side = lax.optimization_barrier((begin, side))
    code_b = far_list(2, later)
    far = (code_a, code_b, totals, mass)
    right_share = side[:share]
    degree_share = side[share : share + share // LANES].reshape(share)
    ground_share = lax.dynamic_slice_in_dim(ground, lane[0] * share, share)
    diagonal = (degree_share + ground_share)[:, None]
    inverse = 1.0 / diagonal

    first, pairs = chebyshev_terms(ITERS)
    residual = right_share
    direction = first * inverse * right_share
    solution_share = direction
    for keep, push in pairs:
        shares = to_all(direction, lanes)
        early = call(
            functools.partial(early_field_kernel, lanes),
            [((slots + 8, LANES), f32, VMEM)],
            [SMEM] * 5 + [VMEM] * 2,
            [pltpu.VMEM((rows, LANES), f32)] + [pltpu.VMEM((slots + 8, LANES), f32)] * BANKS,
            "early_field",
            moved=2**25,
        )(lane, *far, shares[0], shares[2])[0]
        field, message = call(
            functools.partial(field_kernel, lanes),
            [((rows, LANES), f32, HBM), ((blocks, 2 * width, LANES), f32, HBM)],
            [SMEM] * 6 + [VMEM] * (1 + lanes),
            [pltpu.VMEM((rows, LANES), f32)]
            + [pltpu.VMEM((blocks, width, LANES), f32)] * 2
            + [pltpu.SemaphoreType.DMA, pltpu.SemaphoreType.DMA((PARTS,)), pltpu.SemaphoreType.DMA]
            + [pltpu.VMEM((slots + 8, LANES), f32)] * BANKS,
            "field",
        )(lane, *far, lists, early, *shares)
        arrived = across(message)
        near = call(
            near_kernel,
            [((rows, LANES), f32, VMEM)],
            [SMEM] * 3 + [HBM],
            [pltpu.VMEM((rows, LANES), f32), pltpu.SemaphoreType.DMA] + [pltpu.VMEM((rows, LANES), f32)] * BANKS,
            "near",
            moved=2**25,
        )(edge_count, near_order, near_weight, field)[0]
        two, halo, ret_both = call(
            functools.partial(late_join_kernel, lanes),
            [((share, LANES), f32, VMEM), ((blocks + 1, width, LANES), f32, VMEM), ((slots, 2 * LANES), bf16, VMEM)],
            [SMEM] * 5 + [VMEM, VMEM, HBM],
            [pltpu.VMEM((share, slots), bf16), pltpu.VMEM((blocks, width, LANES), f32)]
            + [pltpu.SemaphoreType.DMA] * 2
            + [pltpu.VMEM((share, LANES), f32)] * BANKS,
            "late_join",
        )(lane, *far, listed, near, arrived)
        one, three = call(
            functools.partial(join_kernel, lanes),
            [((share, LANES), f32, VMEM)] * 2,
            [SMEM] * 5 + [VMEM] * 4,
            [pltpu.VMEM((share, slots), bf16)] + [pltpu.VMEM((rows, LANES), f32)] * BANKS,
            "join",
            moved=2**25,
        )(lane, *far, listed, near, halo, ret_both)
        home = call(
            home_kernel,
            [((share, LANES), f32, VMEM)],
            [SMEM] * 5 + [VMEM] * 4,
            [pltpu.VMEM((share, slots), bf16)] + [pltpu.VMEM((share, LANES), f32)] * BANKS,
            "home",
            moved=2**25,
        )(lane, *far, listed, near, halo, ret_both)[0]
        two = moved_by(two, 2, lanes)
        two, one, three = lax.optimization_barrier((two, one, three))
        flows = (home + two) + (moved_by(one, 1, lanes) + moved_by(three, 3, lanes))
        residual = residual - (diagonal * direction - flows)
        direction = keep * direction + push * inverse * residual
        solution_share = solution_share + direction
    field, message = call(
        solution_kernel,
        [((rows, LANES), f32, VMEM), ((blocks, width, LANES), f32, HBM)],
        [SMEM] * 2 + [VMEM] * lanes,
        [pltpu.VMEM((blocks, width, LANES), f32), pltpu.SemaphoreType.DMA((PARTS,))],
        "solution_rows",
    )(lane, lists, *to_all(solution_share, lanes))
    halo = across(message)
    gaps = call(
        near_gap_kernel,
        [((edges, LANES), f32, VMEM)],
        [SMEM] * 2 + [VMEM],
        [pltpu.VMEM((rows + 8, LANES), f32)],
        "near_gap",
        moved=2**25,
    )(edge_count, gap_order, field)[0]
    resistance = call(
        far_gap_kernel,
        [((groups, LANES), f32, VMEM)],
        [SMEM] * 2 + [VMEM, HBM, VMEM],
        [pltpu.VMEM((blocks + 1, width, LANES), f32), pltpu.VMEM((edges, LANES), f32), pltpu.SemaphoreType.DMA],
        "far_gap",
    )(edge_count, gap_slot, gaps, halo, live_rows)[0]
    return (field, resistance.reshape(edges))


def solution(mesh):
    in_specs = (
        P(("vtx", "edg"), None),
        P(("vtx", "edg")),
        P("vtx"),
        P(("vtx", "edg")),
        P(("vtx", "edg")),
        P(("vtx", "edg"), None, None),
        P(("vtx", "edg")),
    )
    out_specs = (P("vtx", None), P(("vtx", "edg")))
    return jax.shard_map(local, mesh=mesh, in_specs=in_specs, out_specs=out_specs, check_vma=False)
```

```python
import functools

import jax
import jax.numpy as jnp
from jax import lax
from jax.experimental import pallas as pl
from jax.experimental.pallas import tpu as pltpu
from jax.sharding import PartitionSpec as P

ITERS = 3
LANES = 128
UNROLL = 16
BANKS = 4
QUARTERS = 4
SPARE = 1536
BESIDE, OPPOSITE, HOME = range(3)
KINDS = 3
PARTS = 8
ROOMY = 32

lam_low = 0.05
lam_high = 2.0

SMEM = pl.BlockSpec(memory_space=pltpu.SMEM)
VMEM = pl.BlockSpec(memory_space=pltpu.VMEM)
HBM = pl.BlockSpec(memory_space=pltpu.HBM)
LIMIT = 24 * 2**20


def chebyshev_terms(steps):
    centre = (lam_high + lam_low) / 2.0
    half_width = (lam_high - lam_low) / 2.0
    sigma_val = centre / half_width
    rho_prev = 1.0 / sigma_val
    pairs = []
    for count_idx in range(steps - 1):
        rho_next = 1.0 / (2.0 * sigma_val - rho_prev)
        pairs.append((rho_next * rho_prev, 2.0 * rho_next / half_width))
        rho_prev = rho_next
    return (1.0 / centre, pairs)


def call(kernel, outs, ins, scratch, name, flops=0, moved=2**22):
    return pl.pallas_call(
        kernel,
        out_shape=[
            pltpu.HBM(shape, dtype) if space is HBM else jax.ShapeDtypeStruct(shape, dtype) for shape, dtype, space in outs
        ],
        in_specs=ins,
        out_specs=[space for _, _, space in outs],
        scratch_shapes=scratch,
        compiler_params=pltpu.CompilerParams(vmem_limit_bytes=LIMIT),
        cost_estimate=pl.CostEstimate(flops=flops, bytes_accessed=moved, transcendentals=0),
        name=name,
    )


def split(x):
    high = x.astype(jnp.bfloat16)
    return high, (x - high.astype(jnp.float32)).astype(jnp.bfloat16)


def put_split(ref, rows, x):
    high, low = split(x)
    ref[rows, :LANES] = high
    ref[rows, LANES:] = low


def halves(x):
    return x[:, :LANES] + x[:, LANES:]


def one_hot(row, height, base):
    place = lax.broadcasted_iota(jnp.int32, (height, row.shape[1]), 0) + base
    return jnp.where(place == row, 1.0, 0.0)


def factored(pick, groups, high_of, low_of, weight_of, height):
    total = jnp.zeros((2 * height, LANES), jnp.float32)
    for k0 in range(0, groups, pick):
        left, right = [], []
        for k in range(k0, k0 + pick):
            member = one_hot(high_of(k), height, 0) * weight_of(k)
            high, low = split(member)
            left.append(jnp.concatenate([high, low], axis=0))
            right.append(one_hot(low_of(k), LANES, 0).astype(jnp.bfloat16))
        total = total + lax.dot_general(
            jnp.concatenate(left, axis=1),
            jnp.concatenate(right, axis=1),
            (((1,), (1,)), ((), ())),
            preferred_element_type=jnp.float32,
        )
    return total[:height] + total[height:]


def halo_side_kernel(rows, slots, width, terms, target, weight, sent, both, hot, out, leave):
    groups = target.shape[0]
    tall = hot.shape[0]
    per = tall // width
    blocks = slots // width
    chunks = slots // tall

    def slot(k):
        return target[k : k + 1, :] - rows

    def block_of(k):
        return jnp.where(slot(k) < 0, -1, lax.shift_right_arithmetic(slot(k) * 1366, 16))

    def within(k):
        return slot(k) - block_of(k) * width

    deg = factored(4, groups, block_of, within, lambda k: weight[k : k + 1, :], blocks)
    for c in range(blocks):
        out[c, width : width + 8, :] = jnp.broadcast_to(deg[c : c + 1, :], (8, LANES))
    put_split(both, slice(None), terms[...])

    def part(i):
        at = pl.ds(i * per, per)
        return pltpu.make_async_copy(out.at[at], sent.at[at], leave.at[i])

    def chunk(i, _):
        base = rows + i * tall
        for k in range(groups):
            hot[:, k * LANES : (k + 1) * LANES] = one_hot(target[k : k + 1, :], tall, base).astype(jnp.bfloat16)
        got = halves(jnp.dot(hot[...], both[...], preferred_element_type=jnp.float32))
        for c in range(per):
            out[i * per + c, :width, :] = -got[c * width : (c + 1) * width]
        part(i).start()
        return 0

    lax.fori_loop(0, chunks, chunk, 0)
    for i in range(chunks):
        part(i).wait()


def own_side_kernel(terms, source, target, weight, kept, degree, both, hot, out, leave):
    groups = target.shape[0]
    rows = out.shape[0]
    put_split(both, slice(None), terms[...])
    tall = hot.shape[0]

    def part(i):
        at = pl.ds(pl.multiple_of(i * tall, tall), tall)
        return pltpu.make_async_copy(out.at[at, :], kept.at[0, at, :], leave.at[i])

    def chunk(i, _):
        base = i * tall
        for k in range(groups):
            plus = one_hot(source[k : k + 1, :], tall, base)
            minus = one_hot(target[k : k + 1, :], tall, base)
            hot[:, k * LANES : (k + 1) * LANES] = (plus - minus).astype(jnp.bfloat16)
        out[pl.ds(pl.multiple_of(i * tall, tall), tall), :] = halves(
            jnp.dot(hot[...], both[...], preferred_element_type=jnp.float32)
        )
        part(i).start()
        return 0

    lax.fori_loop(0, rows // tall, chunk, 0)

    def total(ref):
        return factored(
            4,
            groups,
            lambda k: lax.shift_right_logical(ref[k : k + 1, :], 7),
            lambda k: ref[k : k + 1, :] & (LANES - 1),
            lambda k: weight[k : k + 1, :],
            rows // LANES,
        )

    degree[...] = total(source) + total(target)
    for i in range(rows // tall):
        part(i).wait()


def scatter_back(ret_both, listed, hots, emit, rows):
    tall = hots[0].shape[0]

    def build(i):
        to = hots[i % 2]
        for k in range(listed.shape[0]):
            to[:, k * LANES : (k + 1) * LANES] = one_hot(listed[k : k + 1, :], tall, i * tall).astype(jnp.bfloat16)

    build(0)
    for i in range(rows // tall):
        if (i + 1) * tall < rows:
            build(i + 1)
        emit(i, halves(jnp.dot(hots[i % 2][...], ret_both[...], preferred_element_type=jnp.float32)))


def side_join_kernel(lane, returned, listed, padded, own, own_degree, *refs):
    lanes = 4
    outs, (acc, ret_both, hot, other, landed, arrival, arrival_own) = refs[:lanes], refs[lanes:]
    come = pltpu.make_async_copy(returned, landed, arrival)
    come.start()
    mine = pltpu.make_async_copy(own.at[0], acc, arrival_own)
    mine.start()
    blocks = returned.shape[0]
    rows = own.shape[1]
    width = listed.shape[0] * LANES // blocks
    share = rows // lanes
    come.wait()
    for c in range(blocks):
        put_split(ret_both, slice(c * width, (c + 1) * width), landed[c, :width, :])

    def emit(i, got):
        if i == 0:
            mine.wait()
        at = slice(i * hot.shape[0], (i + 1) * hot.shape[0])
        acc[at, :] = acc[at, :] + got

    scatter_back(ret_both, listed, (hot, other), emit, rows)
    deg = own_degree[...] + factored(
        4,
        blocks,
        lambda k: lax.shift_right_arithmetic(padded[k : k + 1, :], 7),
        lambda k: padded[k : k + 1, :] & (LANES - 1),
        lambda k: landed[k, width : width + 1, :],
        rows // LANES,
    )
    deg_rows = share // LANES
    for s in range(lanes):
        q = lax.rem(lane[0] + s, lanes)
        outs[s][:share, :] = acc[pl.ds(pl.multiple_of(q * share, share), share), :]
        row = jnp.zeros((8, LANES), jnp.float32)
        place = lax.broadcasted_iota(jnp.int32, (8, LANES), 0)
        for p in range(lanes):
            for d in range(deg_rows):
                one = jnp.broadcast_to(deg[p * deg_rows + d : p * deg_rows + d + 1, :], (8, LANES))
                row = jnp.where((place == d) & (q == p), one, row)
        outs[s][share : share + 8, :] = row


def edge_code_kernel(
    rows, slots, room, count, lane, source, target, weight, far_code, spot, totals, mass, near_code, near_mass, gap_code, gap_slot
):
    groups = source.shape[0]
    per = groups // QUARTERS
    s, t = source[...], target[...]
    row = lax.broadcasted_iota(jnp.int32, s.shape, 0)
    number = row * LANES + lax.broadcasted_iota(jnp.int32, s.shape, 1)
    live = number < count[0]
    away = t >= rows
    load = jnp.where(live, weight[...], 0.0)
    mass[...] = load
    near_mass[...] = jnp.where(away, 0.0, load)
    near_code[...] = s | (jnp.where(away, 0, t) << 12)
    gap_code[...] = s | (jnp.minimum(t, rows) << 12)
    gap_slot[...] = jnp.where(away, t - rows, slots)
    far_code[...] = (jnp.where(away, t - rows, 0) << 21) | (s << 10) | (number & (per * LANES - 1))
    left = lax.broadcasted_iota(jnp.int32, (LANES, LANES), 0)
    right = lax.broadcasted_iota(jnp.int32, (LANES, LANES), 1)
    before = jnp.where(left < right, 1.0, 0.0).astype(jnp.bfloat16)
    ones = jnp.ones((LANES, LANES), jnp.bfloat16)
    down = lax.broadcasted_iota(jnp.int32, (groups, groups), 0)
    over = lax.broadcasted_iota(jnp.int32, (groups, groups), 1)
    same = lax.shift_right_logical(down, 3) == lax.shift_right_logical(over, 3)
    above = jnp.where(same & (over < down), 1.0, 0.0).astype(jnp.bfloat16)
    apart = (lax.shift_right_logical(s, 9) - lane[0]) & 3
    kinds = jnp.where(apart == 0, HOME, jnp.where(apart == 2, OPPOSITE, BESIDE))
    region = (lax.shift_right_logical(row, 3) & 1) * KINDS * room
    where = jnp.zeros_like(row) + 2 * KINDS * room
    for kind in range(KINDS):
        counted = away & live & (kinds == kind)
        flags = jnp.where(counted, 1.0, 0.0).astype(jnp.bfloat16)
        within = jnp.dot(flags, before, preferred_element_type=jnp.float32)
        total = jnp.dot(flags, ones, preferred_element_type=jnp.float32)
        base = jnp.dot(above, total.astype(jnp.bfloat16), preferred_element_type=jnp.float32)
        where = jnp.where(counted, region + kind * room + (within + base).astype(jnp.int32), where)
        through = (base + total).astype(jnp.int32)
        for c in range(QUARTERS):
            totals[kind * QUARTERS + c : kind * QUARTERS + c + 1, :] = through[(c + 1) * per - 1 : (c + 1) * per, :]
    spot[...] = where


def far_list_kernel(first, room, count, order, spot, totals, code):
    half = order.shape[0] // 2
    begin = first * order.shape[0] // QUARTERS

    def step(i, _):
        e = begin + i * 8
        given = [order[e + u] for u in range(8)]
        to = [spot[e + u] for u in range(8)]
        for u in range(8):
            code[to[u]] = given[u]
        return 0

    live = jnp.clip(count[0] - begin, 0, half)
    lax.fori_loop(0, lax.div(live + 7, 8), step, 0)
    nothing = jnp.int32(SPARE - 2048) << 21
    for c in range(2):
        for kind in range(KINDS):
            end = (KINDS * c + kind) * room + totals[kind * QUARTERS + first + c, 0]
            for u in range(UNROLL):
                code[end + u] = nothing


def trips(n):
    return lax.div(n + UNROLL - 1, UNROLL)


def clear(banks):
    for a in banks:
        a[...] = jnp.zeros_like(a)


def far_rows(kind, lists, totals, mass, take, give, banks):
    quarter = mass.shape[0] // QUARTERS
    many = len(banks)
    for h, code in enumerate(lists):
        room = (code.shape[0] - LANES) // (2 * KINDS)
        for c in range(2):
            start = (KINDS * c + kind) * room
            base = (2 * h + c) * quarter

            def step(i, _):
                for u in range(0, UNROLL, many):
                    at = start + i * UNROLL + u
                    given = [code[at + k] for k in range(many)]
                    rows = [take(given[k]) * mass[base + (given[k] & 1023)] for k in range(many)]
                    to = [pl.ds(give(given[k]), 1) for k in range(many)]
                    new = [banks[k][to[k], :] + rows[k] for k in range(many)]
                    for k in range(many):
                        banks[k][to[k], :] = new[k]
                return 0

            lax.fori_loop(0, trips(totals[kind * QUARTERS + 2 * h + c, 0]), step, 0)


def far_source(given):
    return lax.shift_right_logical(given, 10) & 2047


def far_slot(given):
    return lax.shift_right_logical(given, 21)


def source_of(given):
    return given & 4095


def target_of(given):
    return lax.shift_right_logical(given, 12)


def place(lane, lanes, shift, share, field):
    q = lax.rem(lane[0] - shift + lanes, lanes)
    rows = share.shape[0]
    field[pl.ds(pl.multiple_of(q * rows, rows), rows), :] = share[...]


def assemble(lane, lanes, shares, field):
    for s in range(lanes):
        place(lane, lanes, s, shares[s], field)


def pack(lists, field, out, width, part):
    per = out.shape[0] // PARTS

    def step(i, _):
        for c in range(per):
            for r in range(width):
                out[i * per + c, pl.ds(r, 1), :] = field[pl.ds(lists[(i * per + c) * width + r], 1), :]
        part(i).start()
        return 0

    lax.fori_loop(0, PARTS, step, 0)


def early_field_kernel(lanes, lane, code_a, code_b, totals, mass, home, opposite, out, field, *banks):
    place(lane, lanes, 0, home, field)
    place(lane, lanes, 2, opposite, field)
    clear(banks)
    for kind in (HOME, OPPOSITE):
        far_rows(
            kind,
            (code_a, code_b),
            totals,
            mass,
            lambda given: field[pl.ds(far_source(given), 1), :],
            far_slot,
            banks,
        )
    total = banks[0][...]
    for a in banks[1:]:
        total = total + a[...]
    out[...] = total


def field_kernel(lanes, lane, code_a, code_b, totals, mass, lists, early, *refs):
    shares, (kept, sent), refs = refs[:lanes], refs[lanes : lanes + 2], refs[lanes + 2 :]
    field, out, sums, leave_field, leave, leave_sums = refs[:6]
    banks = refs[6:]
    blocks, width, _ = out.shape
    assemble(lane, lanes, shares, field)
    keep = pltpu.make_async_copy(field, kept, leave_field)
    keep.start()
    banks[0][...] = early[...]
    clear(banks[1:])
    far_rows(
        BESIDE,
        (code_a, code_b),
        totals,
        mass,
        lambda given: field[pl.ds(far_source(given), 1), :],
        far_slot,
        banks,
    )
    for c in range(blocks):
        at = slice(c * width, (c + 1) * width)
        total = banks[0][at, :]
        for a in banks[1:]:
            total = total + a[at, :]
        sums[c] = total
    more = pltpu.make_async_copy(sums, sent.at[:, width:, :], leave_sums)
    more.start()
    per = blocks // PARTS

    def part(i):
        at = pl.ds(i * per, per)
        return pltpu.make_async_copy(out.at[at], sent.at[at, :width, :], leave.at[i])

    pack(lists, field, out, width, part)
    keep.wait()
    more.wait()
    for i in range(PARTS):
        part(i).wait()


def near_kernel(count, order, heavy, kept, out, field, come, *banks):
    bring = pltpu.make_async_copy(kept, field, come)
    bring.start()
    clear(banks)
    bring.wait()

    def step(i, _):
        for u in range(0, UNROLL, BANKS):
            at = i * UNROLL + u
            code = [order[at + k] for k in range(BANKS)]
            mass = [heavy[at + k] for k in range(BANKS)]
            one = [pl.ds(source_of(code[k]), 1) for k in range(BANKS)]
            two = [pl.ds(target_of(code[k]), 1) for k in range(BANKS)]
            from_one = [field[one[k], :] * mass[k] for k in range(BANKS)]
            from_two = [field[two[k], :] * mass[k] for k in range(BANKS)]
            new = [banks[k][one[k], :] + from_two[k] for k in range(BANKS)]
            for k in range(BANKS):
                banks[k][one[k], :] = new[k]
            new = [banks[k][two[k], :] + from_one[k] for k in range(BANKS)]
            for k in range(BANKS):
                banks[k][two[k], :] = new[k]
        return 0

    lax.fori_loop(0, trips(count[0]), step, 0)
    total = banks[0][...]
    for a in banks[1:]:
        total = total + a[...]
    out[...] = total


def listed_rows(q, share, listed, ret_both, hot):
    for k in range(listed.shape[0]):
        hot[:, k * LANES : (k + 1) * LANES] = one_hot(listed[k : k + 1, :], share, q * share).astype(jnp.bfloat16)
    return halves(jnp.dot(hot[...], ret_both[...], preferred_element_type=jnp.float32))


def late_join_kernel(lanes, lane, code_a, code_b, totals, mass, listed, near, arrived, *refs):
    out, halo, ret_both, hot, ret, come_halo, come_ret = refs[:7]
    banks = refs[7:]
    blocks, width, _ = ret.shape
    share = out.shape[0]
    first = pltpu.make_async_copy(arrived.at[:, :width, :], halo.at[:blocks], come_halo)
    second = pltpu.make_async_copy(arrived.at[:, width:, :], ret, come_ret)
    second.start()
    first.start()
    halo[blocks] = jnp.zeros((width, LANES), jnp.float32)
    clear(banks)
    q = lax.rem(lane[0] + 2, lanes)
    second.wait()
    for c in range(blocks):
        put_split(ret_both, slice(c * width, (c + 1) * width), ret[c])
    total = near[pl.ds(pl.multiple_of(q * share, share), share), :]
    out[...] = total + listed_rows(q, share, listed, ret_both, hot)
    first.wait()
    flat = halo.reshape((blocks + 1) * width, LANES)
    far_rows(
        OPPOSITE,
        (code_a, code_b),
        totals,
        mass,
        lambda given: flat[pl.ds(far_slot(given), 1), :],
        lambda given: far_source(given) & (share - 1),
        banks,
    )
    total = out[...]
    for a in banks:
        total = total + a[...]
    out[...] = total


def join_kernel(lanes, lane, code_a, code_b, totals, mass, listed, near, halo, ret_both, *refs):
    outs, hot, banks = refs[:2], refs[2], refs[3:]
    share = outs[0].shape[0]
    spots = []
    for s in (1, 3):
        q = lax.rem(lane[0] + s, lanes)
        at = pl.ds(pl.multiple_of(q * share, share), share)
        banks[0][at, :] = near[at, :]
        for a in banks[1:]:
            a[at, :] = jnp.zeros((share, LANES), jnp.float32)
        spots.append((q, at))
    flat = halo.reshape(halo.shape[0] * halo.shape[1], LANES)
    far_rows(
        BESIDE,
        (code_a, code_b),
        totals,
        mass,
        lambda given: flat[pl.ds(far_slot(given), 1), :],
        far_source,
        banks,
    )
    for (q, at), out in zip(spots, outs):
        total = banks[0][at, :]
        for a in banks[1:]:
            total = total + a[at, :]
        out[...] = total + listed_rows(q, share, listed, ret_both, hot)


def home_kernel(lane, code_a, code_b, totals, mass, listed, near, halo, ret_both, out, hot, *banks):
    share = out.shape[0]
    clear(banks)
    flat = halo.reshape(halo.shape[0] * halo.shape[1], LANES)
    far_rows(
        HOME,
        (code_a, code_b),
        totals,
        mass,
        lambda given: flat[pl.ds(far_slot(given), 1), :],
        lambda given: far_source(given) & (share - 1),
        banks,
    )
    total = near[pl.ds(pl.multiple_of(lane[0] * share, share), share), :]
    for a in banks:
        total = total + a[...]
    out[...] = total + listed_rows(lane[0], share, listed, ret_both, hot)


def solution_kernel(lane, lists, *refs):
    lanes = 4
    shares, (field, sent, out, leave) = refs[:lanes], refs[lanes:]
    assemble(lane, lanes, shares, field)
    per = out.shape[0] // PARTS

    def part(i):
        at = pl.ds(i * per, per)
        return pltpu.make_async_copy(out.at[at], sent.at[at], leave.at[i])

    pack(lists, field, out, out.shape[1], part)
    for i in range(PARTS):
        part(i).wait()


def near_gap_kernel(count, order, field, gaps, more):
    rows = field.shape[0]
    more[:rows, :] = field[...]
    more[rows:, :] = jnp.zeros((more.shape[0] - rows, LANES), jnp.float32)

    def step(i, _):
        for u in range(UNROLL):
            e = i * UNROLL + u
            code = order[e]
            gaps[pl.ds(e, 1), :] = (
                field[pl.ds(code & 4095, 1), :] - more[pl.ds(lax.shift_right_logical(code, 12), 1), :]
            )
        return 0

    lax.fori_loop(0, trips(count[0]), step, 0)


def far_gap_kernel(count, slot, gaps, arrived, live, out, halo, taken, come):
    blocks, width, _ = arrived.shape
    groups = live.shape[0]
    first = pltpu.make_async_copy(arrived, halo.at[:blocks], come)
    first.start()
    halo[blocks] = jnp.zeros((width, LANES), jnp.float32)
    first.wait()
    flat = halo.reshape((blocks + 1) * width, LANES)

    def gather(k):
        for u in range(LANES):
            e = k * LANES + u
            taken[pl.ds(e, 1), :] = flat[pl.ds(slot[e], 1), :]

    def finish(k):
        at = pl.ds(pl.multiple_of(k * LANES, LANES), LANES)
        gap = gaps[at, :] - taken[at, :]
        total = jnp.sum((gap * gap).T, axis=0, keepdims=True)
        alive = live[pl.ds(k, 1), :]
        out[pl.ds(k, 1), :] = jnp.where(alive > 0, total * (alive / LANES), 0.0)

    def step(k, _):
        finish(k - 1)
        gather(k)
        return 0

    out[...] = jnp.zeros((groups, LANES), jnp.float32)
    many = lax.div(count[0] + LANES - 1, LANES)
    gather(0)
    lax.fori_loop(1, many, step, 0)
    finish(many - 1)


def moved_by(x, shift, lanes):
    return lax.ppermute(x, "edg", [(i, (i + shift) % lanes) for i in range(lanes)])


def passed_round(blocks, lanes):
    return [blocks[0]] + [moved_by(blocks[s], s, lanes) for s in (2, 1, 3)]


def summed(blocks, lanes):
    home, two, one, three = passed_round(blocks, lanes)
    return (home + one) + (two + three)


def to_all(mine, lanes):
    home, two, one, three = passed_round([mine] * lanes, lanes)
    return [home, one, two, three]


def across(x):
    return lax.all_to_all(x, "vtx", split_axis=0, concat_axis=0, tiled=True)


def local(sketch_cols, edge_weight, ground, src_local, dst_index, send_rows, edge_count):
    blocks = lax.axis_size("vtx")
    lanes = lax.axis_size("edg")
    rows = ground.shape[0]
    edges = edge_weight.shape[0]
    width = send_rows.shape[2]
    slots = blocks * width
    share = rows // lanes
    groups = edges // LANES
    f32, i32, bf16 = jnp.float32, jnp.int32, jnp.bfloat16
    lane = lax.axis_index("edg").astype(i32).reshape(1)
    lists = send_rows[0].reshape(-1)
    listed = lists.reshape(slots // LANES, LANES)
    padded = jnp.pad(send_rows[0], ((0, 0), (0, LANES - width)), constant_values=-1)
    live = (jnp.arange(edges, dtype=i32) < edge_count[0]).astype(f32)
    weight = edge_weight * live
    root = jnp.sqrt(edge_weight) * live
    terms = root[:, None] * sketch_cols.astype(f32)
    live_rows = live.reshape(groups, LANES)
    weight_rows = weight.reshape(groups, LANES)
    source_rows = src_local.reshape(groups, LANES)
    target_rows = dst_index.reshape(groups, LANES)

    outgoing = call(
        functools.partial(halo_side_kernel, rows, slots, width),
        [((blocks, width + 8, LANES), f32, HBM)],
        [VMEM] * 3,
        [pltpu.VMEM((edges, 2 * LANES), bf16), pltpu.VMEM((8 * width, edges), bf16)]
        + [pltpu.VMEM((blocks, width + 8, LANES), f32), pltpu.SemaphoreType.DMA((slots // (8 * width),))],
        "halo_side",
        flops=2 * slots * edges * 2 * LANES,
    )(terms, target_rows, weight_rows)[0]
    returned = across(outgoing)
    own, own_degree = call(
        own_side_kernel,
        [((ROOMY, rows, LANES), f32, HBM), ((rows // LANES, LANES), f32, VMEM)],
        [VMEM] * 4,
        [pltpu.VMEM((edges, 2 * LANES), bf16), pltpu.VMEM((256, edges), bf16)]
        + [pltpu.VMEM((rows, LANES), f32), pltpu.SemaphoreType.DMA((rows // 256,))],
        "own_side",
        flops=2 * rows * edges * 2 * LANES,
    )(terms, source_rows, target_rows, weight_rows)
    sides = call(
        side_join_kernel,
        [((share + 8, LANES), f32, VMEM)] * lanes,
        [SMEM, HBM, VMEM, VMEM, HBM, VMEM],
        [pltpu.VMEM((rows, LANES), f32), pltpu.VMEM((slots, 2 * LANES), bf16)]
        + [pltpu.VMEM((256, slots), bf16)] * 2
        + [pltpu.VMEM((blocks, width + 8, LANES), f32)]
        + [pltpu.SemaphoreType.DMA] * 2,
        "side_join",
        flops=2 * rows * slots * 2 * LANES,
    )(lane, returned, listed, padded, own, own_degree)
    late = lax.optimization_barrier((edge_count, source_rows, target_rows, edge_weight, *sides))
    begin, source_late, target_late, weight_late, *sides = late
    quarter = edges // QUARTERS
    room = quarter + LANES // 2
    per_edge = ((groups, LANES), i32, VMEM)
    per_edge_f32 = ((groups, LANES), f32, VMEM)
    coded = list(call(
        functools.partial(edge_code_kernel, rows, slots, room),
        [per_edge, per_edge, ((4 * QUARTERS, LANES), i32, VMEM), per_edge_f32, per_edge, per_edge_f32, per_edge, per_edge],
        [SMEM] * 2 + [VMEM] * 3,
        [],
        "edge_code",
    )(begin, lane, source_late, target_late, weight_late.reshape(groups, LANES)))
    totals = coded.pop(2)
    far_order, spot, mass, near_order, near_weight, gap_order, gap_slot = (x.reshape(edges) for x in coded)

    def far_list(first, count):
        return call(
            functools.partial(far_list_kernel, first, room),
            [((2 * KINDS * room + LANES,), i32, SMEM)],
            [SMEM] * 4,
            [],
            "far_list",
            moved=2**25,
        )(count, far_order, spot, totals)[0]

    code_a = far_list(0, begin)
    side = summed(sides, lanes)
    side, code_a = lax.optimization_barrier((side, code_a))
    later, side = lax.optimization_barrier((begin, side))
    code_b = far_list(2, later)
    far = (code_a, code_b, totals, mass)
    right_share = side[:share]
    degree_share = side[share : share + share // LANES].reshape(share)
    ground_share = lax.dynamic_slice_in_dim(ground, lane[0] * share, share)
    diagonal = (degree_share + ground_share)[:, None]
    inverse = 1.0 / diagonal

    first, pairs = chebyshev_terms(ITERS)
    residual = right_share
    direction = first * inverse * right_share
    solution_share = direction
    for keep, push in pairs:
        shares = to_all(direction, lanes)
        early = call(
            functools.partial(early_field_kernel, lanes),
            [((slots + 8, LANES), f32, VMEM)],
            [SMEM] * 5 + [VMEM] * 2,
            [pltpu.VMEM((rows, LANES), f32)] + [pltpu.VMEM((slots + 8, LANES), f32)] * BANKS,
            "early_field",
            moved=2**25,
        )(lane, *far, shares[0], shares[2])[0]
        field, message = call(
            functools.partial(field_kernel, lanes),
            [((rows, LANES), f32, HBM), ((blocks, 2 * width, LANES), f32, HBM)],
            [SMEM] * 6 + [VMEM] * (1 + lanes),
            [pltpu.VMEM((rows, LANES), f32)]
            + [pltpu.VMEM((blocks, width, LANES), f32)] * 2
            + [pltpu.SemaphoreType.DMA, pltpu.SemaphoreType.DMA((PARTS,)), pltpu.SemaphoreType.DMA]
            + [pltpu.VMEM((slots + 8, LANES), f32)] * BANKS,
            "field",
        )(lane, *far, lists, early, *shares)
        arrived = across(message)
        near = call(
            near_kernel,
            [((rows, LANES), f32, VMEM)],
            [SMEM] * 3 + [HBM],
            [pltpu.VMEM((rows, LANES), f32), pltpu.SemaphoreType.DMA] + [pltpu.VMEM((rows, LANES), f32)] * BANKS,
            "near",
            moved=2**25,
        )(edge_count, near_order, near_weight, field)[0]
        two, halo, ret_both = call(
            functools.partial(late_join_kernel, lanes),
            [((share, LANES), f32, VMEM), ((blocks + 1, width, LANES), f32, VMEM), ((slots, 2 * LANES), bf16, VMEM)],
            [SMEM] * 5 + [VMEM, VMEM, HBM],
            [pltpu.VMEM((share, slots), bf16), pltpu.VMEM((blocks, width, LANES), f32)]
            + [pltpu.SemaphoreType.DMA] * 2
            + [pltpu.VMEM((share, LANES), f32)] * BANKS,
            "late_join",
        )(lane, *far, listed, near, arrived)
        one, three = call(
            functools.partial(join_kernel, lanes),
            [((share, LANES), f32, VMEM)] * 2,
            [SMEM] * 5 + [VMEM] * 4,
            [pltpu.VMEM((share, slots), bf16)] + [pltpu.VMEM((rows, LANES), f32)] * BANKS,
            "join",
            moved=2**25,
        )(lane, *far, listed, near, halo, ret_both)
        home = call(
            home_kernel,
            [((share, LANES), f32, VMEM)],
            [SMEM] * 5 + [VMEM] * 4,
            [pltpu.VMEM((share, slots), bf16)] + [pltpu.VMEM((share, LANES), f32)] * BANKS,
            "home",
            moved=2**25,
        )(lane, *far, listed, near, halo, ret_both)[0]
        two = moved_by(two, 2, lanes)
        two, one, three = lax.optimization_barrier((two, one, three))
        flows = (home + two) + (moved_by(one, 1, lanes) + moved_by(three, 3, lanes))
        residual = residual - (diagonal * direction - flows)
        direction = keep * direction + push * inverse * residual
        solution_share = solution_share + direction
    field, message = call(
        solution_kernel,
        [((rows, LANES), f32, VMEM), ((blocks, width, LANES), f32, HBM)],
        [SMEM] * 2 + [VMEM] * lanes,
        [pltpu.VMEM((blocks, width, LANES), f32), pltpu.SemaphoreType.DMA((PARTS,))],
        "solution_rows",
    )(lane, lists, *to_all(solution_share, lanes))
    halo = across(message)
    gaps = call(
        near_gap_kernel,
        [((edges, LANES), f32, VMEM)],
        [SMEM] * 2 + [VMEM],
        [pltpu.VMEM((rows + 8, LANES), f32)],
        "near_gap",
        moved=2**25,
    )(edge_count, gap_order, field)[0]
    resistance = call(
        far_gap_kernel,
        [((groups, LANES), f32, VMEM)],
        [SMEM] * 2 + [VMEM, HBM, VMEM],
        [pltpu.VMEM((blocks + 1, width, LANES), f32), pltpu.VMEM((edges, LANES), f32), pltpu.SemaphoreType.DMA],
        "far_gap",
    )(edge_count, gap_slot, gaps, halo, live_rows)[0]
    return (field, resistance.reshape(edges))


def solution(mesh):
    in_specs = (
        P(("vtx", "edg"), None),
        P(("vtx", "edg")),
        P("vtx"),
        P(("vtx", "edg")),
        P(("vtx", "edg")),
        P(("vtx", "edg"), None, None),
        P(("vtx", "edg")),
    )
    out_specs = (P("vtx", None), P(("vtx", "edg")))
    return jax.shard_map(local, mesh=mesh, in_specs=in_specs, out_specs=out_specs, check_vma=False)
```
